32 devices in a mesh: dp: 16 (over z, y, x), ctx: 2 (over core).
Axes of the slice: x: 2, y: 2, z: 4, core: 2. Of those that a mesh axis runs over, the one named last changes fastest.
Arguments:
- queries: bfloat16 [4096, 4096], P(('dp', 'ctx')), may hold values from -150 to 150
- keys: bfloat16 [4096, 512], P(('dp', 'ctx')), may hold values from -4 to 4
- values: bfloat16 [4096, 512], P(('dp', 'ctx')), may hold values from -6 to 6
- lengths: int32 [32], replicated, may hold values from 1 to 512, 4096 in all
Outputs:
- attended: bfloat16 [4096, 4096], P(('dp', 'ctx'))
The draws below stay inside these ranges and needn't reach their ends.
Inputs may be any that keep to these rules, and one draw needn't show every extreme that they name: lengths of the 32 documents sum to 4096; the largest is exactly 512.
All inputs are finite; a program needn't handle non-finite values.
Results may differ from the reference program's by a relative error of at most 0.0045.
Values may be sent and summed in bfloat16 or wider, within the bound.
No kernel may reach another device: no remote copies, remote signals or barrier semaphores. Data moves between devices by JAX's collectives and lax.ppermute only.
A program may use at most 128 MiB of HBM per device.

```python
import math
import jax
import jax.numpy as jnp
import numpy as np
from jax import lax

HEAD_SIZE = 128
QUERY_HEADS = 32
KEY_VALUE_HEADS = 4
DEVICE_TOKENS = 128
LONGEST_LENGTH = 512
STREAM_TOKENS = 4096
NDOCS = 32


def draw_pair(key):
    key_query = jax.random.fold_in(key, 11)
    key_random_keys = jax.random.fold_in(key, 12)
    key_layout = jax.random.truncated_normal(key_random_keys, -4.0, 4.0, (STREAM_TOKENS, KEY_VALUE_HEADS, HEAD_SIZE), jnp.float32)
    query_layout = 2.5 * jax.random.truncated_normal(key_query, -6.0, 6.0, (STREAM_TOKENS, QUERY_HEADS, HEAD_SIZE), jnp.float32)
    return (query_layout.reshape(STREAM_TOKENS, QUERY_HEADS * HEAD_SIZE), key_layout.reshape(STREAM_TOKENS, KEY_VALUE_HEADS * HEAD_SIZE))


def draw_queries(key, part):
    return draw_pair(key)[0].astype(jnp.bfloat16)


def draw_keys(key, part):
    return draw_pair(key)[1].astype(jnp.bfloat16)


def steps_of(rng, shape, cuts, low, top_value):
    level, own = 1.0, jax.random.fold_in(rng, 6)
    for dim, shards_of in cuts:
        steps = jnp.exp(jax.random.uniform(jax.random.fold_in(own, dim), (shards_of,), jnp.float32, low / len(cuts), top_value / len(cuts)))
        level = level * jnp.repeat(steps, shape[dim] // shards_of).reshape([-1 if axis == dim else 1 for axis in range(len(shape))])
    return level


def profile(amount, total, reach, lean):
    portions = [(1 << 20) // math.isqrt(grade ** lean) + 1 for grade in range(2, amount + 1)]
    surplus, counts = total - reach - (amount - 1), [1] * (amount - 1)
    while surplus > 0:
        movable = [i for i in range(amount - 1) if counts[i] < reach]
        whole, budget = sum([portions[i] for i in movable]), surplus
        for i in movable:
            addition = min(reach - counts[i], max(1, budget * portions[i] // whole), surplus)
            counts[i] = counts[i] + addition
            surplus = surplus - addition
    return np.array([reach] + counts)


def uneven(own_key, amount, total, most, lean):
    if amount == 2:
        one = jax.random.randint(own_key, (), max(1, total - most), min(most, total - 1) + 1)
        return jnp.stack([one, total - one])
    sizes = jnp.asarray(profile(amount, total, most, lean), jnp.int32)
    twos = (amount - 1) // 2
    source_of, receiver = sizes[1:1 + 2 * twos:2], sizes[2:2 + 2 * twos:2]
    slack = jnp.minimum(source_of - 1, most - receiver)
    passed = jax.random.randint(jax.random.fold_in(own_key, 1), (twos,), 0, 1 << 20) % (slack + 1)
    sizes = sizes.at[1:1 + 2 * twos:2].set(source_of - passed).at[2:2 + 2 * twos:2].set(receiver + passed)
    return sizes[jax.random.permutation(jax.random.fold_in(own_key, 2), amount)]


def bell_draw(rng, extent, width, limit, shards=(), held_as=jnp.bfloat16):
    factor_of = steps_of(rng, extent, shards, -0.22, 0.18) if shards else 1.0
    entries = jax.random.normal(rng, extent, jnp.float32) * width * factor_of
    return jnp.minimum(jnp.maximum(entries, -limit), limit).astype(held_as)


def setup_inputs(seed: int = 0) -> dict:
    arg_keys = jax.random.split(jax.random.key(seed), 5)
    return {
        "queries": draw_queries(jax.random.fold_in(arg_keys[4], 71), 0),
        "keys": draw_keys(jax.random.fold_in(arg_keys[4], 71), 0),
        "values": bell_draw(arg_keys[2], (STREAM_TOKENS, KEY_VALUE_HEADS * HEAD_SIZE), 1.0, 6.0, ((0, 32),)),
        "lengths": uneven(arg_keys[3], NDOCS, STREAM_TOKENS, LONGEST_LENGTH, 2).astype(jnp.int32),
    }


def document_of(position, doc_bounds):
    return jnp.sum((position[:, None] >= doc_bounds[None, :]).astype(jnp.int32), axis=1)


def reference(queries, keys, values, lengths):
    doc_bounds = jnp.cumsum(lengths).astype(jnp.int32)
    visible_span = LONGEST_LENGTH + DEVICE_TOKENS
    query_group_width = QUERY_HEADS // KEY_VALUE_HEADS
    scaling = 1.0 / (HEAD_SIZE ** 0.5)
    padded_keys = jnp.concatenate([jnp.zeros((LONGEST_LENGTH, KEY_VALUE_HEADS * HEAD_SIZE), keys.dtype), keys], axis=0)
    padded_values = jnp.concatenate([jnp.zeros((LONGEST_LENGTH, KEY_VALUE_HEADS * HEAD_SIZE), values.dtype), values], axis=0)

    def one_block(block_id):
        leading_entry = (block_id * DEVICE_TOKENS).astype(jnp.int32)
        query_row_slice = lax.dynamic_slice_in_dim(queries, leading_entry, DEVICE_TOKENS, 0)
        query_row_slice = query_row_slice.reshape(DEVICE_TOKENS, KEY_VALUE_HEADS, query_group_width, HEAD_SIZE).astype(jnp.float32)
        key_row_slice = lax.dynamic_slice_in_dim(padded_keys, leading_entry, visible_span, 0).reshape(visible_span, KEY_VALUE_HEADS, HEAD_SIZE).astype(jnp.float32)
        value_row_slice = lax.dynamic_slice_in_dim(padded_values, leading_entry, visible_span, 0).reshape(visible_span, KEY_VALUE_HEADS, HEAD_SIZE).astype(jnp.float32)
        query_pos = leading_entry + jnp.arange(DEVICE_TOKENS, dtype=jnp.int32)
        key_pos = leading_entry - LONGEST_LENGTH + jnp.arange(visible_span, dtype=jnp.int32)
        allowed = (key_pos[None, :] <= query_pos[:, None]) & (key_pos[None, :] >= 0)
        allowed = allowed & (document_of(key_pos, doc_bounds)[None, :] == document_of(query_pos, doc_bounds)[:, None])
        scores = jnp.einsum("qhgd,khd->hgqk", query_row_slice, key_row_slice) * scaling
        scores = jnp.where(allowed, scores, jnp.float32(-1e30))
        rowmax = jnp.max(scores, axis=-1, keepdims=True)
        expwts = jnp.where(allowed, jnp.exp(scores - rowmax), jnp.float32(0.0))
        total = jnp.sum(expwts, axis=-1)
        weights = expwts.astype(jnp.bfloat16).astype(jnp.float32)
        summed = jnp.einsum("hgqk,khd->hgqd", weights, value_row_slice)
        result = summed / total[..., None]
        return jnp.transpose(result, (2, 0, 1, 3)).reshape(DEVICE_TOKENS, QUERY_HEADS * HEAD_SIZE).astype(jnp.bfloat16)

    blocks = lax.map(one_block, jnp.arange(STREAM_TOKENS // DEVICE_TOKENS, dtype=jnp.int32))
    return blocks.reshape(STREAM_TOKENS, QUERY_HEADS * HEAD_SIZE)
```

```python
import functools
import math

import jax
import jax.numpy as jnp
from jax import lax
from jax.experimental import pallas as pl
from jax.experimental.pallas import tpu as pltpu
from jax.sharding import PartitionSpec as P

HEAD_SIZE = 128
QUERY_HEADS = 32
KEY_VALUE_HEADS = 4
GROUP = QUERY_HEADS // KEY_VALUE_HEADS
HEADS_AT_ONCE = 2
EXCLUDED = -1e30
AXES = ("dp", "ctx")


def attention_kernel(blocks, rows, lengths_ref, places_ref, q_ref, *refs):
    keys = refs[0 : 2 * blocks : 2]
    values = refs[1 : 2 * blocks : 2]
    out_ref = refs[2 * blocks]
    bias_ref = refs[2 * blocks + 1]

    @pl.when(pl.program_id(0) == 0)
    def _():
        query_pos = places_ref[0] + lax.broadcasted_iota(jnp.int32, (8, rows), 1)

        def later(doc, carried):
            bound, start = carried
            bound = bound + lengths_ref[doc]
            return bound, jnp.where(query_pos >= bound, bound, start)

        count = lengths_ref.shape[0]
        _, start = lax.fori_loop(
            0, count, later, (jnp.int32(0), jnp.zeros((8, rows), jnp.int32)), unroll=8
        )
        start = start[0:1]
        query_pos = query_pos[0:1]
        for b in range(blocks):
            key_pos = places_ref[b] + lax.broadcasted_iota(jnp.int32, (rows, rows), 0)
            allowed = (key_pos >= start) & (key_pos <= query_pos)
            bias_ref[b * rows : (b + 1) * rows, :] = jnp.where(
                allowed, jnp.float32(0.0), jnp.float32(EXCLUDED)
            )

    key_all = jnp.concatenate([k[...] for k in keys], axis=0)
    value_all = jnp.concatenate([v[...] for v in values], axis=0)
    value_t = value_all.T
    factor = jnp.float32(math.log2(math.e) / math.sqrt(HEAD_SIZE))
    for h in range(0, GROUP, HEADS_AT_ONCE):
        heads = range(h, h + HEADS_AT_ONCE)
        q = jnp.concatenate(
            [q_ref[:, i * HEAD_SIZE : (i + 1) * HEAD_SIZE] for i in heads], axis=0
        )
        scores = lax.dot_general(
            key_all, q, (((1,), (1,)), ((), ())), preferred_element_type=jnp.float32
        )
        scores = scores + jnp.concatenate([bias_ref[...]] * HEADS_AT_ONCE, axis=1)
        top = jnp.max(scores, axis=0, keepdims=True)
        weights = jnp.exp2((scores - top) * factor)
        total = jnp.sum(weights, axis=0, keepdims=True)
        summed = lax.dot_general(
            value_t,
            weights.astype(jnp.bfloat16),
            (((1,), (0,)), ((), ())),
            preferred_element_type=jnp.float32,
        )
        result = summed * (1.0 / total)
        for n, i in enumerate(heads):
            out_ref[:, i * HEAD_SIZE : (i + 1) * HEAD_SIZE] = (
                result[:, n * rows : (n + 1) * rows].T.astype(jnp.bfloat16)
            )


def attention(queries, key_values, lengths, places):
    rows = queries.shape[0]
    blocks = len(key_values)
    group_width = GROUP * HEAD_SIZE
    smem = pl.BlockSpec(memory_space=pltpu.SMEM)
    key_spec = pl.BlockSpec((rows, HEAD_SIZE), lambda g: (0, g))
    value_spec = pl.BlockSpec((rows, HEAD_SIZE), lambda g: (1, g))
    operands = []
    for pair in key_values:
        operands += [pair, pair]
    area = rows * rows * blocks * QUERY_HEADS
    return pl.pallas_call(
        functools.partial(attention_kernel, blocks, rows),
        grid=(KEY_VALUE_HEADS,),
        out_shape=jax.ShapeDtypeStruct(queries.shape, queries.dtype),
        in_specs=[smem, smem, pl.BlockSpec((rows, group_width), lambda g: (0, g))]
        + [key_spec, value_spec] * blocks,
        out_specs=pl.BlockSpec((rows, group_width), lambda g: (0, g)),
        scratch_shapes=[pltpu.VMEM((blocks * rows, rows), jnp.float32)],
        compiler_params=pltpu.CompilerParams(vmem_limit_bytes=32 * 1024 * 1024),
        cost_estimate=pl.CostEstimate(
            flops=4 * area * HEAD_SIZE,
            bytes_accessed=2 * (2 * queries.size + blocks * key_values[0].size),
            transcendentals=area,
        ),
    )(lengths, places, queries, *operands)


def per_device(queries, keys, values, lengths):
    rows = queries.shape[0]
    count = lax.axis_size("dp") * lax.axis_size("ctx")
    rounds = lax.axis_size("ctx")
    me = lax.axis_index(AXES)
    odd = lax.rem(me, 2)
    is_odd = odd == 1
    own = jnp.concatenate([keys, values], axis=0)

    def back(even, r):
        return 2 * (r + 1) if even else 2 * (rounds - r)

    fetched = []
    for r in range(rounds):
        pairs = [(i - back(i % 2 == 0, r), i) for i in range(count)]
        pairs = [(i, j) for i, j in pairs if i >= 0]
        fetched.append(lax.ppermute(own, AXES, pairs))
    swap = [(i, i ^ 1) for i in range(count)]
    swapped = [lax.ppermute(block, AXES, swap) for block in fetched[:-1]]
    swapped.append(lax.ppermute(jnp.where(is_odd, fetched[-1], own), AXES, swap))

    places = [me]
    for r in range(rounds):
        places.append(me - jnp.where(is_odd, back(False, r), back(True, r)))
    other = me + 1 - 2 * odd
    for r in range(rounds):
        seen_by_odd = other if r == rounds - 1 else other - back(True, r)
        places.append(jnp.where(is_odd, seen_by_odd, other - back(False, r)))
    places = jnp.stack(places).astype(jnp.int32) * rows
    return attention(queries, [own] + fetched + swapped, lengths, places)


def solution(mesh):
    in_specs = (P(AXES, None), P(AXES, None), P(AXES, None), P())
    return jax.shard_map(
        per_device, mesh=mesh, in_specs=in_specs, out_specs=P(AXES, None), check_vma=False
    )
```

```python
import functools
import math

import jax
import jax.numpy as jnp
from jax import lax
from jax.experimental import pallas as pl
from jax.experimental.pallas import tpu as pltpu
from jax.sharding import PartitionSpec as P

HEAD_SIZE = 128
QUERY_HEADS = 32
KEY_VALUE_HEADS = 4
GROUP = QUERY_HEADS // KEY_VALUE_HEADS
HEADS_AT_ONCE = 4
EXCLUDED = -1e30
AXES = ("dp", "ctx")


def attention_kernel(
    counts, rows, lengths_ref, places_ref, q_ref, *refs
):
    blocks = counts[-1]
    pair_refs = refs[:blocks]
    out_ref, bias_ref, key_ref, value_ref, span_ref = refs[blocks:]
    chunk = q_ref.shape[0]
    first = places_ref[0]

    @pl.when((pl.program_id(0) == 0) & (pl.program_id(1) == 0))
    def _():
        query_pos = first + lax.broadcasted_iota(jnp.int32, (rows, rows), 0)

        def later(doc, carried):
            bound, start, first_start, first_end = carried
            following = bound + lengths_ref[doc]
            start = jnp.where(query_pos >= bound, bound, start)
            first_start = jnp.where(first >= bound, bound, first_start)
            first_end = jnp.where(first >= bound, following, first_end)
            return following, start, first_start, first_end

        zero = jnp.int32(0)
        _, start, first_start, first_end = lax.fori_loop(
            0,
            lengths_ref.shape[0],
            later,
            (zero, jnp.zeros((rows, rows), jnp.int32), zero, zero),
            unroll=8,
        )
        span_ref[0] = lax.div(first - first_start + (rows - 1), jnp.int32(rows))
        span_ref[1] = first_end - first
        lane = lax.broadcasted_iota(jnp.int32, (rows, rows), 1)
        for b in range(blocks):
            key_pos = first - b * rows + lane
            allowed = key_pos >= start
            if b == 0:
                allowed = allowed & (key_pos <= query_pos)
            bias_ref[:, b * rows : (b + 1) * rows] = jnp.where(
                allowed, jnp.float32(0.0), jnp.float32(EXCLUDED)
            )
        for b in range(blocks):
            at = pl.ds(pl.multiple_of(places_ref[1 + b] * rows, rows), rows)
            key_ref[at, :] = pair_refs[b][:rows, :]
            value_ref[at, :] = pair_refs[b][rows:, :]

    group = pl.program_id(0)
    base = pl.multiple_of(pl.program_id(1) * chunk, chunk)
    columns = pl.ds(pl.multiple_of(group * HEAD_SIZE, HEAD_SIZE), HEAD_SIZE)
    factor = jnp.float32(math.log2(math.e) / math.sqrt(HEAD_SIZE))

    def attend(count):
        reach = count * rows
        key = key_ref[:reach, columns]
        value = jnp.concatenate(
            [value_ref[:reach, columns], jnp.ones((reach, HEAD_SIZE), jnp.bfloat16)], axis=1
        )
        bias = bias_ref[pl.ds(base, chunk), :reach]
        for h in range(0, GROUP, HEADS_AT_ONCE):
            heads = range(h, h + HEADS_AT_ONCE)
            q = jnp.concatenate(
                [q_ref[:, i * HEAD_SIZE : (i + 1) * HEAD_SIZE] for i in heads], axis=0
            )
            scores = lax.dot_general(
                q, key, (((1,), (1,)), ((), ())), preferred_element_type=jnp.float32
            )
            scores = scores + jnp.concatenate([bias] * HEADS_AT_ONCE, axis=0)
            top = jnp.max(scores, axis=1, keepdims=True)
            weights = jnp.exp2((scores - top) * factor).astype(jnp.bfloat16)
            summed = jnp.dot(weights, value, preferred_element_type=jnp.float32)
            result = (summed[:, :HEAD_SIZE] / summed[:, HEAD_SIZE:]).astype(jnp.bfloat16)
            for n, i in enumerate(heads):
                out_ref[:, i * HEAD_SIZE : (i + 1) * HEAD_SIZE] = result[
                    n * chunk : (n + 1) * chunk
                ]

    needed = 1 + jnp.where(base < span_ref[1], span_ref[0], 0)
    for n, count in enumerate(counts):
        low = counts[n - 1] if n else 0

        @pl.when((needed > low) & (needed <= count))
        def _():
            attend(count)


def attention(queries, key_values, lengths, places):
    rows = queries.shape[0]
    blocks = len(key_values)
    steps = min(blocks, 5)
    counts = sorted({1 + (blocks - 1) * n // (steps - 1) for n in range(steps)})
    chunk = rows // 2
    group_width = GROUP * HEAD_SIZE
    smem = pl.BlockSpec(memory_space=pltpu.SMEM)
    query_spec = pl.BlockSpec((chunk, group_width), lambda g, c: (c, g))
    pair_spec = pl.BlockSpec((2 * rows, KEY_VALUE_HEADS * HEAD_SIZE), lambda g, c: (0, 0))
    area = rows * rows * blocks * QUERY_HEADS
    return pl.pallas_call(
        functools.partial(attention_kernel, counts, rows),
        grid=(KEY_VALUE_HEADS, rows // chunk),
        out_shape=jax.ShapeDtypeStruct(queries.shape, queries.dtype),
        in_specs=[smem, smem, query_spec] + [pair_spec] * blocks,
        out_specs=query_spec,
        scratch_shapes=[
            pltpu.VMEM((rows, blocks * rows), jnp.float32),
            pltpu.VMEM((blocks * rows, KEY_VALUE_HEADS * HEAD_SIZE), jnp.bfloat16),
            pltpu.VMEM((blocks * rows, KEY_VALUE_HEADS * HEAD_SIZE), jnp.bfloat16),
            pltpu.SMEM((2,), jnp.int32),
        ],
        compiler_params=pltpu.CompilerParams(vmem_limit_bytes=40 * 1024 * 1024),
        cost_estimate=pl.CostEstimate(
            flops=4 * area * HEAD_SIZE,
            bytes_accessed=2 * (2 * queries.size + blocks * key_values[0].size),
            transcendentals=area,
        ),
    )(lengths, places, queries, *key_values)


def per_device(queries, keys, values, lengths):
    rows = queries.shape[0]
    count = lax.axis_size("dp") * lax.axis_size("ctx")
    rounds = lax.axis_size("ctx")
    me = lax.axis_index(AXES)
    odd = lax.rem(me, 2)
    is_odd = odd == 1
    own = jnp.concatenate([keys, values], axis=0)

    def back(even, r):
        return 2 * (r + 1) if even else 2 * (rounds - r)

    fetched = []
    for r in range(rounds):
        pairs = [(i - back(i % 2 == 0, r), i) for i in range(count)]
        pairs = [(i, j) for i, j in pairs if i >= 0]
        fetched.append(lax.ppermute(own, AXES, pairs))
    swap = [(i, i ^ 1) for i in range(count)]
    swapped = [lax.ppermute(block, AXES, swap) for block in fetched[:-1]]
    swapped.append(lax.ppermute(jnp.where(is_odd, fetched[-1], own), AXES, swap))

    behind = [jnp.int32(0)]
    for r in range(rounds):
        behind.append(jnp.where(is_odd, back(False, r), back(True, r)))
    for r in range(rounds - 1):
        behind.append(jnp.where(is_odd, 1 + back(True, r), back(False, r) - 1))
    behind.append(jnp.where(is_odd, 1, back(False, rounds - 1) - 1))
    places = jnp.stack([me * rows] + behind).astype(jnp.int32)
    return attention(queries, [own] + fetched + swapped, lengths, places)


def solution(mesh):
    in_specs = (P(AXES, None), P(AXES, None), P(AXES, None), P())
    return jax.shard_map(
        per_device, mesh=mesh, in_specs=in_specs, out_specs=P(AXES, None), check_vma=False
    )
```

```python
import functools
import math

import jax
import jax.numpy as jnp
from jax import lax
from jax.experimental import pallas as pl
from jax.experimental.pallas import tpu as pltpu
from jax.sharding import PartitionSpec as P

HEAD_SIZE = 128
QUERY_HEADS = 32
KEY_VALUE_HEADS = 4
GROUP = QUERY_HEADS // KEY_VALUE_HEADS
HEADS_AT_ONCE = 2
EXCLUDED = -1e30
AXES = ("dp", "ctx")


def attention_kernel(counts, rows, lengths_ref, places_ref, q_hbm, *refs):
    blocks = counts[-1]
    key_hbm, value_hbm = refs[:blocks], refs[blocks : 2 * blocks]
    out_hbm = refs[2 * blocks]
    q_ref, out_ref, bias_ref, key_ref, value_ref = refs[2 * blocks + 1 : 2 * blocks + 6]
    block_sems, q_sems, out_sems = refs[2 * blocks + 6 :]
    first = places_ref[0]
    width = GROUP * HEAD_SIZE

    def group_columns(g):
        return pl.ds(pl.multiple_of(g * width, width), width)

    def query_copy(g):
        at = group_columns(g)
        return pltpu.make_async_copy(q_hbm.at[:, at], q_ref.at[:, at], q_sems.at[g])

    def out_copy(g):
        at = group_columns(g)
        return pltpu.make_async_copy(out_ref.at[:, at], out_hbm.at[:, at], out_sems.at[g])

    block_copies = []
    for b in range(blocks):
        at = pl.ds(pl.multiple_of(places_ref[1 + b] * rows, rows), rows)
        for n, (source, target) in enumerate(((key_hbm, key_ref), (value_hbm, value_ref))):
            block_copies.append(
                pltpu.make_async_copy(source[b], target.at[at, :], block_sems.at[n, b])
            )
    for copy in block_copies[:2]:
        copy.start()
    query_copy(0).start()
    for copy in block_copies[2:]:
        copy.start()
    for g in range(1, KEY_VALUE_HEADS):
        query_copy(g).start()

    query_pos = first + lax.broadcasted_iota(jnp.int32, (rows, rows), 0)

    def later(doc, carried):
        bound, start, first_start = carried
        start = jnp.where(query_pos >= bound, bound, start)
        first_start = jnp.where(first >= bound, bound, first_start)
        return bound + lengths_ref[doc], start, first_start

    zero = jnp.int32(0)
    _, start, first_start = lax.fori_loop(
        0,
        lengths_ref.shape[0],
        later,
        (zero, jnp.zeros((rows, rows), jnp.int32), zero),
        unroll=8,
    )
    needed = 1 + lax.div(first - first_start + (rows - 1), jnp.int32(rows))
    lane = lax.broadcasted_iota(jnp.int32, (rows, rows), 1)
    for b in range(blocks):
        key_pos = first - b * rows + lane
        allowed = key_pos >= start
        if b == 0:
            allowed = allowed & (key_pos <= query_pos)
        bias_ref[:, b * rows : (b + 1) * rows] = jnp.where(
            allowed, jnp.float32(0.0), jnp.float32(EXCLUDED)
        )
    for copy in block_copies:
        copy.wait()

    factor = jnp.float32(math.log2(math.e) / math.sqrt(HEAD_SIZE))

    def attend(count, g):
        reach = count * rows
        columns = pl.ds(pl.multiple_of(g * HEAD_SIZE, HEAD_SIZE), HEAD_SIZE)
        query_copy(g).wait()
        key = key_ref[:reach, columns]
        value = jnp.concatenate(
            [value_ref[:reach, columns], jnp.ones((reach, HEAD_SIZE), jnp.bfloat16)], axis=1
        )
        bias = jnp.concatenate([bias_ref[:, :reach]] * HEADS_AT_ONCE, axis=0)
        for h in range(0, GROUP, HEADS_AT_ONCE):
            heads = [
                pl.ds(pl.multiple_of(g * width + i * HEAD_SIZE, HEAD_SIZE), HEAD_SIZE)
                for i in range(h, h + HEADS_AT_ONCE)
            ]
            q = jnp.concatenate([q_ref[:, at] for at in heads], axis=0)
            scores = lax.dot_general(
                q, key, (((1,), (1,)), ((), ())), preferred_element_type=jnp.float32
            )
            scores = scores + bias
            top = jnp.max(scores, axis=1, keepdims=True)
            weights = jnp.exp2((scores - top) * factor).astype(jnp.bfloat16)
            summed = jnp.dot(weights, value, preferred_element_type=jnp.float32)
            result = (summed[:, :HEAD_SIZE] / summed[:, HEAD_SIZE:]).astype(jnp.bfloat16)
            for n, at in enumerate(heads):
                out_ref[:, at] = result[n * rows : (n + 1) * rows]
        out_copy(g).start()

    for n, count in enumerate(counts):
        low = counts[n - 1] if n else 0

        @pl.when((needed > low) & (needed <= count))
        def _():
            def step(g, _):
                attend(count, g)
                return 0

            lax.fori_loop(0, KEY_VALUE_HEADS, step, 0)

    for g in range(KEY_VALUE_HEADS):
        out_copy(g).wait()


def attention(queries, keys, values, lengths, places):
    rows = queries.shape[0]
    blocks = len(keys)
    steps = min(blocks, 5)
    counts = sorted({1 + (blocks - 1) * n // (steps - 1) for n in range(steps)})
    smem = pl.BlockSpec(memory_space=pltpu.SMEM)
    anywhere = pl.BlockSpec(memory_space=pl.ANY)
    area = rows * rows * blocks * QUERY_HEADS
    return pl.pallas_call(
        functools.partial(attention_kernel, counts, rows),
        out_shape=jax.ShapeDtypeStruct(queries.shape, queries.dtype),
        in_specs=[smem, smem] + [anywhere] * (1 + 2 * blocks),
        out_specs=anywhere,
        scratch_shapes=[
            pltpu.VMEM(queries.shape, queries.dtype),
            pltpu.VMEM(queries.shape, queries.dtype),
            pltpu.VMEM((rows, blocks * rows), jnp.float32),
            pltpu.VMEM((blocks * rows, KEY_VALUE_HEADS * HEAD_SIZE), jnp.bfloat16),
            pltpu.VMEM((blocks * rows, KEY_VALUE_HEADS * HEAD_SIZE), jnp.bfloat16),
            pltpu.SemaphoreType.DMA((2, blocks)),
            pltpu.SemaphoreType.DMA((KEY_VALUE_HEADS,)),
            pltpu.SemaphoreType.DMA((KEY_VALUE_HEADS,)),
        ],
        compiler_params=pltpu.CompilerParams(vmem_limit_bytes=40 * 1024 * 1024),
        cost_estimate=pl.CostEstimate(
            flops=4 * area * HEAD_SIZE,
            bytes_accessed=4 * (queries.size + blocks * keys[0].size),
            transcendentals=area,
        ),
    )(lengths, places, queries, *keys, *values)


def per_device(queries, keys, values, lengths):
    rows = queries.shape[0]
    count = lax.axis_size("dp") * lax.axis_size("ctx")
    rounds = lax.axis_size("ctx")
    me = lax.axis_index(AXES)
    is_odd = lax.rem(me, 2) == 1

    def back(even, r):
        return 2 * (r + 1) if even else 2 * (rounds - r)

    own = (keys, values)
    fetched = []
    for r in range(rounds):
        pairs = [(i - back(i % 2 == 0, r), i) for i in range(count)]
        pairs = [(i, j) for i, j in pairs if i >= 0]
        fetched.append([lax.ppermute(part, AXES, pairs) for part in own])
    swap = [(i, i ^ 1) for i in range(count)]
    swapped = []
    for r in range(rounds):
        parts = fetched[r]
        if r == rounds - 1:
            parts = [jnp.where(is_odd, part, mine) for part, mine in zip(parts, own)]
        swapped.append([lax.ppermute(part, AXES, swap) for part in parts])

    behind = [jnp.int32(0)]
    for r in range(rounds):
        behind.append(jnp.where(is_odd, back(False, r), back(True, r)))
    for r in range(rounds - 1):
        behind.append(jnp.where(is_odd, 1 + back(True, r), back(False, r) - 1))
    behind.append(jnp.where(is_odd, 1, back(False, rounds - 1) - 1))
    places = jnp.stack([me * rows] + behind).astype(jnp.int32)
    blocks = [own] + fetched + swapped
    return attention(queries, [b[0] for b in blocks], [b[1] for b in blocks], lengths, places)


def solution(mesh):
    in_specs = (P(AXES, None), P(AXES, None), P(AXES, None), P())
    return jax.shard_map(
        per_device, mesh=mesh, in_specs=in_specs, out_specs=P(AXES, None), check_vma=False
    )
```

```python
import functools
import math

import jax
import jax.numpy as jnp
from jax import lax
from jax.experimental import pallas as pl
from jax.experimental.pallas import tpu as pltpu
from jax.sharding import PartitionSpec as P

HEAD_SIZE = 128
QUERY_HEADS = 32
KEY_VALUE_HEADS = 4
GROUP = QUERY_HEADS // KEY_VALUE_HEADS
HEADS_AT_ONCE = 2
EXCLUDED = -1e30
AXES = ("dp", "ctx")


def plan_kernel(blocks, rows, lengths_ref, places_ref, bias_ref, needed_ref):
    first = places_ref[0]
    query_pos = first + lax.broadcasted_iota(jnp.int32, (rows, rows), 0)

    def later(doc, carried):
        bound, start, first_start = carried
        start = jnp.where(query_pos >= bound, bound, start)
        first_start = jnp.where(first >= bound, bound, first_start)
        return bound + lengths_ref[doc], start, first_start

    zero = jnp.int32(0)
    _, start, first_start = lax.fori_loop(
        0,
        lengths_ref.shape[0],
        later,
        (zero, jnp.zeros((rows, rows), jnp.int32), zero),
        unroll=8,
    )
    needed_ref[0] = 1 + lax.div(first - first_start + (rows - 1), jnp.int32(rows))
    lane = lax.broadcasted_iota(jnp.int32, (rows, rows), 1)
    for b in range(blocks):
        key_pos = first - places_ref[1 + b] * rows + lane
        allowed = key_pos >= start
        if b == 0:
            allowed = allowed & (key_pos <= query_pos)
        bias_ref[:, b * rows : (b + 1) * rows] = jnp.where(
            allowed, jnp.float32(0.0), jnp.float32(EXCLUDED)
        )


def plan(lengths, places, blocks, rows):
    smem = pl.BlockSpec(memory_space=pltpu.SMEM)
    return pl.pallas_call(
        functools.partial(plan_kernel, blocks, rows),
        out_shape=(
            pltpu.VMEM((rows, blocks * rows), jnp.float32),
            jax.ShapeDtypeStruct((1,), jnp.int32),
        ),
        in_specs=[smem, smem],
        out_specs=(pl.BlockSpec(memory_space=pltpu.VMEM), smem),
        cost_estimate=pl.CostEstimate(flops=1000000, bytes_accessed=1000000, transcendentals=0),
    )(lengths, places)


def attention_kernel(blocks, rows, needed_ref, bias_ref, q_ref, key_ref, value_ref, *refs):
    pair_refs = refs[: blocks - 1]
    out_hbm, out_ref, out_sems = refs[blocks - 1 :]
    width = GROUP * HEAD_SIZE
    needed = needed_ref[0]

    def out_copy(g):
        at = pl.ds(pl.multiple_of(g * width, width), width)
        return pltpu.make_async_copy(out_ref.at[:, at], out_hbm.at[:, at], out_sems.at[g])

    factor = jnp.float32(math.log2(math.e) / math.sqrt(HEAD_SIZE))

    def attend(count, g):
        reach = count * rows
        columns = pl.ds(pl.multiple_of(g * HEAD_SIZE, HEAD_SIZE), HEAD_SIZE)
        behind = pair_refs[: count - 1]
        key = jnp.concatenate(
            [key_ref[:, columns]] + [pair[:rows, columns] for pair in behind], axis=0
        )
        value = jnp.concatenate(
            [value_ref[:, columns]] + [pair[rows:, columns] for pair in behind], axis=0
        )
        value = jnp.concatenate([value, jnp.ones((reach, HEAD_SIZE), jnp.bfloat16)], axis=1)
        bias = jnp.concatenate([bias_ref[:, :reach]] * HEADS_AT_ONCE, axis=0)
        for h in range(0, GROUP, HEADS_AT_ONCE):
            heads = [
                pl.ds(pl.multiple_of(g * width + i * HEAD_SIZE, HEAD_SIZE), HEAD_SIZE)
                for i in range(h, h + HEADS_AT_ONCE)
            ]
            q = jnp.concatenate([q_ref[:, at] for at in heads], axis=0)
            scores = lax.dot_general(
                q, key, (((1,), (1,)), ((), ())), preferred_element_type=jnp.float32
            )
            scores = scores + bias
            top = jnp.max(scores, axis=1, keepdims=True)
            weights = jnp.exp2((scores - top) * factor).astype(jnp.bfloat16)
            summed = jnp.dot(weights, value, preferred_element_type=jnp.float32)
            result = (summed[:, :HEAD_SIZE] / summed[:, HEAD_SIZE:]).astype(jnp.bfloat16)
            for n, at in enumerate(heads):
                out_ref[:, at] = result[n * rows : (n + 1) * rows]
        out_copy(g).start()

    for low, count in ((0, 1), (1, 2), (2, blocks)):
        @pl.when((needed > low) & (needed <= count))
        def _():
            def step(g, _):
                attend(count, g)
                return 0

            lax.fori_loop(0, KEY_VALUE_HEADS, step, 0)

    for g in range(KEY_VALUE_HEADS):
        out_copy(g).wait()


def attention(needed, bias, queries, keys, values, pairs):
    rows = queries.shape[0]
    blocks = 1 + len(pairs)
    area = rows * rows * blocks * QUERY_HEADS
    operands = [bias, queries, keys, values, *pairs]
    operands = [pltpu.with_memory_space_constraint(x, pltpu.VMEM) for x in operands]
    return pl.pallas_call(
        functools.partial(attention_kernel, blocks, rows),
        out_shape=jax.ShapeDtypeStruct(queries.shape, queries.dtype),
        in_specs=[pl.BlockSpec(memory_space=pltpu.SMEM)]
        + [pl.BlockSpec(memory_space=pltpu.VMEM)] * len(operands),
        out_specs=pl.BlockSpec(memory_space=pl.ANY),
        scratch_shapes=[
            pltpu.VMEM(queries.shape, queries.dtype),
            pltpu.SemaphoreType.DMA((KEY_VALUE_HEADS,)),
        ],
        compiler_params=pltpu.CompilerParams(vmem_limit_bytes=40 * 1024 * 1024),
        cost_estimate=pl.CostEstimate(
            flops=4 * area * HEAD_SIZE,
            bytes_accessed=4 * (queries.size + blocks * keys.size),
            transcendentals=area,
        ),
    )(needed, *operands)


def per_device(queries, keys, values, lengths):
    rows = queries.shape[0]
    count = lax.axis_size("dp") * lax.axis_size("ctx")
    rounds = lax.axis_size("ctx")
    me = lax.axis_index(AXES)
    is_odd = lax.rem(me, 2) == 1
    own = jnp.concatenate([keys, values], axis=0)

    def back(even, r):
        return 2 * (r + 1) if even else 2 * (rounds - r)

    fetched = []
    for r in range(rounds):
        pairs = [(i - back(i % 2 == 0, r), i) for i in range(count)]
        pairs = [(i, j) for i, j in pairs if i >= 0]
        fetched.append(lax.ppermute(own, AXES, pairs))
    swap = [(i, i ^ 1) for i in range(count)]
    swapped = [lax.ppermute(block, AXES, swap) for block in fetched[:-1]]
    nearest = lax.ppermute(jnp.where(is_odd, fetched[-1], own), AXES, swap)

    behind = [0, 1]
    for r in range(rounds):
        behind.append(jnp.where(is_odd, back(False, r), back(True, r)))
    for r in range(rounds - 1):
        behind.append(jnp.where(is_odd, 1 + back(True, r), back(False, r) - 1))
    places = jnp.stack([me * rows] + [jnp.int32(b) for b in behind]).astype(jnp.int32)
    bias, needed = plan(lengths, places, len(behind), rows)
    return attention(needed, bias, queries, keys, values, [nearest] + fetched + swapped)


def solution(mesh):
    in_specs = (P(AXES, None), P(AXES, None), P(AXES, None), P())
    return jax.shard_map(
        per_device, mesh=mesh, in_specs=in_specs, out_specs=P(AXES, None), check_vma=False
    )
```

```python
import functools
import math

import jax
import jax.numpy as jnp
from jax import lax
from jax.experimental import pallas as pl
from jax.experimental.pallas import tpu as pltpu
from jax.sharding import PartitionSpec as P

HEAD_SIZE = 128
QUERY_HEADS = 32
KEY_VALUE_HEADS = 4
GROUP = QUERY_HEADS // KEY_VALUE_HEADS
HEADS_AT_ONCE = 4
EXCLUDED = -1e30
AXES = ("dp", "ctx")


FACTOR = math.log2(math.e) / math.sqrt(HEAD_SIZE)


def head_columns(g, i):
    return pl.ds(pl.multiple_of((g * GROUP + i) * HEAD_SIZE, HEAD_SIZE), HEAD_SIZE)


def stacked(ref, g, heads):
    return jnp.concatenate([ref[:, head_columns(g, i)] for i in heads], axis=0)


def spread(ref, g, heads, rows, value):
    for n, i in enumerate(heads):
        ref[:, head_columns(g, i)] = value[n * rows : (n + 1) * rows].astype(ref.dtype)


def with_ones(value):
    return jnp.concatenate([value, jnp.ones(value.shape, value.dtype)], axis=1)


def scores_of(q, key, bias):
    scores = lax.dot_general(
        q, key, (((1,), (1,)), ((), ())), preferred_element_type=jnp.float32
    )
    return scores + jnp.concatenate([bias] * (q.shape[0] // bias.shape[0]), axis=0)


def weights_of(scores, top):
    return jnp.exp2((scores - top) * jnp.float32(FACTOR)).astype(jnp.bfloat16)


def normalised(summed, total):
    inverse = pl.reciprocal(total, approx=True)
    return summed * (inverse * (2.0 - total * inverse))


def own_kernel(
    rounds, rows, lengths_ref, q_ref, key_ref, value_ref,
    bias_ref, flags_ref, top_ref, total_ref, sum_ref, own_bias_ref,
):
    me = lax.axis_index("dp") * lax.axis_size("ctx") + lax.axis_index("ctx")
    first = me * rows
    query_pos = first + lax.broadcasted_iota(jnp.int32, (rows, rows), 0)

    def later(doc, carried):
        bound, start, first_start = carried
        start = jnp.where(query_pos >= bound, bound, start)
        first_start = jnp.where(first >= bound, bound, first_start)
        return bound + lengths_ref[doc], start, first_start

    zero = jnp.int32(0)
    _, start, first_start = lax.fori_loop(
        0,
        lengths_ref.shape[0],
        later,
        (zero, jnp.zeros((rows, rows), jnp.int32), zero),
        unroll=8,
    )
    odd = lax.rem(me, 2)
    flags_ref[0] = lax.div(first - first_start + (rows - 1), jnp.int32(rows))
    flags_ref[1] = odd
    lane = lax.broadcasted_iota(jnp.int32, (rows, rows), 1)

    def bias_of(allowed):
        return jnp.where(allowed, jnp.float32(0.0), jnp.float32(EXCLUDED))

    for b, behind in enumerate(places_behind(rounds, odd == 1)):
        key_pos = first - behind * rows + lane
        bias_ref[:, b * rows : (b + 1) * rows] = bias_of(key_pos >= start)
    key_pos = first + lane
    own_bias_ref[...] = bias_of((key_pos >= start) & (key_pos <= query_pos))

    def step(g, _):
        key, value = key_ref[:, head_columns(0, g)], value_ref[:, head_columns(0, g)]
        value = with_ones(value)
        for h in range(0, GROUP, HEADS_AT_ONCE):
            heads = range(h, h + HEADS_AT_ONCE)
            scores = scores_of(stacked(q_ref, g, heads), key, own_bias_ref[...])
            top = jnp.max(scores, axis=1, keepdims=True)
            summed = jnp.dot(
                weights_of(scores, top), value, preferred_element_type=jnp.float32
            )
            spread(top_ref, g, heads, rows, jnp.broadcast_to(top, scores.shape))
            spread(sum_ref, g, heads, rows, summed[:, :HEAD_SIZE])
            spread(total_ref, g, heads, rows, summed[:, HEAD_SIZE:])
        return 0

    lax.fori_loop(0, KEY_VALUE_HEADS, step, 0)


def in_vmem(*operands):
    return [pltpu.with_memory_space_constraint(x, pltpu.VMEM) for x in operands]


SMEM = pl.BlockSpec(memory_space=pltpu.SMEM)
VMEM = pl.BlockSpec(memory_space=pltpu.VMEM)


def own_part(lengths, queries, keys, values, rounds):
    rows = queries.shape[0]
    partial = pltpu.VMEM(queries.shape, jnp.float32)
    return pl.pallas_call(
        functools.partial(own_kernel, rounds, rows),
        out_shape=(
            pltpu.VMEM((rows, 2 * rounds * rows), jnp.float32),
            jax.ShapeDtypeStruct((2,), jnp.int32),
            partial,
            partial,
            partial,
        ),
        in_specs=[SMEM, VMEM, VMEM, VMEM],
        out_specs=(VMEM, SMEM, VMEM, VMEM, VMEM),
        scratch_shapes=[pltpu.VMEM((rows, rows), jnp.float32)],
        compiler_params=pltpu.CompilerParams(vmem_limit_bytes=32 * 1024 * 1024),
        cost_estimate=pl.CostEstimate(
            flops=4 * 10**9, bytes_accessed=16 * 10**6, transcendentals=rows * queries.size
        ),
    )(lengths, *in_vmem(queries, keys, values))


def behind_kernel(blocks, rows, flags_ref, bias_ref, q_ref, top_ref, total_ref, sum_ref, *refs):
    pair_refs = refs[:blocks]
    out_hbm, out_ref, out_sems = refs[blocks:]
    width = GROUP * HEAD_SIZE
    needed = flags_ref[0]

    def out_copy(g):
        at = pl.ds(pl.multiple_of(g * width, width), width)
        return pltpu.make_async_copy(out_ref.at[:, at], out_hbm.at[:, at], out_sems.at[g])

    def attend(count, g):
        columns = head_columns(0, g)
        if count:
            key = jnp.concatenate([pair[:rows, columns] for pair in pair_refs[:count]], axis=0)
            value = jnp.concatenate([pair[rows:, columns] for pair in pair_refs[:count]], axis=0)
            value = with_ones(value)
            bias = bias_ref[:, : count * rows]
        for h in range(0, GROUP, HEADS_AT_ONCE):
            heads = range(h, h + HEADS_AT_ONCE)
            summed = stacked(sum_ref, g, heads)
            total = stacked(total_ref, g, heads)
            if count:
                scores = scores_of(stacked(q_ref, g, heads), key, bias)
                own_top = stacked(top_ref, g, heads)
                top = jnp.maximum(own_top, jnp.max(scores, axis=1, keepdims=True))
                fade = jnp.exp2((own_top - top) * jnp.float32(FACTOR))
                more = jnp.dot(
                    weights_of(scores, jnp.concatenate([top] * count, axis=1)),
                    value,
                    preferred_element_type=jnp.float32,
                )
                summed = summed * fade + more[:, :HEAD_SIZE]
                total = total * fade + more[:, HEAD_SIZE:]
            spread(out_ref, g, heads, rows, normalised(summed, total))
        out_copy(g).start()

    for low, count in ((-1, 0), (0, 1), (1, blocks)):
        @pl.when((needed > low) & (needed <= count))
        def _():
            def step(g, _):
                attend(count, g)
                return 0

            lax.fori_loop(0, KEY_VALUE_HEADS, step, 0)

    for g in range(KEY_VALUE_HEADS):
        out_copy(g).wait()


def behind_part(flags, bias, queries, top, total, summed, pairs):
    rows = queries.shape[0]
    area = rows * rows * len(pairs) * QUERY_HEADS
    operands = in_vmem(bias, queries, top, total, summed, *pairs)
    return pl.pallas_call(
        functools.partial(behind_kernel, len(pairs), rows),
        out_shape=jax.ShapeDtypeStruct(queries.shape, queries.dtype),
        in_specs=[SMEM] + [VMEM] * len(operands),
        out_specs=pl.BlockSpec(memory_space=pl.ANY),
        scratch_shapes=[
            pltpu.VMEM(queries.shape, queries.dtype),
            pltpu.SemaphoreType.DMA((KEY_VALUE_HEADS,)),
        ],
        compiler_params=pltpu.CompilerParams(vmem_limit_bytes=32 * 1024 * 1024),
        cost_estimate=pl.CostEstimate(
            flops=4 * area * HEAD_SIZE,
            bytes_accessed=16 * queries.size,
            transcendentals=area,
        ),
    )(flags, *operands)


def fetch_back(rounds, even, r):
    return 2 * (r + 1) if even else 2 * (rounds - r)


def places_behind(rounds, is_odd):
    behind = [1]
    for r in range(rounds):
        behind.append(jnp.where(is_odd, fetch_back(rounds, False, r), fetch_back(rounds, True, r)))
    for r in range(rounds - 1):
        behind.append(
            jnp.where(is_odd, 1 + fetch_back(rounds, True, r), fetch_back(rounds, False, r) - 1)
        )
    return behind


def per_device(queries, keys, values, lengths):
    count = lax.axis_size("dp") * lax.axis_size("ctx")
    rounds = lax.axis_size("ctx")
    own = jnp.concatenate([keys, values], axis=0)

    fetched = []
    for r in range(rounds):
        pairs = [(i - fetch_back(rounds, i % 2 == 0, r), i) for i in range(count)]
        pairs = [(i, j) for i, j in pairs if i >= 0]
        fetched.append(lax.ppermute(own, AXES, pairs))
    bias, flags, top, total, summed = own_part(lengths, queries, keys, values, rounds)
    is_odd = flags[1] == 1
    swap = [(i, i ^ 1) for i in range(count)]
    swapped = [lax.ppermute(block, AXES, swap) for block in fetched[:-1]]
    nearest = lax.ppermute(jnp.where(is_odd, fetched[-1], own), AXES, swap)
    return behind_part(
        flags, bias, queries, top, total, summed, [nearest] + fetched + swapped
    )


def solution(mesh):
    in_specs = (P(AXES, None), P(AXES, None), P(AXES, None), P())
    return jax.shard_map(
        per_device, mesh=mesh, in_specs=in_specs, out_specs=P(AXES, None), check_vma=False
    )
```

```python
import functools
import math

import jax
import jax.numpy as jnp
from jax import lax
from jax.experimental import pallas as pl
from jax.experimental.pallas import tpu as pltpu
from jax.sharding import PartitionSpec as P

HEAD_SIZE = 128
QUERY_HEADS = 32
KEY_VALUE_HEADS = 4
GROUP = QUERY_HEADS // KEY_VALUE_HEADS
HEADS_AT_ONCE = 4
EXCLUDED = -1e30
AXES = ("dp", "ctx")


FACTOR = math.log2(math.e) / math.sqrt(HEAD_SIZE)


def head_columns(i):
    return slice(i * HEAD_SIZE, (i + 1) * HEAD_SIZE)


def stacked(ref, heads):
    return jnp.concatenate([ref[:, head_columns(i)] for i in heads], axis=0)


def spread(ref, heads, rows, value):
    for n, i in enumerate(heads):
        ref[:, head_columns(i)] = value[n * rows : (n + 1) * rows].astype(ref.dtype)


def with_ones(value):
    return jnp.concatenate([value, jnp.ones(value.shape, value.dtype)], axis=1)


def scores_of(q, key, bias):
    scores = lax.dot_general(
        q, key, (((1,), (1,)), ((), ())), preferred_element_type=jnp.float32
    )
    return scores + jnp.concatenate([bias] * (q.shape[0] // bias.shape[0]), axis=0)


def weights_of(scores, top):
    return jnp.exp2((scores - top) * jnp.float32(FACTOR)).astype(jnp.bfloat16)


def normalised(summed, total):
    inverse = pl.reciprocal(total, approx=True)
    return summed * (inverse * (2.0 - total * inverse))


def chains():
    return [
        (range(h, h + HEADS_AT_ONCE), h // GROUP) for h in range(0, QUERY_HEADS, HEADS_AT_ONCE)
    ]


def in_turn(*stages):
    runs = chains()
    results = {}
    for turn in range(len(runs) + len(stages) - 1):
        for n, stage in enumerate(stages):
            i = turn - n
            if 0 <= i < len(runs):
                results[i] = stage(*runs[i], *results.pop(i, ()))


def pack_kernel(key_hbm, value_hbm, out_ref, sems):
    rows = key_hbm.shape[0]
    copies = [
        pltpu.make_async_copy(key_hbm, out_ref.at[:rows], sems.at[0]),
        pltpu.make_async_copy(value_hbm, out_ref.at[rows:], sems.at[1]),
    ]
    for copy in copies:
        copy.start()
    for copy in copies:
        copy.wait()


def pack(keys, values):
    rows, width = keys.shape
    return pl.pallas_call(
        pack_kernel,
        out_shape=pltpu.VMEM((2 * rows, width), keys.dtype),
        in_specs=[HBM, HBM],
        out_specs=VMEM,
        scratch_shapes=[pltpu.SemaphoreType.DMA((2,))],
    )(*in_hbm(keys, values))


def own_kernel(
    rounds, rows, own_ref, lengths_hbm, q_hbm,
    bias_ref, flags_ref, odd_ref, q_ref, top_ref, total_ref, sum_ref,
    own_bias_ref, lengths_ref, lengths_sem, q_sems,
):
    lengths_copy = pltpu.make_async_copy(lengths_hbm, lengths_ref, lengths_sem)
    lengths_copy.start()
    width = GROUP * HEAD_SIZE
    q_copies = []
    for g in range(KEY_VALUE_HEADS):
        at = slice(g * width, (g + 1) * width)
        q_copies.append(pltpu.make_async_copy(q_hbm.at[:, at], q_ref.at[:, at], q_sems.at[g]))
        q_copies[g].start()
    me = lax.axis_index("dp") * lax.axis_size("ctx") + lax.axis_index("ctx")
    odd = lax.rem(me, 2)
    odd_ref[...] = jnp.full(odd_ref.shape, odd, jnp.int32)
    first = me * rows
    query_pos = first + lax.broadcasted_iota(jnp.int32, (rows, rows), 0)
    lengths_copy.wait()

    def later(doc, carried):
        bound, start, first_start = carried
        start = jnp.where(query_pos >= bound, bound, start)
        first_start = jnp.where(first >= bound, bound, first_start)
        return bound + lengths_ref[doc], start, first_start

    zero = jnp.int32(0)
    _, start, first_start = lax.fori_loop(
        0,
        lengths_ref.shape[0],
        later,
        (zero, jnp.zeros((rows, rows), jnp.int32), zero),
        unroll=8,
    )
    flags_ref[0] = lax.div(first - first_start + (rows - 1), jnp.int32(rows))
    lane = lax.broadcasted_iota(jnp.int32, (rows, rows), 1)

    def bias_of(allowed):
        return jnp.where(allowed, jnp.float32(0.0), jnp.float32(EXCLUDED))

    key_pos = first + lane
    own_bias_ref[...] = bias_of((key_pos >= start) & (key_pos <= query_pos))
    for b, behind in enumerate(places_behind(rounds, odd == 1)):
        key_pos = first - behind * rows + lane
        bias_ref[:, b * rows : (b + 1) * rows] = bias_of(key_pos >= start)

    def match(heads, g):
        if heads[0] % GROUP == 0:
            q_copies[g].wait()
        return (scores_of(stacked(q_ref, heads), own_ref[:rows, head_columns(g)], own_bias_ref[...]),)

    def weigh(heads, g, scores):
        top = jnp.max(scores, axis=1, keepdims=True)
        spread(top_ref, heads, rows, jnp.broadcast_to(top, scores.shape))
        return (weights_of(scores, top),)

    def gather(heads, g, weights):
        value = with_ones(own_ref[rows:, head_columns(g)])
        summed = jnp.dot(weights, value, preferred_element_type=jnp.float32)
        spread(sum_ref, heads, rows, summed[:, :HEAD_SIZE])
        spread(total_ref, heads, rows, summed[:, HEAD_SIZE:])

    in_turn(match, weigh, gather)


def in_vmem(*operands):
    return [pltpu.with_memory_space_constraint(x, pltpu.VMEM) for x in operands]


def in_hbm(*operands):
    return [pltpu.with_memory_space_constraint(x, pltpu.HBM) for x in operands]


SMEM = pl.BlockSpec(memory_space=pltpu.SMEM)
VMEM = pl.BlockSpec(memory_space=pltpu.VMEM)
HBM = pl.BlockSpec(memory_space=pltpu.HBM)


def own_part(lengths, queries, own, rounds):
    rows = queries.shape[0]
    partial = pltpu.VMEM(queries.shape, jnp.float32)
    return pl.pallas_call(
        functools.partial(own_kernel, rounds, rows),
        out_shape=(
            pltpu.VMEM((rows, 2 * rounds * rows), jnp.float32),
            jax.ShapeDtypeStruct((1,), jnp.int32),
            pltpu.VMEM((1, own.shape[1]), jnp.int32),
            pltpu.VMEM(queries.shape, queries.dtype),
            partial,
            partial,
            partial,
        ),
        in_specs=[VMEM, HBM, HBM],
        out_specs=(VMEM, SMEM, VMEM, VMEM, VMEM, VMEM, VMEM),
        scratch_shapes=[
            pltpu.VMEM((rows, rows), jnp.float32),
            pltpu.SMEM(lengths.shape, jnp.int32),
            pltpu.SemaphoreType.DMA,
            pltpu.SemaphoreType.DMA((KEY_VALUE_HEADS,)),
        ],
        compiler_params=pltpu.CompilerParams(vmem_limit_bytes=32 * 1024 * 1024),
        cost_estimate=pl.CostEstimate(
            flops=4 * 10**9, bytes_accessed=16 * 10**6, transcendentals=rows * queries.size
        ),
    )(*in_vmem(own), *in_hbm(lengths, queries))


def behind_kernel(blocks, rows, flags_ref, bias_ref, q_ref, top_ref, total_ref, sum_ref, *refs):
    pair_refs = refs[:blocks]
    out_hbm, out_ref, out_sems = refs[blocks:]
    width = GROUP * HEAD_SIZE
    needed = flags_ref[0]

    def out_copy(g):
        at = slice(g * width, (g + 1) * width)
        return pltpu.make_async_copy(out_ref.at[:, at], out_hbm.at[:, at], out_sems.at[g])

    def finish(heads, g, summed, total):
        spread(out_ref, heads, rows, normalised(summed, total))
        if heads[-1] % GROUP == GROUP - 1:
            out_copy(g).start()

    def attend(count):
        behind = pair_refs[:count]

        def match(heads, g):
            key = jnp.concatenate([pair[:rows, head_columns(g)] for pair in behind], axis=0)
            return (scores_of(stacked(q_ref, heads), key, bias_ref[:, : count * rows]),)

        def weigh(heads, g, scores):
            own_top = stacked(top_ref, heads)
            top = jnp.maximum(own_top, jnp.max(scores, axis=1, keepdims=True))
            fade = jnp.exp2((own_top - top) * jnp.float32(FACTOR))
            return weights_of(scores, jnp.concatenate([top] * count, axis=1)), fade

        def gather(heads, g, weights, fade):
            value = jnp.concatenate([pair[rows:, head_columns(g)] for pair in behind], axis=0)
            more = jnp.dot(weights, with_ones(value), preferred_element_type=jnp.float32)
            summed = stacked(sum_ref, heads) * fade + more[:, :HEAD_SIZE]
            total = stacked(total_ref, heads) * fade + more[:, HEAD_SIZE:]
            finish(heads, g, summed, total)

        in_turn(match, weigh, gather)

    @pl.when(needed == 0)
    def _():
        in_turn(lambda heads, g: finish(heads, g, stacked(sum_ref, heads), stacked(total_ref, heads)))

    @pl.when(needed == 1)
    def _():
        attend(1)

    @pl.when(needed > 1)
    def _():
        attend(blocks)

    for g in range(KEY_VALUE_HEADS):
        out_copy(g).wait()


def behind_part(flags, bias, queries, top, total, summed, pairs):
    rows = queries.shape[0]
    area = rows * rows * len(pairs) * QUERY_HEADS
    operands = in_vmem(bias, queries, top, total, summed, *pairs)
    return pl.pallas_call(
        functools.partial(behind_kernel, len(pairs), rows),
        out_shape=jax.ShapeDtypeStruct(queries.shape, queries.dtype),
        in_specs=[SMEM] + [VMEM] * len(operands),
        out_specs=HBM,
        scratch_shapes=[
            pltpu.VMEM(queries.shape, queries.dtype),
            pltpu.SemaphoreType.DMA((KEY_VALUE_HEADS,)),
        ],
        compiler_params=pltpu.CompilerParams(vmem_limit_bytes=32 * 1024 * 1024),
        cost_estimate=pl.CostEstimate(
            flops=4 * area * HEAD_SIZE,
            bytes_accessed=16 * queries.size,
            transcendentals=area,
        ),
    )(flags, *operands)


def fetch_back(rounds, even, r):
    return 2 * (r + 1) if even else 2 * (rounds - r)


def places_behind(rounds, is_odd):
    behind = [1]
    for r in range(rounds):
        behind.append(jnp.where(is_odd, fetch_back(rounds, False, r), fetch_back(rounds, True, r)))
    for r in range(rounds - 1):
        behind.append(
            jnp.where(is_odd, 1 + fetch_back(rounds, True, r), fetch_back(rounds, False, r) - 1)
        )
    return behind


def per_device(queries, keys, values, lengths):
    count = lax.axis_size("dp") * lax.axis_size("ctx")
    rounds = lax.axis_size("ctx")
    own = pack(keys, values)

    fetched = []
    for r in range(rounds):
        pairs = [(i - fetch_back(rounds, i % 2 == 0, r), i) for i in range(count)]
        pairs = [(i, j) for i, j in pairs if i >= 0]
        fetched.append(lax.ppermute(own, AXES, pairs))
    bias, flags, odd, queries, top, total, summed = own_part(lengths, queries, own, rounds)
    swap = [(i, i ^ 1) for i in range(count)]
    swapped = [lax.ppermute(block, AXES, swap) for block in fetched[:-1]]
    nearest = lax.ppermute(jnp.where(odd == 1, fetched[-1], own), AXES, swap)
    return behind_part(
        flags, bias, queries, top, total, summed, [nearest] + fetched + swapped
    )


def solution(mesh):
    in_specs = (P(AXES, None), P(AXES, None), P(AXES, None), P())
    return jax.shard_map(
        per_device, mesh=mesh, in_specs=in_specs, out_specs=P(AXES, None), check_vma=False
    )
```

```python
import functools
import math

import jax
import jax.numpy as jnp
from jax import lax
from jax.experimental import pallas as pl
from jax.experimental.pallas import tpu as pltpu
from jax.sharding import PartitionSpec as P

HEAD_SIZE = 128
QUERY_HEADS = 32
KEY_VALUE_HEADS = 4
GROUP = QUERY_HEADS // KEY_VALUE_HEADS
HEADS_AT_ONCE = 4
EXCLUDED = -1e30
AXES = ("dp", "ctx")


FACTOR = math.log2(math.e) / math.sqrt(HEAD_SIZE)


def head_columns(i):
    return slice(i * HEAD_SIZE, (i + 1) * HEAD_SIZE)


def stacked(ref, heads):
    return jnp.concatenate([ref[:, head_columns(i)] for i in heads], axis=0)


def spread(ref, heads, rows, value):
    for n, i in enumerate(heads):
        ref[:, head_columns(i)] = value[n * rows : (n + 1) * rows].astype(ref.dtype)


def with_ones(value):
    return jnp.concatenate([value, jnp.ones(value.shape, value.dtype)], axis=1)


def scores_of(q, key, bias):
    scores = lax.dot_general(
        q, key, (((1,), (1,)), ((), ())), preferred_element_type=jnp.float32
    )
    return scores + jnp.concatenate([bias] * (q.shape[0] // bias.shape[0]), axis=0)


def weights_of(scores, top):
    return jnp.exp2((scores - top) * jnp.float32(FACTOR)).astype(jnp.bfloat16)


def normalised(summed, total):
    inverse = pl.reciprocal(total, approx=True)
    return summed * (inverse * (2.0 - total * inverse))


def chains():
    return [
        (range(h, h + HEADS_AT_ONCE), h // GROUP) for h in range(0, QUERY_HEADS, HEADS_AT_ONCE)
    ]


def in_turn(*stages):
    runs = chains()
    results = {}
    for turn in range(len(runs) + len(stages) - 1):
        for n, stage in enumerate(stages):
            i = turn - n
            if 0 <= i < len(runs):
                results[i] = stage(*runs[i], *results.pop(i, ()))


def pack_kernel(key_hbm, value_hbm, *refs):
    *outs, sems = refs
    rows = key_hbm.shape[0]
    copies = []
    for n, out in enumerate(outs):
        copies.append(pltpu.make_async_copy(key_hbm, out.at[:rows], sems.at[n, 0]))
        copies.append(pltpu.make_async_copy(value_hbm, out.at[rows:], sems.at[n, 1]))
    for copy in copies:
        copy.start()
    for copy in copies:
        copy.wait()


def pack(keys, values):
    rows, width = keys.shape
    packed = pltpu.VMEM((2 * rows, width), keys.dtype)
    return pl.pallas_call(
        pack_kernel,
        out_shape=(packed, packed),
        in_specs=[HBM, HBM],
        out_specs=(VMEM, VMEM),
        scratch_shapes=[pltpu.SemaphoreType.DMA((2, 2))],
    )(*in_hbm(keys, values))


def own_kernel(
    rounds, rows, own_ref, lengths_hbm, q_hbm,
    _, bias_ref, needed_ref, q_ref, top_ref, total_ref, sum_ref,
    own_bias_ref, lengths_ref, lengths_sem, q_sems,
):
    lengths_copy = pltpu.make_async_copy(lengths_hbm, lengths_ref, lengths_sem)
    lengths_copy.start()
    width = GROUP * HEAD_SIZE
    q_copies = []
    for g in range(KEY_VALUE_HEADS):
        at = slice(g * width, (g + 1) * width)
        q_copies.append(pltpu.make_async_copy(q_hbm.at[:, at], q_ref.at[:, at], q_sems.at[g]))
        q_copies[g].start()
    me = lax.axis_index("dp") * lax.axis_size("ctx") + lax.axis_index("ctx")
    first = me * rows
    query_pos = first + lax.broadcasted_iota(jnp.int32, (rows, rows), 0)
    lengths_copy.wait()

    def later(doc, carried):
        bound, start, first_start = carried
        start = jnp.where(query_pos >= bound, bound, start)
        first_start = jnp.where(first >= bound, bound, first_start)
        return bound + lengths_ref[doc], start, first_start

    zero = jnp.int32(0)
    _, start, first_start = lax.fori_loop(
        0,
        lengths_ref.shape[0],
        later,
        (zero, jnp.zeros((rows, rows), jnp.int32), zero),
        unroll=8,
    )
    needed_ref[0] = lax.div(first - first_start + (rows - 1), jnp.int32(rows))
    lane = lax.broadcasted_iota(jnp.int32, (rows, rows), 1)

    def bias_of(allowed):
        return jnp.where(allowed, jnp.float32(0.0), jnp.float32(EXCLUDED))

    key_pos = first + lane
    own_bias_ref[...] = bias_of((key_pos >= start) & (key_pos <= query_pos))
    for b in range(2 * rounds):
        key_pos = first - (b + 1) * rows + lane
        bias_ref[:, b * rows : (b + 1) * rows] = bias_of(key_pos >= start)

    def match(heads, g):
        if heads[0] % GROUP == 0:
            q_copies[g].wait()
        return (scores_of(stacked(q_ref, heads), own_ref[:rows, head_columns(g)], own_bias_ref[...]),)

    def weigh(heads, g, scores):
        top = jnp.max(scores, axis=1, keepdims=True)
        spread(top_ref, heads, rows, jnp.broadcast_to(top, scores.shape))
        return (weights_of(scores, top),)

    def gather(heads, g, weights):
        value = with_ones(own_ref[rows:, head_columns(g)])
        summed = jnp.dot(weights, value, preferred_element_type=jnp.float32)
        spread(sum_ref, heads, rows, summed[:, :HEAD_SIZE])
        spread(total_ref, heads, rows, summed[:, HEAD_SIZE:])

    in_turn(match, weigh, gather)


def in_vmem(*operands):
    return [pltpu.with_memory_space_constraint(x, pltpu.VMEM) for x in operands]


def in_hbm(*operands):
    return [pltpu.with_memory_space_constraint(x, pltpu.HBM) for x in operands]


SMEM = pl.BlockSpec(memory_space=pltpu.SMEM)
VMEM = pl.BlockSpec(memory_space=pltpu.VMEM)
HBM = pl.BlockSpec(memory_space=pltpu.HBM)


def own_part(lengths, queries, own, rounds):
    rows = queries.shape[0]
    partial = pltpu.VMEM(queries.shape, jnp.float32)
    return pl.pallas_call(
        functools.partial(own_kernel, rounds, rows),
        out_shape=(
            pltpu.VMEM(own.shape, own.dtype),
            pltpu.VMEM((rows, 2 * rounds * rows), jnp.float32),
            jax.ShapeDtypeStruct((1,), jnp.int32),
            pltpu.VMEM(queries.shape, queries.dtype),
            partial,
            partial,
            partial,
        ),
        in_specs=[VMEM, HBM, HBM],
        out_specs=(VMEM, VMEM, SMEM, VMEM, VMEM, VMEM, VMEM),
        input_output_aliases={0: 0},
        scratch_shapes=[
            pltpu.VMEM((rows, rows), jnp.float32),
            pltpu.SMEM(lengths.shape, jnp.int32),
            pltpu.SemaphoreType.DMA,
            pltpu.SemaphoreType.DMA((KEY_VALUE_HEADS,)),
        ],
        compiler_params=pltpu.CompilerParams(vmem_limit_bytes=32 * 1024 * 1024),
        cost_estimate=pl.CostEstimate(
            flops=4 * 10**9, bytes_accessed=16 * 10**6, transcendentals=rows * queries.size
        ),
    )(*in_vmem(own), *in_hbm(lengths, queries))


def behind_kernel(
    before, last, rows, needed_ref, bias_ref, q_ref, swapped_ref, further_ref, top_ref, total_ref, sum_ref, *refs
):
    width = GROUP * HEAD_SIZE
    beyond = needed_ref[0] - before
    nearer_ref = swapped_ref.at[1 - lax.rem(lax.axis_index("ctx"), 2)]
    if last:
        out_hbm, out_ref, out_sems = refs

        def out_copy(g):
            at = slice(g * width, (g + 1) * width)
            return pltpu.make_async_copy(out_ref.at[:, at], out_hbm.at[:, at], out_sems.at[g])

    else:
        _, new_top_ref, new_total_ref, new_sum_ref = refs

    def finish(heads, g, summed, total):
        if last:
            spread(out_ref, heads, rows, normalised(summed, total))
            if heads[-1] % GROUP == GROUP - 1:
                out_copy(g).start()
        else:
            spread(new_sum_ref, heads, rows, summed)
            spread(new_total_ref, heads, rows, total)

    def attend(count):
        pairs = (nearer_ref, further_ref)[:count]

        def match(heads, g):
            key = jnp.concatenate([pair[:rows, head_columns(g)] for pair in pairs], axis=0)
            bias = bias_ref[:, before * rows : (before + count) * rows]
            return (scores_of(stacked(q_ref, heads), key, bias),)

        def weigh(heads, g, scores):
            old_top = stacked(top_ref, heads)
            top = jnp.maximum(old_top, jnp.max(scores, axis=1, keepdims=True))
            fade = jnp.exp2((old_top - top) * jnp.float32(FACTOR))
            if not last:
                spread(new_top_ref, heads, rows, top)
            return weights_of(scores, jnp.concatenate([top] * count, axis=1)), fade

        def gather(heads, g, weights, fade):
            value = jnp.concatenate([pair[rows:, head_columns(g)] for pair in pairs], axis=0)
            more = jnp.dot(weights, with_ones(value), preferred_element_type=jnp.float32)
            summed = stacked(sum_ref, heads) * fade + more[:, :HEAD_SIZE]
            total = stacked(total_ref, heads) * fade + more[:, HEAD_SIZE:]
            finish(heads, g, summed, total)

        in_turn(match, weigh, gather)

    @pl.when(beyond > 1)
    def _():
        attend(2)

    @pl.when(beyond == 1)
    def _():
        attend(1)

    if last:
        @pl.when(beyond < 1)
        def _():
            in_turn(
                lambda heads, g: finish(heads, g, stacked(sum_ref, heads), stacked(total_ref, heads))
            )

        for g in range(KEY_VALUE_HEADS):
            out_copy(g).wait()


def behind_part(before, last, needed, bias, queries, swapped, further, parts):
    rows = queries.shape[0]
    area = rows * rows * 2 * QUERY_HEADS
    operands = in_vmem(bias, queries, swapped, further, *parts)
    if last:
        out_shape = jax.ShapeDtypeStruct(queries.shape, queries.dtype)
        out_specs = HBM
        scratch = [
            pltpu.VMEM(queries.shape, queries.dtype),
            pltpu.SemaphoreType.DMA((KEY_VALUE_HEADS,)),
        ]
        aliases = {}
    else:
        kept = (further, *parts)
        out_shape = tuple(pltpu.VMEM(part.shape, part.dtype) for part in kept)
        out_specs = (VMEM,) * len(kept)
        scratch = []
        aliases = {4 + n: n for n in range(len(kept))}
    return pl.pallas_call(
        functools.partial(behind_kernel, before, last, rows),
        out_shape=out_shape,
        in_specs=[SMEM] + [VMEM] * len(operands),
        out_specs=out_specs,
        scratch_shapes=scratch,
        input_output_aliases=aliases,
        compiler_params=pltpu.CompilerParams(vmem_limit_bytes=32 * 1024 * 1024),
        cost_estimate=pl.CostEstimate(
            flops=4 * area, bytes_accessed=queries.size, transcendentals=0
        ),
    )(needed, *operands)


def per_device(queries, keys, values, lengths):
    count = lax.axis_size("dp") * lax.axis_size("ctx")
    rounds = lax.axis_size("ctx")

    def from_behind(block, r):
        by = 2 * (r + 1)
        return lax.ppermute(block, AXES, [(i, i + by) for i in range(count - by)])

    packed, own = pack(keys, values)
    fetched = [from_behind(packed, 0)]
    own, bias, needed, queries, *parts = own_part(lengths, queries, own, rounds)
    fetched += [from_behind(own, r) for r in range(1, rounds)]
    cores = [[i, i + 1] for i in range(0, rounds, 2)]
    nearer = own
    for r, further in enumerate(fetched):
        swapped = lax.all_to_all(
            jnp.stack([further, nearer]), "ctx", 0, 0, axis_index_groups=cores
        )
        last = r == rounds - 1
        result = behind_part(2 * r, last, needed, bias, queries, swapped, further, parts)
        if not last:
            nearer, *parts = result
    return result


def solution(mesh):
    in_specs = (P(AXES, None), P(AXES, None), P(AXES, None), P())
    return jax.shard_map(
        per_device, mesh=mesh, in_specs=in_specs, out_specs=P(AXES, None), check_vma=False
    )
```

```python
import functools
import math

import jax
import jax.numpy as jnp
from jax import lax
from jax.experimental import pallas as pl
from jax.experimental.pallas import tpu as pltpu
from jax.sharding import PartitionSpec as P

HEAD_SIZE = 128
QUERY_HEADS = 32
KEY_VALUE_HEADS = 4
GROUP = QUERY_HEADS // KEY_VALUE_HEADS
HEADS_AT_ONCE = 4
EXCLUDED = -1e30
AXES = ("dp", "ctx")


FACTOR = math.log2(math.e) / math.sqrt(HEAD_SIZE)


def head_columns(i):
    return slice(i * HEAD_SIZE, (i + 1) * HEAD_SIZE)


def stacked(ref, heads):
    return jnp.concatenate([ref[:, head_columns(i)] for i in heads], axis=0)


def spread(ref, heads, rows, value):
    for n, i in enumerate(heads):
        ref[:, head_columns(i)] = value[n * rows : (n + 1) * rows].astype(ref.dtype)


def with_ones(value):
    return jnp.concatenate([value, jnp.ones(value.shape, value.dtype)], axis=1)


def scores_of(q, key, bias):
    scores = lax.dot_general(
        q, key, (((1,), (1,)), ((), ())), preferred_element_type=jnp.float32
    )
    return scores + jnp.concatenate([bias] * (q.shape[0] // bias.shape[0]), axis=0)


def weights_of(scores, top):
    return jnp.exp2((scores - top) * jnp.float32(FACTOR)).astype(jnp.bfloat16)


def normalised(summed, total):
    inverse = pl.reciprocal(total, approx=True)
    return summed * (inverse * (2.0 - total * inverse))


def chains():
    return [
        (range(h, h + HEADS_AT_ONCE), h // GROUP) for h in range(0, QUERY_HEADS, HEADS_AT_ONCE)
    ]


def in_turn(*stages):
    runs = chains()
    results = {}
    for turn in range(len(runs) + len(stages) - 1):
        for n, stage in enumerate(stages):
            i = turn - n
            if 0 <= i < len(runs):
                results[i] = stage(*runs[i], *results.pop(i, ()))


def pack_kernel(key_hbm, value_hbm, *refs):
    *outs, sems = refs
    rows = key_hbm.shape[0]
    copies = []
    for n, out in enumerate(outs):
        copies.append(pltpu.make_async_copy(key_hbm, out.at[:rows], sems.at[n, 0]))
        copies.append(pltpu.make_async_copy(value_hbm, out.at[rows:], sems.at[n, 1]))
    for copy in copies:
        copy.start()
    for copy in copies:
        copy.wait()


def pack(keys, values):
    rows, width = keys.shape
    packed = pltpu.VMEM((2 * rows, width), keys.dtype)
    return pl.pallas_call(
        pack_kernel,
        out_shape=(packed, packed),
        in_specs=[HBM, HBM],
        out_specs=(VMEM, VMEM),
        scratch_shapes=[pltpu.SemaphoreType.DMA((2, 2))],
    )(*in_hbm(keys, values))


def own_kernel(
    rounds, rows, own_ref, lengths_hbm, q_hbm,
    _, bias_ref, needed_ref, q_ref, top_ref, total_ref, sum_ref,
    own_bias_ref, lengths_ref, lengths_sem, q_sems,
):
    lengths_copy = pltpu.make_async_copy(lengths_hbm, lengths_ref, lengths_sem)
    lengths_copy.start()
    width = GROUP * HEAD_SIZE
    q_copies = []
    for g in range(KEY_VALUE_HEADS):
        at = slice(g * width, (g + 1) * width)
        q_copies.append(pltpu.make_async_copy(q_hbm.at[:, at], q_ref.at[:, at], q_sems.at[g]))
        q_copies[g].start()
    me = lax.axis_index("dp") * lax.axis_size("ctx") + lax.axis_index("ctx")
    first = me * rows
    query_pos = first + lax.broadcasted_iota(jnp.int32, (rows, rows), 0)
    lengths_copy.wait()

    def later(doc, carried):
        bound, start, first_start = carried
        start = jnp.where(query_pos >= bound, bound, start)
        first_start = jnp.where(first >= bound, bound, first_start)
        return bound + lengths_ref[doc], start, first_start

    zero = jnp.int32(0)
    _, start, first_start = lax.fori_loop(
        0,
        lengths_ref.shape[0],
        later,
        (zero, jnp.zeros((rows, rows), jnp.int32), zero),
        unroll=8,
    )
    needed_ref[0] = lax.div(first - first_start + (rows - 1), jnp.int32(rows))
    lane = lax.broadcasted_iota(jnp.int32, (rows, rows), 1)

    def bias_of(allowed):
        return jnp.where(allowed, jnp.float32(0.0), jnp.float32(EXCLUDED))

    key_pos = first + lane
    own_bias_ref[...] = bias_of((key_pos >= start) & (key_pos <= query_pos))
    for b in range(2 * rounds):
        key_pos = first - (b + 1) * rows + lane
        bias_ref[:, b * rows : (b + 1) * rows] = bias_of(key_pos >= start)

    def match(heads, g):
        if heads[0] % GROUP == 0:
            q_copies[g].wait()
        return (scores_of(stacked(q_ref, heads), own_ref[:rows, head_columns(g)], own_bias_ref[...]),)

    def weigh(heads, g, scores):
        top = jnp.max(scores, axis=1, keepdims=True)
        spread(top_ref, heads, rows, jnp.broadcast_to(top, scores.shape))
        return (weights_of(scores, top),)

    def gather(heads, g, weights):
        value = with_ones(own_ref[rows:, head_columns(g)])
        summed = jnp.dot(weights, value, preferred_element_type=jnp.float32)
        spread(sum_ref, heads, rows, summed[:, :HEAD_SIZE])
        spread(total_ref, heads, rows, summed[:, HEAD_SIZE:])

    in_turn(match, weigh, gather)


def in_vmem(*operands):
    return [pltpu.with_memory_space_constraint(x, pltpu.VMEM) for x in operands]


def in_hbm(*operands):
    return [pltpu.with_memory_space_constraint(x, pltpu.HBM) for x in operands]


SMEM = pl.BlockSpec(memory_space=pltpu.SMEM)
VMEM = pl.BlockSpec(memory_space=pltpu.VMEM)
HBM = pl.BlockSpec(memory_space=pltpu.HBM)


def own_part(lengths, queries, own, rounds):
    rows = queries.shape[0]
    partial = pltpu.VMEM(queries.shape, jnp.float32)
    return pl.pallas_call(
        functools.partial(own_kernel, rounds, rows),
        out_shape=(
            pltpu.VMEM(own.shape, own.dtype),
            pltpu.VMEM((rows, 2 * rounds * rows), jnp.float32),
            jax.ShapeDtypeStruct((1,), jnp.int32),
            pltpu.VMEM(queries.shape, queries.dtype),
            partial,
            partial,
            partial,
        ),
        in_specs=[VMEM, HBM, HBM],
        out_specs=(VMEM, VMEM, SMEM, VMEM, VMEM, VMEM, VMEM),
        input_output_aliases={0: 0},
        scratch_shapes=[
            pltpu.VMEM((rows, rows), jnp.float32),
            pltpu.SMEM(lengths.shape, jnp.int32),
            pltpu.SemaphoreType.DMA,
            pltpu.SemaphoreType.DMA((KEY_VALUE_HEADS,)),
        ],
        compiler_params=pltpu.CompilerParams(vmem_limit_bytes=32 * 1024 * 1024),
        cost_estimate=pl.CostEstimate(
            flops=4 * 10**9, bytes_accessed=16 * 10**6, transcendentals=rows * queries.size
        ),
    )(*in_vmem(own), *in_hbm(lengths, queries))


def behind_kernel(
    before, last, rows, needed_ref, bias_ref, q_ref, *refs
):
    width = GROUP * HEAD_SIZE
    beyond = needed_ref[0] - before
    *near_refs, further_ref, top_ref, total_ref, sum_ref = refs[: 5 if last else 6]
    refs = refs[5 if last else 6 :]
    if last:
        near_refs = (near_refs[0].at[:rows], near_refs[0].at[rows:])
    pairs = (near_refs, (further_ref.at[:rows], further_ref.at[rows:]))
    if last:
        out_hbm, out_ref, out_sems = refs

        def out_copy(g):
            at = slice(g * width, (g + 1) * width)
            return pltpu.make_async_copy(out_ref.at[:, at], out_hbm.at[:, at], out_sems.at[g])

    else:
        _, new_top_ref, new_total_ref, new_sum_ref = refs

    def finish(heads, g, summed, total):
        if last:
            spread(out_ref, heads, rows, normalised(summed, total))
            if heads[-1] % GROUP == GROUP - 1:
                out_copy(g).start()
        else:
            spread(new_sum_ref, heads, rows, summed)
            spread(new_total_ref, heads, rows, total)

    def attend(count):
        def match(heads, g):
            key = jnp.concatenate([key[:, head_columns(g)] for key, _ in pairs[:count]], axis=0)
            bias = bias_ref[:, before * rows : (before + count) * rows]
            return (scores_of(stacked(q_ref, heads), key, bias),)

        def weigh(heads, g, scores):
            old_top = stacked(top_ref, heads)
            top = jnp.maximum(old_top, jnp.max(scores, axis=1, keepdims=True))
            fade = jnp.exp2((old_top - top) * jnp.float32(FACTOR))
            if not last:
                spread(new_top_ref, heads, rows, top)
            return weights_of(scores, jnp.concatenate([top] * count, axis=1)), fade

        def gather(heads, g, weights, fade):
            value = jnp.concatenate([value[:, head_columns(g)] for _, value in pairs[:count]], axis=0)
            more = jnp.dot(weights, with_ones(value), preferred_element_type=jnp.float32)
            summed = stacked(sum_ref, heads) * fade + more[:, :HEAD_SIZE]
            total = stacked(total_ref, heads) * fade + more[:, HEAD_SIZE:]
            finish(heads, g, summed, total)

        in_turn(match, weigh, gather)

    @pl.when(beyond > 1)
    def _():
        attend(2)

    @pl.when(beyond == 1)
    def _():
        attend(1)

    if last:
        @pl.when(beyond < 1)
        def _():
            in_turn(
                lambda heads, g: finish(heads, g, stacked(sum_ref, heads), stacked(total_ref, heads))
            )

        for g in range(KEY_VALUE_HEADS):
            out_copy(g).wait()


def behind_part(before, last, needed, bias, queries, halves, further, parts):
    rows = queries.shape[0]
    area = rows * rows * 2 * QUERY_HEADS
    operands = in_vmem(bias, queries, *halves, further, *parts)
    if last:
        out_shape = jax.ShapeDtypeStruct(queries.shape, queries.dtype)
        out_specs = HBM
        scratch = [
            pltpu.VMEM(queries.shape, queries.dtype),
            pltpu.SemaphoreType.DMA((KEY_VALUE_HEADS,)),
        ]
        aliases = {}
    else:
        kept = (further, *parts)
        out_shape = tuple(pltpu.VMEM(part.shape, part.dtype) for part in kept)
        out_specs = (VMEM,) * len(kept)
        scratch = []
        aliases = {5 + n: n for n in range(len(kept))}
    return pl.pallas_call(
        functools.partial(behind_kernel, before, last, rows),
        out_shape=out_shape,
        in_specs=[SMEM] + [VMEM] * len(operands),
        out_specs=out_specs,
        scratch_shapes=scratch,
        input_output_aliases=aliases,
        compiler_params=pltpu.CompilerParams(vmem_limit_bytes=32 * 1024 * 1024),
        cost_estimate=pl.CostEstimate(
            flops=4 * area, bytes_accessed=queries.size, transcendentals=0
        ),
    )(needed, *operands)


def per_device(queries, keys, values, lengths):
    count = lax.axis_size("dp") * lax.axis_size("ctx")
    rounds = lax.axis_size("ctx")

    def from_behind(block, r):
        by = 2 * (r + 1)
        return lax.ppermute(block, AXES, [(i, i + by) for i in range(count - by)])

    packed, own = pack(keys, values)
    fetched = [from_behind(packed, 0)]
    own, bias, needed, queries, *parts = own_part(lengths, queries, own, rounds)
    fetched += [from_behind(own, r) for r in range(1, rounds)]
    swap = [(i, i ^ 1) for i in range(count)]
    is_odd = lax.rem(lax.axis_index("ctx"), 2) == 1
    nearer = own
    for r, further in enumerate(fetched):
        last = r == rounds - 1
        cuts = 1 if last else 2
        halves = []
        for old, new in zip(jnp.split(nearer, cuts), jnp.split(further, cuts)):
            halves.append(lax.ppermute(jnp.where(is_odd, new, old), AXES, swap))
        result = behind_part(2 * r, last, needed, bias, queries, halves, further, parts)
        if not last:
            nearer, *parts = result
    return result


def solution(mesh):
    in_specs = (P(AXES, None), P(AXES, None), P(AXES, None), P())
    return jax.shard_map(
        per_device, mesh=mesh, in_specs=in_specs, out_specs=P(AXES, None), check_vma=False
    )
```

```python
import functools
import math

import jax
import jax.numpy as jnp
from jax import lax
from jax.experimental import pallas as pl
from jax.experimental.pallas import tpu as pltpu
from jax.sharding import PartitionSpec as P

HEAD_SIZE = 128
QUERY_HEADS = 32
KEY_VALUE_HEADS = 4
GROUP = QUERY_HEADS // KEY_VALUE_HEADS
HEADS_AT_ONCE = 4
EXCLUDED = -1e30
AXES = ("dp", "ctx")


FACTOR = math.log2(math.e) / math.sqrt(HEAD_SIZE)


def head_columns(i):
    return slice(i * HEAD_SIZE, (i + 1) * HEAD_SIZE)


def stacked(ref, heads):
    return jnp.concatenate([ref[:, head_columns(i)] for i in heads], axis=0)


def spread(ref, heads, rows, value):
    for n, i in enumerate(heads):
        ref[:, head_columns(i)] = value[n * rows : (n + 1) * rows].astype(ref.dtype)


def with_ones(value):
    return jnp.concatenate([value, jnp.ones(value.shape, value.dtype)], axis=1)


def scores_of(q, key, bias):
    scores = lax.dot_general(
        q, key, (((1,), (1,)), ((), ())), preferred_element_type=jnp.float32
    )
    return scores + jnp.concatenate([bias] * (q.shape[0] // bias.shape[0]), axis=0)


def weights_of(scores, top):
    return jnp.exp2((scores - top) * jnp.float32(FACTOR)).astype(jnp.bfloat16)


def normalised(summed, total):
    inverse = pl.reciprocal(total, approx=True)
    return summed * (inverse * (2.0 - total * inverse))


def chains():
    return [
        (range(h, h + HEADS_AT_ONCE), h // GROUP) for h in range(0, QUERY_HEADS, HEADS_AT_ONCE)
    ]


def in_turn(*stages):
    runs = chains()
    results = {}
    for turn in range(len(runs) + len(stages) - 1):
        for n, stage in enumerate(stages):
            i = turn - n
            if 0 <= i < len(runs):
                results[i] = stage(*runs[i], *results.pop(i, ()))


def pack_kernel(key_hbm, value_hbm, *refs):
    *outs, sems = refs
    rows = key_hbm.shape[0]
    copies = []
    for n, out in enumerate(outs):
        copies.append(pltpu.make_async_copy(key_hbm, out.at[:rows], sems.at[n, 0]))
        copies.append(pltpu.make_async_copy(value_hbm, out.at[rows:], sems.at[n, 1]))
    for copy in copies:
        copy.start()
    for copy in copies:
        copy.wait()


def pack(keys, values):
    rows, width = keys.shape
    packed = pltpu.VMEM((2 * rows, width), keys.dtype)
    return pl.pallas_call(
        pack_kernel,
        out_shape=(packed, packed),
        in_specs=[HBM, HBM],
        out_specs=(VMEM, VMEM),
        scratch_shapes=[pltpu.SemaphoreType.DMA((2, 2))],
    )(*in_hbm(keys, values))


def own_kernel(
    rounds, rows, own_ref, lengths_hbm, q_hbm,
    _, bias_ref, needed_ref, q_ref, top_ref, total_ref, sum_ref,
    own_bias_ref, lengths_ref, lengths_sem, q_sems,
):
    lengths_copy = pltpu.make_async_copy(lengths_hbm, lengths_ref, lengths_sem)
    lengths_copy.start()
    width = GROUP * HEAD_SIZE
    q_copies = []
    for g in range(KEY_VALUE_HEADS):
        at = slice(g * width, (g + 1) * width)
        q_copies.append(pltpu.make_async_copy(q_hbm.at[:, at], q_ref.at[:, at], q_sems.at[g]))
        q_copies[g].start()
    me = lax.axis_index("dp") * lax.axis_size("ctx") + lax.axis_index("ctx")
    first = me * rows
    query_pos = first + lax.broadcasted_iota(jnp.int32, (rows, rows), 0)
    lengths_copy.wait()

    def later(doc, carried):
        bound, start, first_start = carried
        start = jnp.where(query_pos >= bound, bound, start)
        first_start = jnp.where(first >= bound, bound, first_start)
        return bound + lengths_ref[doc], start, first_start

    zero = jnp.int32(0)
    _, start, first_start = lax.fori_loop(
        0,
        lengths_ref.shape[0],
        later,
        (zero, jnp.zeros((rows, rows), jnp.int32), zero),
        unroll=8,
    )
    needed_ref[0] = lax.div(first - first_start + (rows - 1), jnp.int32(rows))
    lane = lax.broadcasted_iota(jnp.int32, (rows, rows), 1)

    def bias_of(allowed):
        return jnp.where(allowed, jnp.float32(0.0), jnp.float32(EXCLUDED))

    key_pos = first + lane
    own_bias_ref[...] = bias_of((key_pos >= start) & (key_pos <= query_pos))
    for b in range(2 * rounds):
        key_pos = first - (b + 1) * rows + lane
        bias_ref[:, b * rows : (b + 1) * rows] = bias_of(key_pos >= start)

    def match(heads, g):
        if heads[0] % GROUP == 0:
            q_copies[g].wait()
        return (scores_of(stacked(q_ref, heads), own_ref[:rows, head_columns(g)], own_bias_ref[...]),)

    def weigh(heads, g, scores):
        top = jnp.max(scores, axis=1, keepdims=True)
        spread(top_ref, heads, rows, jnp.broadcast_to(top, scores.shape))
        return (weights_of(scores, top),)

    def gather(heads, g, weights):
        value = with_ones(own_ref[rows:, head_columns(g)])
        summed = jnp.dot(weights, value, preferred_element_type=jnp.float32)
        spread(sum_ref, heads, rows, summed[:, :HEAD_SIZE])
        spread(total_ref, heads, rows, summed[:, HEAD_SIZE:])

    in_turn(match, weigh, gather)


def in_vmem(*operands):
    return [pltpu.with_memory_space_constraint(x, pltpu.VMEM) for x in operands]


def in_hbm(*operands):
    return [pltpu.with_memory_space_constraint(x, pltpu.HBM) for x in operands]


SMEM = pl.BlockSpec(memory_space=pltpu.SMEM)
VMEM = pl.BlockSpec(memory_space=pltpu.VMEM)
HBM = pl.BlockSpec(memory_space=pltpu.HBM)


def own_part(lengths, queries, own, rounds):
    rows = queries.shape[0]
    partial = pltpu.VMEM(queries.shape, jnp.float32)
    return pl.pallas_call(
        functools.partial(own_kernel, rounds, rows),
        out_shape=(
            pltpu.VMEM(own.shape, own.dtype),
            pltpu.VMEM((rows, 2 * rounds * rows), jnp.float32),
            jax.ShapeDtypeStruct((1,), jnp.int32),
            pltpu.VMEM(queries.shape, queries.dtype),
            partial,
            partial,
            partial,
        ),
        in_specs=[VMEM, HBM, HBM],
        out_specs=(VMEM, VMEM, SMEM, VMEM, VMEM, VMEM, VMEM),
        input_output_aliases={0: 0},
        scratch_shapes=[
            pltpu.VMEM((rows, rows), jnp.float32),
            pltpu.SMEM(lengths.shape, jnp.int32),
            pltpu.SemaphoreType.DMA,
            pltpu.SemaphoreType.DMA((KEY_VALUE_HEADS,)),
        ],
        compiler_params=pltpu.CompilerParams(vmem_limit_bytes=10 * 1024 * 1024),
        cost_estimate=pl.CostEstimate(
            flops=4 * 10**9, bytes_accessed=16 * 10**6, transcendentals=rows * queries.size
        ),
    )(*in_vmem(own), *in_hbm(lengths, queries))


def behind_kernel(
    before, last, rows, needed_ref, bias_ref, q_ref, *refs
):
    width = GROUP * HEAD_SIZE
    beyond = needed_ref[0] - before
    *near_refs, further_ref, top_ref, total_ref, sum_ref = refs[: 5 if last else 6]
    refs = refs[5 if last else 6 :]
    if last:
        near_refs = (near_refs[0].at[:rows], near_refs[0].at[rows:])
    pairs = (near_refs, (further_ref.at[:rows], further_ref.at[rows:]))
    if last:
        out_hbm, out_ref, out_sems = refs

        def out_copy(g):
            at = slice(g * width, (g + 1) * width)
            return pltpu.make_async_copy(out_ref.at[:, at], out_hbm.at[:, at], out_sems.at[g])

    else:
        _, new_top_ref, new_total_ref, new_sum_ref = refs

    def finish(heads, g, summed, total):
        if last:
            spread(out_ref, heads, rows, normalised(summed, total))
            if heads[-1] % GROUP == GROUP - 1:
                out_copy(g).start()
        else:
            spread(new_sum_ref, heads, rows, summed)
            spread(new_total_ref, heads, rows, total)

    def attend(count):
        def match(heads, g):
            key = jnp.concatenate([key[:, head_columns(g)] for key, _ in pairs[:count]], axis=0)
            bias = bias_ref[:, before * rows : (before + count) * rows]
            return (scores_of(stacked(q_ref, heads), key, bias),)

        def weigh(heads, g, scores):
            old_top = stacked(top_ref, heads)
            top = jnp.maximum(old_top, jnp.max(scores, axis=1, keepdims=True))
            fade = jnp.exp2((old_top - top) * jnp.float32(FACTOR))
            if not last:
                spread(new_top_ref, heads, rows, top)
            return weights_of(scores, jnp.concatenate([top] * count, axis=1)), fade

        def gather(heads, g, weights, fade):
            value = jnp.concatenate([value[:, head_columns(g)] for _, value in pairs[:count]], axis=0)
            more = jnp.dot(weights, with_ones(value), preferred_element_type=jnp.float32)
            summed = stacked(sum_ref, heads) * fade + more[:, :HEAD_SIZE]
            total = stacked(total_ref, heads) * fade + more[:, HEAD_SIZE:]
            finish(heads, g, summed, total)

        in_turn(match, weigh, gather)

    @pl.when(beyond > 1)
    def _():
        attend(2)

    @pl.when(beyond == 1)
    def _():
        attend(1)

    if last:
        @pl.when(beyond < 1)
        def _():
            in_turn(
                lambda heads, g: finish(heads, g, stacked(sum_ref, heads), stacked(total_ref, heads))
            )

        for g in range(KEY_VALUE_HEADS):
            out_copy(g).wait()


def behind_part(before, last, needed, bias, queries, halves, further, parts):
    rows = queries.shape[0]
    area = rows * rows * 2 * QUERY_HEADS
    operands = in_vmem(bias, queries, *halves, further, *parts)
    if last:
        out_shape = jax.ShapeDtypeStruct(queries.shape, queries.dtype)
        out_specs = HBM
        scratch = [
            pltpu.VMEM(queries.shape, queries.dtype),
            pltpu.SemaphoreType.DMA((KEY_VALUE_HEADS,)),
        ]
        aliases = {}
    else:
        kept = (further, *parts)
        out_shape = tuple(pltpu.VMEM(part.shape, part.dtype) for part in kept)
        out_specs = (VMEM,) * len(kept)
        scratch = []
        aliases = {5 + n: n for n in range(len(kept))}
    return pl.pallas_call(
        functools.partial(behind_kernel, before, last, rows),
        out_shape=out_shape,
        in_specs=[SMEM] + [VMEM] * len(operands),
        out_specs=out_specs,
        scratch_shapes=scratch,
        input_output_aliases=aliases,
        compiler_params=pltpu.CompilerParams(vmem_limit_bytes=10 * 1024 * 1024),
        cost_estimate=pl.CostEstimate(
            flops=4 * area, bytes_accessed=queries.size, transcendentals=0
        ),
    )(needed, *operands)


def per_device(queries, keys, values, lengths):
    count = lax.axis_size("dp") * lax.axis_size("ctx")
    rounds = lax.axis_size("ctx")

    def from_behind(block, r):
        by = 2 * (r + 1)
        return lax.ppermute(block, AXES, [(i, i + by) for i in range(count - by)])

    packed, own = pack(keys, values)
    fetched = [from_behind(packed, 0)]
    own, bias, needed, queries, *parts = own_part(lengths, queries, own, rounds)
    fetched += [from_behind(own, r) for r in range(1, rounds)]
    swap = [(i, i ^ 1) for i in range(count)]
    is_odd = lax.rem(lax.axis_index("ctx"), 2) == 1
    nearer = own
    for r, further in enumerate(fetched):
        last = r == rounds - 1
        cuts = 1 if last else 2
        halves = []
        for old, new in zip(jnp.split(nearer, cuts), jnp.split(further, cuts)):
            halves.append(lax.ppermute(jnp.where(is_odd, new, old), AXES, swap))
        result = behind_part(2 * r, last, needed, bias, queries, halves, further, parts)
        if not last:
            nearer, *parts = result
    return result


def solution(mesh):
    in_specs = (P(AXES, None), P(AXES, None), P(AXES, None), P())
    return jax.shard_map(
        per_device, mesh=mesh, in_specs=in_specs, out_specs=P(AXES, None), check_vma=False
    )
```

```python
import functools
import math

import jax
import jax.numpy as jnp
from jax import lax
from jax.experimental import pallas as pl
from jax.experimental.pallas import tpu as pltpu
from jax.sharding import PartitionSpec as P

HEAD_SIZE = 128
QUERY_HEADS = 32
KEY_VALUE_HEADS = 4
GROUP = QUERY_HEADS // KEY_VALUE_HEADS
HEADS_AT_ONCE = 4
EXCLUDED = -1e30
AXES = ("dp", "ctx")


FACTOR = math.log2(math.e) / math.sqrt(HEAD_SIZE)


def head_columns(i):
    return slice(i * HEAD_SIZE, (i + 1) * HEAD_SIZE)


def stacked(ref, heads):
    return jnp.concatenate([ref[:, head_columns(i)] for i in heads], axis=0)


def spread(ref, heads, rows, value):
    for n, i in enumerate(heads):
        ref[:, head_columns(i)] = value[n * rows : (n + 1) * rows].astype(ref.dtype)


def with_ones(value):
    return jnp.concatenate([value, jnp.ones(value.shape, value.dtype)], axis=1)


def scores_of(q, key, bias):
    scores = lax.dot_general(
        q, key, (((1,), (1,)), ((), ())), preferred_element_type=jnp.float32
    )
    return scores + jnp.concatenate([bias] * (q.shape[0] // bias.shape[0]), axis=0)


def weights_of(scores, top):
    return jnp.exp2((scores - top) * jnp.float32(FACTOR)).astype(jnp.bfloat16)


def normalised(summed, total):
    inverse = pl.reciprocal(total, approx=True)
    return summed * (inverse * (2.0 - total * inverse))


def chains():
    return [
        (range(h, h + HEADS_AT_ONCE), h // GROUP) for h in range(0, QUERY_HEADS, HEADS_AT_ONCE)
    ]


def in_turn(*stages):
    runs = chains()
    results = {}
    for turn in range(len(runs) + len(stages) - 1):
        for n, stage in enumerate(stages):
            i = turn - n
            if 0 <= i < len(runs):
                results[i] = stage(*runs[i], *results.pop(i, ()))


def pack_kernel(key_hbm, value_hbm, *refs):
    *outs, sems = refs
    rows = key_hbm.shape[0]
    copies = []
    for n, out in enumerate(outs):
        copies.append(pltpu.make_async_copy(key_hbm, out.at[:rows], sems.at[n, 0]))
        copies.append(pltpu.make_async_copy(value_hbm, out.at[rows:], sems.at[n, 1]))
    for copy in copies:
        copy.start()
    for copy in copies:
        copy.wait()


def pack(keys, values):
    rows, width = keys.shape
    packed = pltpu.VMEM((2 * rows, width), keys.dtype)
    return pl.pallas_call(
        pack_kernel,
        out_shape=(packed, packed),
        in_specs=[HBM, HBM],
        out_specs=(VMEM, VMEM),
        scratch_shapes=[pltpu.SemaphoreType.DMA((2, 2))],
        compiler_params=pltpu.CompilerParams(vmem_limit_bytes=1024 * 1024),
    )(*in_hbm(keys, values))


def own_kernel(
    rounds, rows, own_ref, lengths_hbm, q_hbm,
    _, bias_ref, needed_ref, q_ref, top_ref, total_ref, sum_ref,
    own_bias_ref, lengths_ref, lengths_sem, q_sems,
):
    lengths_copy = pltpu.make_async_copy(lengths_hbm, lengths_ref, lengths_sem)
    lengths_copy.start()
    width = GROUP * HEAD_SIZE
    q_copies = []
    for g in range(KEY_VALUE_HEADS):
        at = slice(g * width, (g + 1) * width)
        q_copies.append(pltpu.make_async_copy(q_hbm.at[:, at], q_ref.at[:, at], q_sems.at[g]))
        q_copies[g].start()
    me = lax.axis_index("dp") * lax.axis_size("ctx") + lax.axis_index("ctx")
    first = me * rows
    query_pos = first + lax.broadcasted_iota(jnp.int32, (rows, rows), 0)
    lengths_copy.wait()

    def later(doc, carried):
        bound, start, first_start = carried
        start = jnp.where(query_pos >= bound, bound, start)
        first_start = jnp.where(first >= bound, bound, first_start)
        return bound + lengths_ref[doc], start, first_start

    zero = jnp.int32(0)
    _, start, first_start = lax.fori_loop(
        0,
        lengths_ref.shape[0],
        later,
        (zero, jnp.zeros((rows, rows), jnp.int32), zero),
        unroll=8,
    )
    needed_ref[0] = lax.div(first - first_start + (rows - 1), jnp.int32(rows))
    lane = lax.broadcasted_iota(jnp.int32, (rows, rows), 1)

    def bias_of(allowed):
        return jnp.where(allowed, jnp.float32(0.0), jnp.float32(EXCLUDED))

    key_pos = first + lane
    own_bias_ref[...] = bias_of((key_pos >= start) & (key_pos <= query_pos))
    for b in range(2 * rounds):
        key_pos = first - (b + 1) * rows + lane
        bias_ref[:, b * rows : (b + 1) * rows] = bias_of(key_pos >= start)

    def match(heads, g):
        if heads[0] % GROUP == 0:
            q_copies[g].wait()
        return (scores_of(stacked(q_ref, heads), own_ref[:rows, head_columns(g)], own_bias_ref[...]),)

    def weigh(heads, g, scores):
        top = jnp.max(scores, axis=1, keepdims=True)
        spread(top_ref, heads, rows, jnp.broadcast_to(top, scores.shape))
        return (weights_of(scores, top),)

    def gather(heads, g, weights):
        value = with_ones(own_ref[rows:, head_columns(g)])
        summed = jnp.dot(weights, value, preferred_element_type=jnp.float32)
        spread(sum_ref, heads, rows, summed[:, :HEAD_SIZE])
        spread(total_ref, heads, rows, summed[:, HEAD_SIZE:])

    in_turn(match, weigh, gather)


def in_vmem(*operands):
    return [pltpu.with_memory_space_constraint(x, pltpu.VMEM) for x in operands]


def in_hbm(*operands):
    return [pltpu.with_memory_space_constraint(x, pltpu.HBM) for x in operands]


SMEM = pl.BlockSpec(memory_space=pltpu.SMEM)
VMEM = pl.BlockSpec(memory_space=pltpu.VMEM)
HBM = pl.BlockSpec(memory_space=pltpu.HBM)


def own_part(lengths, queries, own, rounds):
    rows = queries.shape[0]
    partial = pltpu.VMEM(queries.shape, jnp.float32)
    return pl.pallas_call(
        functools.partial(own_kernel, rounds, rows),
        out_shape=(
            pltpu.VMEM(own.shape, own.dtype),
            pltpu.VMEM((rows, 2 * rounds * rows), jnp.float32),
            jax.ShapeDtypeStruct((1,), jnp.int32),
            pltpu.VMEM(queries.shape, queries.dtype),
            partial,
            partial,
            partial,
        ),
        in_specs=[VMEM, HBM, HBM],
        out_specs=(VMEM, VMEM, SMEM, VMEM, VMEM, VMEM, VMEM),
        input_output_aliases={0: 0},
        scratch_shapes=[
            pltpu.VMEM((rows, rows), jnp.float32),
            pltpu.SMEM(lengths.shape, jnp.int32),
            pltpu.SemaphoreType.DMA,
            pltpu.SemaphoreType.DMA((KEY_VALUE_HEADS,)),
        ],
        compiler_params=pltpu.CompilerParams(vmem_limit_bytes=10 * 1024 * 1024),
        cost_estimate=pl.CostEstimate(
            flops=4 * 10**9, bytes_accessed=16 * 10**6, transcendentals=rows * queries.size
        ),
    )(*in_vmem(own), *in_hbm(lengths, queries))


def behind_kernel(
    before, last, rows, needed_ref, bias_ref, q_ref, *refs
):
    width = GROUP * HEAD_SIZE
    beyond = needed_ref[0] - before
    *near_refs, further_ref, top_ref, total_ref, sum_ref = refs[: 5 if last else 6]
    refs = refs[5 if last else 6 :]
    if last:
        near_refs = (near_refs[0].at[:rows], near_refs[0].at[rows:])
    pairs = (near_refs, (further_ref.at[:rows], further_ref.at[rows:]))
    if last:
        out_hbm, out_ref, out_sems = refs

        def out_copy(g):
            at = slice(g * width, (g + 1) * width)
            return pltpu.make_async_copy(out_ref.at[:, at], out_hbm.at[:, at], out_sems.at[g])

    else:
        _, new_top_ref, new_total_ref, new_sum_ref = refs

    def finish(heads, g, summed, total):
        if last:
            spread(out_ref, heads, rows, normalised(summed, total))
            if heads[-1] % GROUP == GROUP - 1:
                out_copy(g).start()
        else:
            spread(new_sum_ref, heads, rows, summed)
            spread(new_total_ref, heads, rows, total)

    def attend(count):
        def match(heads, g):
            key = jnp.concatenate([key[:, head_columns(g)] for key, _ in pairs[:count]], axis=0)
            bias = bias_ref[:, before * rows : (before + count) * rows]
            return (scores_of(stacked(q_ref, heads), key, bias),)

        def weigh(heads, g, scores):
            old_top = stacked(top_ref, heads)
            top = jnp.maximum(old_top, jnp.max(scores, axis=1, keepdims=True))
            fade = jnp.exp2((old_top - top) * jnp.float32(FACTOR))
            if not last:
                spread(new_top_ref, heads, rows, top)
            return weights_of(scores, jnp.concatenate([top] * count, axis=1)), fade

        def gather(heads, g, weights, fade):
            value = jnp.concatenate([value[:, head_columns(g)] for _, value in pairs[:count]], axis=0)
            more = jnp.dot(weights, with_ones(value), preferred_element_type=jnp.float32)
            summed = stacked(sum_ref, heads) * fade + more[:, :HEAD_SIZE]
            total = stacked(total_ref, heads) * fade + more[:, HEAD_SIZE:]
            finish(heads, g, summed, total)

        in_turn(match, weigh, gather)

    @pl.when(beyond > 1)
    def _():
        attend(2)

    @pl.when(beyond == 1)
    def _():
        attend(1)

    if last:
        @pl.when(beyond < 1)
        def _():
            in_turn(
                lambda heads, g: finish(heads, g, stacked(sum_ref, heads), stacked(total_ref, heads))
            )

        for g in range(KEY_VALUE_HEADS):
            out_copy(g).wait()


def behind_part(before, last, needed, bias, queries, halves, further, parts):
    rows = queries.shape[0]
    area = rows * rows * 2 * QUERY_HEADS
    operands = in_vmem(bias, queries, *halves, further, *parts)
    if last:
        out_shape = jax.ShapeDtypeStruct(queries.shape, queries.dtype)
        out_specs = HBM
        scratch = [
            pltpu.VMEM(queries.shape, queries.dtype),
            pltpu.SemaphoreType.DMA((KEY_VALUE_HEADS,)),
        ]
        aliases = {}
    else:
        kept = (further, *parts)
        out_shape = tuple(pltpu.VMEM(part.shape, part.dtype) for part in kept)
        out_specs = (VMEM,) * len(kept)
        scratch = []
        aliases = {5 + n: n for n in range(len(kept))}
    return pl.pallas_call(
        functools.partial(behind_kernel, before, last, rows),
        out_shape=out_shape,
        in_specs=[SMEM] + [VMEM] * len(operands),
        out_specs=out_specs,
        scratch_shapes=scratch,
        input_output_aliases=aliases,
        compiler_params=pltpu.CompilerParams(vmem_limit_bytes=10 * 1024 * 1024),
        cost_estimate=pl.CostEstimate(
            flops=4 * area, bytes_accessed=queries.size, transcendentals=0
        ),
    )(needed, *operands)


def per_device(queries, keys, values, lengths):
    count = lax.axis_size("dp") * lax.axis_size("ctx")
    rounds = lax.axis_size("ctx")

    def from_behind(block, r):
        by = 2 * (r + 1)
        return lax.ppermute(block, AXES, [(i, i + by) for i in range(count - by)])

    packed, own = pack(keys, values)
    fetched = [from_behind(packed, 0)]
    own, bias, needed, queries, *parts = own_part(lengths, queries, own, rounds)
    fetched += [from_behind(own, r) for r in range(1, rounds)]
    swap = [(i, i ^ 1) for i in range(count)]
    is_odd = lax.rem(lax.axis_index("ctx"), 2) == 1
    nearer = own
    for r, further in enumerate(fetched):
        last = r == rounds - 1
        cuts = 1 if last else 2
        halves = []
        for old, new in zip(jnp.split(nearer, cuts), jnp.split(further, cuts)):
            halves.append(lax.ppermute(jnp.where(is_odd, new, old), AXES, swap))
        result = behind_part(2 * r, last, needed, bias, queries, halves, further, parts)
        if not last:
            nearer, *parts = result
    return result


def solution(mesh):
    in_specs = (P(AXES, None), P(AXES, None), P(AXES, None), P())
    return jax.shard_map(
        per_device, mesh=mesh, in_specs=in_specs, out_specs=P(AXES, None), check_vma=False
    )
```

```python
import functools
import math

import jax
import jax.numpy as jnp
from jax import lax
from jax.experimental import pallas as pl
from jax.experimental.pallas import tpu as pltpu
from jax.sharding import PartitionSpec as P

HEAD_SIZE = 128
QUERY_HEADS = 32
KEY_VALUE_HEADS = 4
GROUP = QUERY_HEADS // KEY_VALUE_HEADS
HEADS_AT_ONCE = 4
EXCLUDED = -1e30
AXES = ("dp", "ctx")


FACTOR = math.log2(math.e) / math.sqrt(HEAD_SIZE)


def head_columns(i):
    return slice(i * HEAD_SIZE, (i + 1) * HEAD_SIZE)


def stacked(ref, heads):
    return jnp.concatenate([ref[:, head_columns(i)] for i in heads], axis=0)


def spread(ref, heads, rows, value):
    for n, i in enumerate(heads):
        ref[:, head_columns(i)] = value[n * rows : (n + 1) * rows].astype(ref.dtype)


def with_ones(value):
    return jnp.concatenate([value, jnp.ones(value.shape, value.dtype)], axis=1)


def scores_of(q, key, bias):
    scores = lax.dot_general(
        q, key, (((1,), (1,)), ((), ())), preferred_element_type=jnp.float32
    )
    return scores + jnp.concatenate([bias] * (q.shape[0] // bias.shape[0]), axis=0)


def weights_of(scores, top):
    return jnp.exp2((scores - top) * jnp.float32(FACTOR)).astype(jnp.bfloat16)


def normalised(summed, total):
    inverse = pl.reciprocal(total, approx=True)
    return summed * (inverse * (2.0 - total * inverse))


def chains():
    return [
        (range(h, h + HEADS_AT_ONCE), h // GROUP) for h in range(0, QUERY_HEADS, HEADS_AT_ONCE)
    ]


def in_turn(*stages):
    runs = chains()
    results = {}
    for turn in range(len(runs) + len(stages) - 1):
        for n, stage in enumerate(stages):
            i = turn - n
            if 0 <= i < len(runs):
                results[i] = stage(*runs[i], *results.pop(i, ()))


def pack_kernel(key_hbm, value_hbm, *refs):
    *outs, sems = refs
    rows = key_hbm.shape[0]
    copies = []
    for n, out in enumerate(outs):
        copies.append(pltpu.make_async_copy(key_hbm, out.at[:rows], sems.at[n, 0]))
        copies.append(pltpu.make_async_copy(value_hbm, out.at[rows:], sems.at[n, 1]))
    for copy in copies:
        copy.start()
    for copy in copies:
        copy.wait()


def pack(keys, values):
    rows, width = keys.shape
    packed = pltpu.VMEM((2 * rows, width), keys.dtype)
    return pl.pallas_call(
        pack_kernel,
        out_shape=(packed, packed),
        in_specs=[HBM, HBM],
        out_specs=(VMEM, VMEM),
        scratch_shapes=[pltpu.SemaphoreType.DMA((2, 2))],
        compiler_params=pltpu.CompilerParams(vmem_limit_bytes=1024 * 1024),
    )(*in_hbm(keys, values))


def own_kernel(
    rounds, rows, own_ref, lengths_hbm, q_hbm,
    _, bias_ref, needed_ref, odd_ref, q_ref, top_ref, total_ref, sum_ref,
    own_bias_ref, lengths_ref, lengths_sem, q_sems,
):
    lengths_copy = pltpu.make_async_copy(lengths_hbm, lengths_ref, lengths_sem)
    lengths_copy.start()
    width = GROUP * HEAD_SIZE
    q_copies = []
    for g in range(KEY_VALUE_HEADS):
        at = slice(g * width, (g + 1) * width)
        q_copies.append(pltpu.make_async_copy(q_hbm.at[:, at], q_ref.at[:, at], q_sems.at[g]))
        q_copies[g].start()
    me = lax.axis_index("dp") * lax.axis_size("ctx") + lax.axis_index("ctx")
    odd_ref[...] = jnp.full(odd_ref.shape, lax.rem(me, 2), jnp.int32)
    first = me * rows
    query_pos = first + lax.broadcasted_iota(jnp.int32, (rows, rows), 0)
    lengths_copy.wait()

    def later(doc, carried):
        bound, start, first_start = carried
        start = jnp.where(query_pos >= bound, bound, start)
        first_start = jnp.where(first >= bound, bound, first_start)
        return bound + lengths_ref[doc], start, first_start

    zero = jnp.int32(0)
    _, start, first_start = lax.fori_loop(
        0,
        lengths_ref.shape[0],
        later,
        (zero, jnp.zeros((rows, rows), jnp.int32), zero),
        unroll=8,
    )
    needed_ref[0] = lax.div(first - first_start + (rows - 1), jnp.int32(rows))
    lane = lax.broadcasted_iota(jnp.int32, (rows, rows), 1)

    def bias_of(allowed):
        return jnp.where(allowed, jnp.float32(0.0), jnp.float32(EXCLUDED))

    key_pos = first + lane
    own_bias_ref[...] = bias_of((key_pos >= start) & (key_pos <= query_pos))
    for b in range(2 * rounds):
        key_pos = first - (b + 1) * rows + lane
        bias_ref[:, b * rows : (b + 1) * rows] = bias_of(key_pos >= start)

    def match(heads, g):
        if heads[0] % GROUP == 0:
            q_copies[g].wait()
        return (scores_of(stacked(q_ref, heads), own_ref[:rows, head_columns(g)], own_bias_ref[...]),)

    def weigh(heads, g, scores):
        top = jnp.max(scores, axis=1, keepdims=True)
        spread(top_ref, heads, rows, jnp.broadcast_to(top, scores.shape))
        return (weights_of(scores, top),)

    def gather(heads, g, weights):
        value = with_ones(own_ref[rows:, head_columns(g)])
        summed = jnp.dot(weights, value, preferred_element_type=jnp.float32)
        spread(sum_ref, heads, rows, summed[:, :HEAD_SIZE])
        spread(total_ref, heads, rows, summed[:, HEAD_SIZE:])

    in_turn(match, weigh, gather)


def in_vmem(*operands):
    return [pltpu.with_memory_space_constraint(x, pltpu.VMEM) for x in operands]


def in_hbm(*operands):
    return [pltpu.with_memory_space_constraint(x, pltpu.HBM) for x in operands]


SMEM = pl.BlockSpec(memory_space=pltpu.SMEM)
VMEM = pl.BlockSpec(memory_space=pltpu.VMEM)
HBM = pl.BlockSpec(memory_space=pltpu.HBM)


def own_part(lengths, queries, own, rounds):
    rows = queries.shape[0]
    partial = pltpu.VMEM(queries.shape, jnp.float32)
    return pl.pallas_call(
        functools.partial(own_kernel, rounds, rows),
        out_shape=(
            pltpu.VMEM(own.shape, own.dtype),
            pltpu.VMEM((rows, 2 * rounds * rows), jnp.float32),
            jax.ShapeDtypeStruct((1,), jnp.int32),
            pltpu.VMEM((1, own.shape[1]), jnp.int32),
            pltpu.VMEM(queries.shape, queries.dtype),
            partial,
            partial,
            partial,
        ),
        in_specs=[VMEM, HBM, HBM],
        out_specs=(VMEM, VMEM, SMEM, VMEM, VMEM, VMEM, VMEM, VMEM),
        input_output_aliases={0: 0},
        scratch_shapes=[
            pltpu.VMEM((rows, rows), jnp.float32),
            pltpu.SMEM(lengths.shape, jnp.int32),
            pltpu.SemaphoreType.DMA,
            pltpu.SemaphoreType.DMA((KEY_VALUE_HEADS,)),
        ],
        compiler_params=pltpu.CompilerParams(vmem_limit_bytes=10 * 1024 * 1024),
        cost_estimate=pl.CostEstimate(
            flops=4 * 10**9, bytes_accessed=16 * 10**6, transcendentals=rows * queries.size
        ),
    )(*in_vmem(own), *in_hbm(lengths, queries))


def behind_kernel(
    before, last, rows, needed_ref, bias_ref, q_ref, *refs
):
    width = GROUP * HEAD_SIZE
    beyond = needed_ref[0] - before
    *near_refs, further_ref, top_ref, total_ref, sum_ref = refs[: 5 if last else 6]
    refs = refs[5 if last else 6 :]
    if last:
        near_refs = (near_refs[0].at[:rows], near_refs[0].at[rows:])
    pairs = (near_refs, (further_ref.at[:rows], further_ref.at[rows:]))
    if last:
        out_hbm, out_ref, out_sems = refs

        def out_copy(g):
            at = slice(g * width, (g + 1) * width)
            return pltpu.make_async_copy(out_ref.at[:, at], out_hbm.at[:, at], out_sems.at[g])

    else:
        _, new_top_ref, new_total_ref, new_sum_ref = refs

    def finish(heads, g, summed, total):
        if last:
            spread(out_ref, heads, rows, normalised(summed, total))
            if heads[-1] % GROUP == GROUP - 1:
                out_copy(g).start()
        else:
            spread(new_sum_ref, heads, rows, summed)
            spread(new_total_ref, heads, rows, total)

    def attend(count):
        def match(heads, g):
            key = jnp.concatenate([key[:, head_columns(g)] for key, _ in pairs[:count]], axis=0)
            bias = bias_ref[:, before * rows : (before + count) * rows]
            return (scores_of(stacked(q_ref, heads), key, bias),)

        def weigh(heads, g, scores):
            old_top = stacked(top_ref, heads)
            top = jnp.maximum(old_top, jnp.max(scores, axis=1, keepdims=True))
            fade = jnp.exp2((old_top - top) * jnp.float32(FACTOR))
            if not last:
                spread(new_top_ref, heads, rows, top)
            return weights_of(scores, jnp.concatenate([top] * count, axis=1)), fade

        def gather(heads, g, weights, fade):
            value = jnp.concatenate([value[:, head_columns(g)] for _, value in pairs[:count]], axis=0)
            more = jnp.dot(weights, with_ones(value), preferred_element_type=jnp.float32)
            summed = stacked(sum_ref, heads) * fade + more[:, :HEAD_SIZE]
            total = stacked(total_ref, heads) * fade + more[:, HEAD_SIZE:]
            finish(heads, g, summed, total)

        in_turn(match, weigh, gather)

    @pl.when(beyond > 1)
    def _():
        attend(2)

    @pl.when(beyond == 1)
    def _():
        attend(1)

    if last:
        @pl.when(beyond < 1)
        def _():
            in_turn(
                lambda heads, g: finish(heads, g, stacked(sum_ref, heads), stacked(total_ref, heads))
            )

        for g in range(KEY_VALUE_HEADS):
            out_copy(g).wait()


def behind_part(before, last, needed, bias, queries, halves, further, parts):
    rows = queries.shape[0]
    area = rows * rows * 2 * QUERY_HEADS
    operands = in_vmem(bias, queries, *halves, further, *parts)
    if last:
        out_shape = jax.ShapeDtypeStruct(queries.shape, queries.dtype)
        out_specs = HBM
        scratch = [
            pltpu.VMEM(queries.shape, queries.dtype),
            pltpu.SemaphoreType.DMA((KEY_VALUE_HEADS,)),
        ]
        aliases = {}
    else:
        kept = (further, *parts)
        out_shape = tuple(pltpu.VMEM(part.shape, part.dtype) for part in kept)
        out_specs = (VMEM,) * len(kept)
        scratch = []
        aliases = {5 + n: n for n in range(len(kept))}
    return pl.pallas_call(
        functools.partial(behind_kernel, before, last, rows),
        out_shape=out_shape,
        in_specs=[SMEM] + [VMEM] * len(operands),
        out_specs=out_specs,
        scratch_shapes=scratch,
        input_output_aliases=aliases,
        compiler_params=pltpu.CompilerParams(vmem_limit_bytes=10 * 1024 * 1024),
        cost_estimate=pl.CostEstimate(
            flops=4 * area, bytes_accessed=queries.size, transcendentals=0
        ),
    )(needed, *operands)


def per_device(queries, keys, values, lengths):
    count = lax.axis_size("dp") * lax.axis_size("ctx")
    rounds = lax.axis_size("ctx")

    def from_behind(block, r):
        by = 2 * (r + 1)
        return lax.ppermute(block, AXES, [(i, i + by) for i in range(count - by)])

    packed, own = pack(keys, values)
    fetched = [from_behind(packed, 0)]
    own, bias, needed, odd, queries, *parts = own_part(lengths, queries, own, rounds)
    fetched += [from_behind(own, r) for r in range(1, rounds)]
    swap = [(i, i ^ 1) for i in range(count)]
    nearer = own
    for r, further in enumerate(fetched):
        last = r == rounds - 1
        cuts = 1 if last else 2
        halves = []
        for old, new in zip(jnp.split(nearer, cuts), jnp.split(further, cuts)):
            halves.append(lax.ppermute(jnp.where(odd == 1, new, old), AXES, swap))
        result = behind_part(2 * r, last, needed, bias, queries, halves, further, parts)
        if not last:
            nearer, *parts = result
    return result


def solution(mesh):
    in_specs = (P(AXES, None), P(AXES, None), P(AXES, None), P())
    return jax.shard_map(
        per_device, mesh=mesh, in_specs=in_specs, out_specs=P(AXES, None), check_vma=False
    )
```

```python
import functools
import math

import jax
import jax.numpy as jnp
from jax import lax
from jax.experimental import pallas as pl
from jax.experimental.pallas import tpu as pltpu
from jax.sharding import PartitionSpec as P

HEAD_SIZE = 128
QUERY_HEADS = 32
KEY_VALUE_HEADS = 4
GROUP = QUERY_HEADS // KEY_VALUE_HEADS
HEADS_AT_ONCE = 4
EXCLUDED = -1e30
PAD = 16
AXES = ("dp", "ctx")


FACTOR = math.log2(math.e) / math.sqrt(HEAD_SIZE)


def head_columns(i):
    return slice(i * HEAD_SIZE, (i + 1) * HEAD_SIZE)


def stacked(ref, heads):
    return jnp.concatenate([ref[:, head_columns(i)] for i in heads], axis=0)


def spread(ref, heads, rows, value):
    for n, i in enumerate(heads):
        ref[:, head_columns(i)] = value[n * rows : (n + 1) * rows].astype(ref.dtype)


def with_ones(value):
    return jnp.concatenate([value, jnp.ones(value.shape, value.dtype)], axis=1)


def scores_of(q, key, bias):
    scores = lax.dot_general(
        q, key, (((1,), (1,)), ((), ())), preferred_element_type=jnp.float32
    )
    return scores + jnp.concatenate([bias] * (q.shape[0] // bias.shape[0]), axis=0)


def weights_of(scores, top):
    return jnp.exp2((scores - top) * jnp.float32(FACTOR)).astype(jnp.bfloat16)


def normalised(summed, total):
    inverse = pl.reciprocal(total, approx=True)
    return summed * (inverse * (2.0 - total * inverse))


def chains():
    return [
        (range(h, h + HEADS_AT_ONCE), h // GROUP) for h in range(0, QUERY_HEADS, HEADS_AT_ONCE)
    ]


def in_turn(*stages):
    runs = chains()
    results = {}
    for turn in range(len(runs) + len(stages) - 1):
        for n, stage in enumerate(stages):
            i = turn - n
            if 0 <= i < len(runs):
                results[i] = stage(*runs[i], *results.pop(i, ()))


def pack_kernel(key_hbm, value_hbm, *refs):
    *outs, sems = refs
    rows = key_hbm.shape[0]
    copies = []
    for n, out in enumerate(outs):
        copies.append(pltpu.make_async_copy(key_hbm, out.at[:rows], sems.at[n, 0]))
        copies.append(pltpu.make_async_copy(value_hbm, out.at[rows : 2 * rows], sems.at[n, 1]))
    for copy in copies:
        copy.start()
    for copy in copies:
        copy.wait()


def pack(keys, values):
    rows, width = keys.shape
    packed = pltpu.VMEM((2 * rows, width), keys.dtype)
    longer = pltpu.VMEM((2 * rows + PAD, width), keys.dtype)
    return pl.pallas_call(
        pack_kernel,
        out_shape=(packed, longer),
        in_specs=[HBM, HBM],
        out_specs=(VMEM, VMEM),
        scratch_shapes=[pltpu.SemaphoreType.DMA((2, 2))],
        compiler_params=pltpu.CompilerParams(vmem_limit_bytes=1024 * 1024),
    )(*in_hbm(keys, values))


def own_kernel(
    rounds, rows, own_ref, lengths_hbm, q_hbm,
    longer_ref, bias_ref, needed_ref, odd_ref, q_ref, top_ref, total_ref, sum_ref,
    own_bias_ref, lengths_ref, lengths_sem, q_sems,
):
    lengths_copy = pltpu.make_async_copy(lengths_hbm, lengths_ref, lengths_sem)
    lengths_copy.start()
    width = GROUP * HEAD_SIZE
    q_copies = []
    for g in range(KEY_VALUE_HEADS):
        at = slice(g * width, (g + 1) * width)
        q_copies.append(pltpu.make_async_copy(q_hbm.at[:, at], q_ref.at[:, at], q_sems.at[g]))
        q_copies[g].start()
    me = lax.axis_index("dp") * lax.axis_size("ctx") + lax.axis_index("ctx")
    longer_ref[2 * rows :, :] = jnp.zeros((PAD, longer_ref.shape[1]), longer_ref.dtype)
    odd_ref[...] = jnp.full(odd_ref.shape, lax.rem(me, 2), jnp.int32)
    first = me * rows
    query_pos = first + lax.broadcasted_iota(jnp.int32, (rows, rows), 0)
    lengths_copy.wait()

    def later(doc, carried):
        bound, start, first_start = carried
        start = jnp.where(query_pos >= bound, bound, start)
        first_start = jnp.where(first >= bound, bound, first_start)
        return bound + lengths_ref[doc], start, first_start

    zero = jnp.int32(0)
    _, start, first_start = lax.fori_loop(
        0,
        lengths_ref.shape[0],
        later,
        (zero, jnp.zeros((rows, rows), jnp.int32), zero),
        unroll=8,
    )
    needed = lax.div(first - first_start + (rows - 1), jnp.int32(rows))
    needed_ref[...] = jnp.full(needed_ref.shape, needed, jnp.int32)
    lane = lax.broadcasted_iota(jnp.int32, (rows, rows), 1)

    def bias_of(allowed):
        return jnp.where(allowed, jnp.float32(0.0), jnp.float32(EXCLUDED))

    key_pos = first + lane
    own_bias_ref[...] = bias_of((key_pos >= start) & (key_pos <= query_pos))
    for b in range(2 * rounds):
        key_pos = first - (b + 1) * rows + lane
        bias_ref[:, b * rows : (b + 1) * rows] = bias_of(key_pos >= start)

    def match(heads, g):
        if heads[0] % GROUP == 0:
            q_copies[g].wait()
        return (scores_of(stacked(q_ref, heads), own_ref[:rows, head_columns(g)], own_bias_ref[...]),)

    def weigh(heads, g, scores):
        top = jnp.max(scores, axis=1, keepdims=True)
        spread(top_ref, heads, rows, jnp.broadcast_to(top, scores.shape))
        return (weights_of(scores, top),)

    def gather(heads, g, weights):
        value = with_ones(own_ref[rows : 2 * rows, head_columns(g)])
        summed = jnp.dot(weights, value, preferred_element_type=jnp.float32)
        spread(sum_ref, heads, rows, summed[:, :HEAD_SIZE])
        spread(total_ref, heads, rows, summed[:, HEAD_SIZE:])

    in_turn(match, weigh, gather)


def in_vmem(*operands):
    return [pltpu.with_memory_space_constraint(x, pltpu.VMEM) for x in operands]


def in_hbm(*operands):
    return [pltpu.with_memory_space_constraint(x, pltpu.HBM) for x in operands]


SMEM = pl.BlockSpec(memory_space=pltpu.SMEM)
VMEM = pl.BlockSpec(memory_space=pltpu.VMEM)
HBM = pl.BlockSpec(memory_space=pltpu.HBM)


def own_part(lengths, queries, own, rounds):
    rows = queries.shape[0]
    partial = pltpu.VMEM(queries.shape, jnp.float32)
    return pl.pallas_call(
        functools.partial(own_kernel, rounds, rows),
        out_shape=(
            pltpu.VMEM(own.shape, own.dtype),
            pltpu.VMEM((rows, 2 * rounds * rows), jnp.float32),
            pltpu.VMEM((8, 128), jnp.int32),
            pltpu.VMEM((1, own.shape[1]), jnp.int32),
            pltpu.VMEM(queries.shape, queries.dtype),
            partial,
            partial,
            partial,
        ),
        in_specs=[VMEM, HBM, HBM],
        out_specs=(VMEM,) * 8,
        input_output_aliases={0: 0},
        scratch_shapes=[
            pltpu.VMEM((rows, rows), jnp.float32),
            pltpu.SMEM(lengths.shape, jnp.int32),
            pltpu.SemaphoreType.DMA,
            pltpu.SemaphoreType.DMA((KEY_VALUE_HEADS,)),
        ],
        compiler_params=pltpu.CompilerParams(vmem_limit_bytes=10 * 1024 * 1024),
        cost_estimate=pl.CostEstimate(
            flops=4 * 10**9, bytes_accessed=16 * 10**6, transcendentals=rows * queries.size
        ),
    )(*in_vmem(own), *in_hbm(lengths, queries))


def behind_kernel(
    before, last, rows, needed_ref, bias_ref, q_ref, near_ref, further_ref, top_ref, total_ref, sum_ref, *refs
):
    width = GROUP * HEAD_SIZE
    beyond = needed_ref[0, 0] - before
    pairs = [(ref.at[:rows], ref.at[rows : 2 * rows]) for ref in (near_ref, further_ref)]
    if last:
        out_hbm, out_ref, out_sems = refs

        def out_copy(g):
            at = slice(g * width, (g + 1) * width)
            return pltpu.make_async_copy(out_ref.at[:, at], out_hbm.at[:, at], out_sems.at[g])

    else:
        _, new_top_ref, new_total_ref, new_sum_ref = refs

    def finish(heads, g, summed, total):
        if last:
            spread(out_ref, heads, rows, normalised(summed, total))
            if heads[-1] % GROUP == GROUP - 1:
                out_copy(g).start()
        else:
            spread(new_sum_ref, heads, rows, summed)
            spread(new_total_ref, heads, rows, total)

    def attend(count):
        def match(heads, g):
            key = jnp.concatenate([key[:, head_columns(g)] for key, _ in pairs[:count]], axis=0)
            bias = bias_ref[:, before * rows : (before + count) * rows]
            return (scores_of(stacked(q_ref, heads), key, bias),)

        def weigh(heads, g, scores):
            old_top = stacked(top_ref, heads)
            top = jnp.maximum(old_top, jnp.max(scores, axis=1, keepdims=True))
            fade = jnp.exp2((old_top - top) * jnp.float32(FACTOR))
            if not last:
                spread(new_top_ref, heads, rows, top)
            return weights_of(scores, jnp.concatenate([top] * count, axis=1)), fade

        def gather(heads, g, weights, fade):
            value = jnp.concatenate([value[:, head_columns(g)] for _, value in pairs[:count]], axis=0)
            more = jnp.dot(weights, with_ones(value), preferred_element_type=jnp.float32)
            summed = stacked(sum_ref, heads) * fade + more[:, :HEAD_SIZE]
            total = stacked(total_ref, heads) * fade + more[:, HEAD_SIZE:]
            finish(heads, g, summed, total)

        in_turn(match, weigh, gather)

    @pl.when(beyond > 1)
    def _():
        attend(2)

    @pl.when(beyond == 1)
    def _():
        attend(1)

    if last:
        @pl.when(beyond < 1)
        def _():
            in_turn(
                lambda heads, g: finish(heads, g, stacked(sum_ref, heads), stacked(total_ref, heads))
            )

        for g in range(KEY_VALUE_HEADS):
            out_copy(g).wait()


def behind_part(before, last, needed, bias, queries, near, further, parts):
    rows = queries.shape[0]
    area = rows * rows * 2 * QUERY_HEADS
    operands = in_vmem(needed, bias, queries, near, further, *parts)
    if last:
        out_shape = jax.ShapeDtypeStruct(queries.shape, queries.dtype)
        out_specs = HBM
        scratch = [
            pltpu.VMEM(queries.shape, queries.dtype),
            pltpu.SemaphoreType.DMA((KEY_VALUE_HEADS,)),
        ]
        aliases = {}
    else:
        kept = (further, *parts)
        out_shape = tuple(pltpu.VMEM(part.shape, part.dtype) for part in kept)
        out_specs = (VMEM,) * len(kept)
        scratch = []
        aliases = {4 + n: n for n in range(len(kept))}
    return pl.pallas_call(
        functools.partial(behind_kernel, before, last, rows),
        out_shape=out_shape,
        in_specs=[VMEM] * len(operands),
        out_specs=out_specs,
        scratch_shapes=scratch,
        input_output_aliases=aliases,
        compiler_params=pltpu.CompilerParams(vmem_limit_bytes=10 * 1024 * 1024),
        cost_estimate=pl.CostEstimate(
            flops=4 * area, bytes_accessed=queries.size, transcendentals=0
        ),
    )(*operands)


def per_device(queries, keys, values, lengths):
    count = lax.axis_size("dp") * lax.axis_size("ctx")
    rounds = lax.axis_size("ctx")

    def from_behind(block, r):
        by = 2 * (r + 1)
        return lax.ppermute(block, AXES, [(i, i + by) for i in range(count - by)])

    packed, own = pack(keys, values)
    fetched = [from_behind(packed, 0)]
    own, bias, needed, odd, queries, *parts = own_part(lengths, queries, own, rounds)
    fetched += [from_behind(own, r) for r in range(1, rounds)]
    swap = [(i, i ^ 1) for i in range(count)]
    nearer = own
    size = 2 * keys.shape[0]
    for r, further in enumerate(fetched):
        last = r == rounds - 1
        near = lax.ppermute(jnp.where(odd == 1, further[:size], nearer[:size]), AXES, swap)
        result = behind_part(2 * r, last, needed, bias, queries, near, further, parts)
        if not last:
            nearer, *parts = result
    return result


def solution(mesh):
    in_specs = (P(AXES, None), P(AXES, None), P(AXES, None), P())
    return jax.shard_map(
        per_device, mesh=mesh, in_specs=in_specs, out_specs=P(AXES, None), check_vma=False
    )
```

```python
import functools
import math

import jax
import jax.numpy as jnp
from jax import lax
from jax.experimental import pallas as pl
from jax.experimental.pallas import tpu as pltpu
from jax.sharding import PartitionSpec as P

HEAD_SIZE = 128
QUERY_HEADS = 32
KEY_VALUE_HEADS = 4
GROUP = QUERY_HEADS // KEY_VALUE_HEADS
HEADS_AT_ONCE = 4
EARLY_CHAINS = 4
EXCLUDED = -1e30
PAD = 16
AXES = ("dp", "ctx")


FACTOR = math.log2(math.e) / math.sqrt(HEAD_SIZE)


def head_columns(i):
    return slice(i * HEAD_SIZE, (i + 1) * HEAD_SIZE)


def stacked(ref, heads):
    return jnp.concatenate([ref[:, head_columns(i)] for i in heads], axis=0)


def spread(ref, heads, rows, value):
    for n, i in enumerate(heads):
        ref[:, head_columns(i)] = value[n * rows : (n + 1) * rows].astype(ref.dtype)


def with_ones(value):
    return jnp.concatenate([value, jnp.ones(value.shape, value.dtype)], axis=1)


def scores_of(q, key, bias):
    scores = lax.dot_general(
        q, key, (((1,), (1,)), ((), ())), preferred_element_type=jnp.float32
    )
    return scores + jnp.concatenate([bias] * (q.shape[0] // bias.shape[0]), axis=0)


def weights_of(scores, top):
    return jnp.exp2((scores - top) * jnp.float32(FACTOR)).astype(jnp.bfloat16)


def normalised(summed, total):
    inverse = pl.reciprocal(total, approx=True)
    return summed * (inverse * (2.0 - total * inverse))


def chains():
    return [
        (range(h, h + HEADS_AT_ONCE), h // GROUP) for h in range(0, QUERY_HEADS, HEADS_AT_ONCE)
    ]


def in_turn(runs, *stages):
    results = {}
    for turn in range(len(runs) + len(stages) - 1):
        for n, stage in enumerate(stages):
            i = turn - n
            if 0 <= i < len(runs):
                results[i] = stage(*runs[i], *results.pop(i, ()))


def pack_kernel(key_hbm, value_hbm, out_ref, sems):
    rows = key_hbm.shape[0]
    copies = [
        pltpu.make_async_copy(key_hbm, out_ref.at[:rows], sems.at[0]),
        pltpu.make_async_copy(value_hbm, out_ref.at[rows:], sems.at[1]),
    ]
    for copy in copies:
        copy.start()
    for copy in copies:
        copy.wait()


def pack(keys, values):
    rows, width = keys.shape
    return pl.pallas_call(
        pack_kernel,
        out_shape=pltpu.VMEM((2 * rows, width), keys.dtype),
        in_specs=[HBM, HBM],
        out_specs=VMEM,
        scratch_shapes=[pltpu.SemaphoreType.DMA((2,))],
        compiler_params=pltpu.CompilerParams(vmem_limit_bytes=1024 * 1024),
    )(*in_hbm(keys, values))


def attend_own(runs, rows, own_ref, own_bias_ref, q_ref, top_ref, total_ref, sum_ref, ready):
    def match(heads, g):
        ready(heads, g)
        key = own_ref[:rows, head_columns(g)]
        return (scores_of(stacked(q_ref, heads), key, own_bias_ref[...]),)

    def weigh(heads, g, scores):
        top = jnp.max(scores, axis=1, keepdims=True)
        spread(top_ref, heads, rows, jnp.broadcast_to(top, scores.shape))
        return (weights_of(scores, top),)

    def gather(heads, g, weights):
        value = with_ones(own_ref[rows:, head_columns(g)])
        summed = jnp.dot(weights, value, preferred_element_type=jnp.float32)
        spread(sum_ref, heads, rows, summed[:, :HEAD_SIZE])
        spread(total_ref, heads, rows, summed[:, HEAD_SIZE:])

    in_turn(runs, match, weigh, gather)


def own_kernel(
    rounds, rows, own_ref, lengths_hbm, q_hbm,
    longer_ref, bias_ref, needed_ref, own_bias_ref, q_ref, odd_ref, top_ref, total_ref, sum_ref,
    lengths_ref, lengths_sem, q_sems,
):
    lengths_copy = pltpu.make_async_copy(lengths_hbm, lengths_ref, lengths_sem)
    lengths_copy.start()
    width = GROUP * HEAD_SIZE
    q_copies = []
    for g in range(KEY_VALUE_HEADS):
        at = slice(g * width, (g + 1) * width)
        q_copies.append(pltpu.make_async_copy(q_hbm.at[:, at], q_ref.at[:, at], q_sems.at[g]))
        q_copies[g].start()
    me = lax.axis_index("dp") * lax.axis_size("ctx") + lax.axis_index("ctx")
    longer_ref[: 2 * rows, :] = own_ref[...]
    longer_ref[2 * rows :, :] = jnp.zeros((PAD, longer_ref.shape[1]), longer_ref.dtype)
    odd_ref[...] = jnp.full(odd_ref.shape, lax.rem(me, 2), jnp.int32)
    first = me * rows
    query_pos = first + lax.broadcasted_iota(jnp.int32, (rows, rows), 0)
    lengths_copy.wait()

    def later(doc, carried):
        bound, start, first_start = carried
        start = jnp.where(query_pos >= bound, bound, start)
        first_start = jnp.where(first >= bound, bound, first_start)
        return bound + lengths_ref[doc], start, first_start

    zero = jnp.int32(0)
    _, start, first_start = lax.fori_loop(
        0,
        lengths_ref.shape[0],
        later,
        (zero, jnp.zeros((rows, rows), jnp.int32), zero),
        unroll=8,
    )
    needed = lax.div(first - first_start + (rows - 1), jnp.int32(rows))
    needed_ref[...] = jnp.full(needed_ref.shape, needed, jnp.int32)
    lane = lax.broadcasted_iota(jnp.int32, (rows, rows), 1)

    def bias_of(allowed):
        return jnp.where(allowed, jnp.float32(0.0), jnp.float32(EXCLUDED))

    key_pos = first + lane
    own_bias_ref[...] = bias_of((key_pos >= start) & (key_pos <= query_pos))
    for b in range(2 * rounds):
        key_pos = first - (b + 1) * rows + lane
        bias_ref[:, b * rows : (b + 1) * rows] = bias_of(key_pos >= start)

    def ready(heads, g):
        if heads[0] % GROUP == 0:
            q_copies[g].wait()

    runs = chains()[:EARLY_CHAINS]
    attend_own(runs, rows, own_ref, own_bias_ref, q_ref, top_ref, total_ref, sum_ref, ready)
    for copy in q_copies[runs[-1][1] + 1 :]:
        copy.wait()


def own_rest_kernel(
    rows, own_ref, own_bias_ref, q_ref, odd_ref, *parts
):
    runs = chains()[EARLY_CHAINS:]
    parts = parts[4:]
    attend_own(runs, rows, own_ref, own_bias_ref, q_ref, *parts, lambda heads, g: None)


def in_vmem(*operands):
    return [pltpu.with_memory_space_constraint(x, pltpu.VMEM) for x in operands]


def in_hbm(*operands):
    return [pltpu.with_memory_space_constraint(x, pltpu.HBM) for x in operands]


SMEM = pl.BlockSpec(memory_space=pltpu.SMEM)
VMEM = pl.BlockSpec(memory_space=pltpu.VMEM)
HBM = pl.BlockSpec(memory_space=pltpu.HBM)


def own_part(lengths, queries, own, rounds):
    rows = queries.shape[0]
    part = pltpu.VMEM(queries.shape, jnp.float32)
    return pl.pallas_call(
        functools.partial(own_kernel, rounds, rows),
        out_shape=(
            pltpu.VMEM((2 * rows + PAD, own.shape[1]), own.dtype),
            pltpu.VMEM((rows, 2 * rounds * rows), jnp.float32),
            pltpu.VMEM((8, 128), jnp.int32),
            pltpu.VMEM((rows, rows), jnp.float32),
            pltpu.VMEM(queries.shape, queries.dtype),
            pltpu.VMEM((1, own.shape[1]), jnp.int32),
            part,
            part,
            part,
        ),
        in_specs=[VMEM, HBM, HBM],
        out_specs=(VMEM,) * 9,
        scratch_shapes=[
            pltpu.SMEM(lengths.shape, jnp.int32),
            pltpu.SemaphoreType.DMA,
            pltpu.SemaphoreType.DMA((KEY_VALUE_HEADS,)),
        ],
        compiler_params=pltpu.CompilerParams(vmem_limit_bytes=10 * 1024 * 1024),
        cost_estimate=pl.CostEstimate(
            flops=4 * 10**9, bytes_accessed=16 * 10**6, transcendentals=rows * queries.size
        ),
    )(*in_vmem(own), *in_hbm(lengths, queries))


def own_rest(own, own_bias, queries, kept):
    rows = queries.shape[0]
    operands = in_vmem(own, own_bias, queries, *kept)
    return pl.pallas_call(
        functools.partial(own_rest_kernel, rows),
        out_shape=tuple(pltpu.VMEM(x.shape, x.dtype) for x in kept),
        in_specs=[VMEM] * len(operands),
        out_specs=(VMEM,) * len(kept),
        input_output_aliases={3 + n: n for n in range(len(kept))},
        compiler_params=pltpu.CompilerParams(vmem_limit_bytes=10 * 1024 * 1024),
        cost_estimate=pl.CostEstimate(
            flops=4 * 10**9, bytes_accessed=16 * 10**6, transcendentals=rows * queries.size
        ),
    )(*operands)


def behind_kernel(
    before, last, rows, needed_ref, bias_ref, q_ref, near_ref, further_ref, top_ref, total_ref, sum_ref, *refs
):
    beyond = needed_ref[0, 0] - before
    pairs = [(ref.at[:rows], ref.at[rows : 2 * rows]) for ref in (near_ref, further_ref)]
    if last:
        out_hbm, out_ref, out_sems = refs

        def out_copy(n):
            width = HEADS_AT_ONCE * HEAD_SIZE
            at = slice(n * width, (n + 1) * width)
            return pltpu.make_async_copy(out_ref.at[:, at], out_hbm.at[:, at], out_sems.at[n])

    else:
        _, new_top_ref, new_total_ref, new_sum_ref = refs

    def finish(heads, g, summed, total):
        if last:
            spread(out_ref, heads, rows, normalised(summed, total))
            out_copy(heads[0] // HEADS_AT_ONCE).start()
        else:
            spread(new_sum_ref, heads, rows, summed)
            spread(new_total_ref, heads, rows, total)

    def attend(count):
        def match(heads, g):
            key = jnp.concatenate([key[:, head_columns(g)] for key, _ in pairs[:count]], axis=0)
            bias = bias_ref[:, before * rows : (before + count) * rows]
            return (scores_of(stacked(q_ref, heads), key, bias),)

        def weigh(heads, g, scores):
            old_top = stacked(top_ref, heads)
            top = jnp.maximum(old_top, jnp.max(scores, axis=1, keepdims=True))
            fade = jnp.exp2((old_top - top) * jnp.float32(FACTOR))
            if not last:
                spread(new_top_ref, heads, rows, top)
            return weights_of(scores, jnp.concatenate([top] * count, axis=1)), fade

        def gather(heads, g, weights, fade):
            value = jnp.concatenate([value[:, head_columns(g)] for _, value in pairs[:count]], axis=0)
            more = jnp.dot(weights, with_ones(value), preferred_element_type=jnp.float32)
            summed = stacked(sum_ref, heads) * fade + more[:, :HEAD_SIZE]
            total = stacked(total_ref, heads) * fade + more[:, HEAD_SIZE:]
            finish(heads, g, summed, total)

        in_turn(chains(), match, weigh, gather)

    @pl.when(beyond > 1)
    def _():
        attend(2)

    @pl.when(beyond == 1)
    def _():
        attend(1)

    if last:
        @pl.when(beyond < 1)
        def _():
            in_turn(
                chains(),
                lambda heads, g: finish(heads, g, stacked(sum_ref, heads), stacked(total_ref, heads)),
            )

        for n in range(len(chains())):
            out_copy(n).wait()


def behind_part(before, last, needed, bias, queries, near, further, parts):
    rows = queries.shape[0]
    area = rows * rows * 2 * QUERY_HEADS
    operands = in_vmem(needed, bias, queries, near, further, *parts)
    if last:
        out_shape = jax.ShapeDtypeStruct(queries.shape, queries.dtype)
        out_specs = HBM
        scratch = [
            pltpu.VMEM(queries.shape, queries.dtype),
            pltpu.SemaphoreType.DMA((len(chains()),)),
        ]
        aliases = {}
    else:
        kept = (further, *parts)
        out_shape = tuple(pltpu.VMEM(part.shape, part.dtype) for part in kept)
        out_specs = (VMEM,) * len(kept)
        scratch = []
        aliases = {4 + n: n for n in range(len(kept))}
    return pl.pallas_call(
        functools.partial(behind_kernel, before, last, rows),
        out_shape=out_shape,
        in_specs=[VMEM] * len(operands),
        out_specs=out_specs,
        scratch_shapes=scratch,
        input_output_aliases=aliases,
        compiler_params=pltpu.CompilerParams(vmem_limit_bytes=10 * 1024 * 1024),
        cost_estimate=pl.CostEstimate(
            flops=4 * area, bytes_accessed=queries.size, transcendentals=0
        ),
    )(*operands)


def per_device(queries, keys, values, lengths):
    count = lax.axis_size("dp") * lax.axis_size("ctx")
    rounds = lax.axis_size("ctx")

    def from_behind(block, r):
        by = 2 * (r + 1)
        return lax.ppermute(block, AXES, [(i, i + by) for i in range(count - by)])

    own = pack(keys, values)
    fetched = [from_behind(own, 0)]
    longer, bias, needed, own_bias, queries, *kept = own_part(lengths, queries, own, rounds)
    fetched += [from_behind(longer, r) for r in range(1, rounds)]
    odd, *parts = own_rest(own, own_bias, queries, kept)
    swap = [(i, i ^ 1) for i in range(count)]
    nearer = own
    size = 2 * keys.shape[0]
    for r, further in enumerate(fetched):
        last = r == rounds - 1
        near = lax.ppermute(jnp.where(odd == 1, further[:size], nearer[:size]), AXES, swap)
        result = behind_part(2 * r, last, needed, bias, queries, near, further, parts)
        if not last:
            nearer, *parts = result
    return result


def solution(mesh):
    in_specs = (P(AXES, None), P(AXES, None), P(AXES, None), P())
    return jax.shard_map(
        per_device, mesh=mesh, in_specs=in_specs, out_specs=P(AXES, None), check_vma=False
    )
```

```python
import functools
import math

import jax
import jax.numpy as jnp
from jax import lax
from jax.experimental import pallas as pl
from jax.experimental.pallas import tpu as pltpu
from jax.sharding import PartitionSpec as P

HEAD_SIZE = 128
QUERY_HEADS = 32
KEY_VALUE_HEADS = 4
GROUP = QUERY_HEADS // KEY_VALUE_HEADS
HEADS_AT_ONCE = 4
EARLY_CHAINS = 4
EXCLUDED = -1e30
PAD = 16
AXES = ("dp", "ctx")


FACTOR = math.log2(math.e) / math.sqrt(HEAD_SIZE)


def head_columns(i):
    return slice(i * HEAD_SIZE, (i + 1) * HEAD_SIZE)


def stacked(ref, heads):
    return jnp.concatenate([ref[:, head_columns(i)] for i in heads], axis=0)


def spread(ref, heads, rows, value):
    for n, i in enumerate(heads):
        ref[:, head_columns(i)] = value[n * rows : (n + 1) * rows].astype(ref.dtype)


def with_ones(value):
    return jnp.concatenate([value, jnp.ones(value.shape, value.dtype)], axis=1)


def scores_of(q, key, bias):
    scores = lax.dot_general(
        q, key, (((1,), (1,)), ((), ())), preferred_element_type=jnp.float32
    )
    return scores + jnp.concatenate([bias] * (q.shape[0] // bias.shape[0]), axis=0)


def weights_of(scores, top):
    return jnp.exp2((scores - top) * jnp.float32(FACTOR)).astype(jnp.bfloat16)


def normalised(summed, total):
    inverse = pl.reciprocal(total, approx=True)
    return summed * (inverse * (2.0 - total * inverse))


def chains():
    return [
        (range(h, h + HEADS_AT_ONCE), h // GROUP) for h in range(0, QUERY_HEADS, HEADS_AT_ONCE)
    ]


def in_turn(runs, *stages):
    results = {}
    for turn in range(len(runs) + len(stages) - 1):
        for n, stage in enumerate(stages):
            i = turn - n
            if 0 <= i < len(runs):
                results[i] = stage(*runs[i], *results.pop(i, ()))


def pack_kernel(key_hbm, value_hbm, out_ref, sems):
    rows = key_hbm.shape[0]
    copies = [
        pltpu.make_async_copy(key_hbm, out_ref.at[:rows], sems.at[0]),
        pltpu.make_async_copy(value_hbm, out_ref.at[rows:], sems.at[1]),
    ]
    for copy in copies:
        copy.start()
    for copy in copies:
        copy.wait()


def pack(keys, values):
    rows, width = keys.shape
    return pl.pallas_call(
        pack_kernel,
        out_shape=pltpu.VMEM((2 * rows, width), keys.dtype),
        in_specs=[HBM, HBM],
        out_specs=VMEM,
        scratch_shapes=[pltpu.SemaphoreType.DMA((2,))],
        compiler_params=pltpu.CompilerParams(vmem_limit_bytes=1024 * 1024),
    )(*in_hbm(keys, values))


def attend_own(runs, rows, own_ref, own_bias_ref, q_ref, top_ref, total_ref, sum_ref, ready):
    def match(heads, g):
        ready(heads, g)
        key = own_ref[:rows, head_columns(g)]
        return (scores_of(stacked(q_ref, heads), key, own_bias_ref[...]),)

    def weigh(heads, g, scores):
        top = jnp.max(scores, axis=1, keepdims=True)
        spread(top_ref, heads, rows, jnp.broadcast_to(top, scores.shape))
        return (weights_of(scores, top),)

    def gather(heads, g, weights):
        value = with_ones(own_ref[rows:, head_columns(g)])
        summed = jnp.dot(weights, value, preferred_element_type=jnp.float32)
        spread(sum_ref, heads, rows, summed[:, :HEAD_SIZE])
        spread(total_ref, heads, rows, summed[:, HEAD_SIZE:])

    in_turn(runs, match, weigh, gather)


def own_kernel(
    rounds, rows, own_ref, lengths_hbm, q_hbm,
    longer_ref, bias_ref, needed_ref, own_bias_ref, q_ref, odd_ref, top_ref, total_ref, sum_ref,
    lengths_ref, lengths_sem, q_sems,
):
    lengths_copy = pltpu.make_async_copy(lengths_hbm, lengths_ref, lengths_sem)
    lengths_copy.start()
    width = GROUP * HEAD_SIZE
    q_copies = []
    for g in range(KEY_VALUE_HEADS):
        at = slice(g * width, (g + 1) * width)
        q_copies.append(pltpu.make_async_copy(q_hbm.at[:, at], q_ref.at[:, at], q_sems.at[g]))
        q_copies[g].start()
    me = lax.axis_index("dp") * lax.axis_size("ctx") + lax.axis_index("ctx")
    longer_ref[: 2 * rows, :] = own_ref[...]
    longer_ref[2 * rows :, :] = jnp.zeros((PAD, longer_ref.shape[1]), longer_ref.dtype)
    odd_ref[...] = jnp.full(odd_ref.shape, lax.rem(me, 2).astype(jnp.float32)).astype(odd_ref.dtype)
    first = me * rows
    query_pos = first + lax.broadcasted_iota(jnp.int32, (rows, rows), 0)
    lengths_copy.wait()

    def later(doc, carried):
        bound, start, first_start = carried
        start = jnp.where(query_pos >= bound, bound, start)
        first_start = jnp.where(first >= bound, bound, first_start)
        return bound + lengths_ref[doc], start, first_start

    zero = jnp.int32(0)
    _, start, first_start = lax.fori_loop(
        0,
        lengths_ref.shape[0],
        later,
        (zero, jnp.zeros((rows, rows), jnp.int32), zero),
        unroll=8,
    )
    needed = lax.div(first - first_start + (rows - 1), jnp.int32(rows))
    needed_ref[...] = jnp.full(needed_ref.shape, needed, jnp.int32)
    lane = lax.broadcasted_iota(jnp.int32, (rows, rows), 1)

    def bias_of(allowed):
        return jnp.where(allowed, jnp.float32(0.0), jnp.float32(EXCLUDED))

    key_pos = first + lane
    own_bias_ref[...] = bias_of((key_pos >= start) & (key_pos <= query_pos))
    for b in range(2 * rounds):
        key_pos = first - (b + 1) * rows + lane
        bias_ref[:, b * rows : (b + 1) * rows] = bias_of(key_pos >= start)

    def ready(heads, g):
        if heads[0] % GROUP == 0:
            q_copies[g].wait()

    runs = chains()[:EARLY_CHAINS]
    attend_own(runs, rows, own_ref, own_bias_ref, q_ref, top_ref, total_ref, sum_ref, ready)
    for copy in q_copies[runs[-1][1] + 1 :]:
        copy.wait()


def own_rest_kernel(
    rows, own_ref, own_bias_ref, q_ref, odd_ref, *parts
):
    runs = chains()[EARLY_CHAINS:]
    parts = parts[4:]
    attend_own(runs, rows, own_ref, own_bias_ref, q_ref, *parts, lambda heads, g: None)


def in_vmem(*operands):
    return [pltpu.with_memory_space_constraint(x, pltpu.VMEM) for x in operands]


def in_hbm(*operands):
    return [pltpu.with_memory_space_constraint(x, pltpu.HBM) for x in operands]


SMEM = pl.BlockSpec(memory_space=pltpu.SMEM)
VMEM = pl.BlockSpec(memory_space=pltpu.VMEM)
HBM = pl.BlockSpec(memory_space=pltpu.HBM)


def own_part(lengths, queries, own, rounds):
    rows = queries.shape[0]
    part = pltpu.VMEM(queries.shape, jnp.float32)
    return pl.pallas_call(
        functools.partial(own_kernel, rounds, rows),
        out_shape=(
            pltpu.VMEM((2 * rows + PAD, own.shape[1]), own.dtype),
            pltpu.VMEM((rows, 2 * rounds * rows), jnp.float32),
            pltpu.VMEM((8, 128), jnp.int32),
            pltpu.VMEM((rows, rows), jnp.float32),
            pltpu.VMEM(queries.shape, queries.dtype),
            pltpu.VMEM(own.shape, own.dtype),
            part,
            part,
            part,
        ),
        in_specs=[VMEM, HBM, HBM],
        out_specs=(VMEM,) * 9,
        scratch_shapes=[
            pltpu.SMEM(lengths.shape, jnp.int32),
            pltpu.SemaphoreType.DMA,
            pltpu.SemaphoreType.DMA((KEY_VALUE_HEADS,)),
        ],
        compiler_params=pltpu.CompilerParams(vmem_limit_bytes=10 * 1024 * 1024),
        cost_estimate=pl.CostEstimate(
            flops=4 * 10**9, bytes_accessed=16 * 10**6, transcendentals=rows * queries.size
        ),
    )(*in_vmem(own), *in_hbm(lengths, queries))


def own_rest(own, own_bias, queries, kept):
    rows = queries.shape[0]
    operands = in_vmem(own, own_bias, queries, *kept)
    return pl.pallas_call(
        functools.partial(own_rest_kernel, rows),
        out_shape=tuple(pltpu.VMEM(x.shape, x.dtype) for x in kept),
        in_specs=[VMEM] * len(operands),
        out_specs=(VMEM,) * len(kept),
        input_output_aliases={3 + n: n for n in range(len(kept))},
        compiler_params=pltpu.CompilerParams(vmem_limit_bytes=10 * 1024 * 1024),
        cost_estimate=pl.CostEstimate(
            flops=4 * 10**9, bytes_accessed=16 * 10**6, transcendentals=rows * queries.size
        ),
    )(*operands)


def behind_kernel(
    behind, last, rows, needed_ref, bias_ref, q_ref, block_ref, _, top_ref, total_ref, sum_ref, *refs
):
    wanted = needed_ref[0, 0] >= behind
    if last:
        out_hbm, out_ref, out_sems = refs

        def out_copy(n):
            width = HEADS_AT_ONCE * HEAD_SIZE
            at = slice(n * width, (n + 1) * width)
            return pltpu.make_async_copy(out_ref.at[:, at], out_hbm.at[:, at], out_sems.at[n])

    else:
        _, new_top_ref, new_total_ref, new_sum_ref = refs

    def finish(heads, g, summed, total):
        if last:
            spread(out_ref, heads, rows, normalised(summed, total))
            out_copy(heads[0] // HEADS_AT_ONCE).start()
        else:
            spread(new_sum_ref, heads, rows, summed)
            spread(new_total_ref, heads, rows, total)

    def match(heads, g):
        key = block_ref[:rows, head_columns(g)]
        bias = bias_ref[:, (behind - 1) * rows : behind * rows]
        return (scores_of(stacked(q_ref, heads), key, bias),)

    def weigh(heads, g, scores):
        old_top = stacked(top_ref, heads)
        top = jnp.maximum(old_top, jnp.max(scores, axis=1, keepdims=True))
        fade = jnp.exp2((old_top - top) * jnp.float32(FACTOR))
        if not last:
            spread(new_top_ref, heads, rows, top)
        return weights_of(scores, top), fade

    def gather(heads, g, weights, fade):
        value = with_ones(block_ref[rows : 2 * rows, head_columns(g)])
        more = jnp.dot(weights, value, preferred_element_type=jnp.float32)
        summed = stacked(sum_ref, heads) * fade + more[:, :HEAD_SIZE]
        total = stacked(total_ref, heads) * fade + more[:, HEAD_SIZE:]
        finish(heads, g, summed, total)

    @pl.when(wanted)
    def _():
        in_turn(chains(), match, weigh, gather)

    if last:
        @pl.when(jnp.logical_not(wanted))
        def _():
            in_turn(
                chains(),
                lambda heads, g: finish(heads, g, stacked(sum_ref, heads), stacked(total_ref, heads)),
            )

        for n in range(len(chains())):
            out_copy(n).wait()


def behind_part(behind, last, needed, bias, queries, block, kept):
    rows = queries.shape[0]
    area = rows * rows * QUERY_HEADS
    operands = in_vmem(needed, bias, queries, block, *kept)
    if last:
        out_shape = jax.ShapeDtypeStruct(queries.shape, queries.dtype)
        out_specs = HBM
        scratch = [
            pltpu.VMEM(queries.shape, queries.dtype),
            pltpu.SemaphoreType.DMA((len(chains()),)),
        ]
        aliases = {}
    else:
        out_shape = tuple(pltpu.VMEM(x.shape, x.dtype) for x in kept)
        out_specs = (VMEM,) * len(kept)
        scratch = []
        aliases = {4 + n: n for n in range(len(kept))}
    return pl.pallas_call(
        functools.partial(behind_kernel, behind, last, rows),
        out_shape=out_shape,
        in_specs=[VMEM] * len(operands),
        out_specs=out_specs,
        scratch_shapes=scratch,
        input_output_aliases=aliases,
        compiler_params=pltpu.CompilerParams(vmem_limit_bytes=10 * 1024 * 1024),
        cost_estimate=pl.CostEstimate(
            flops=4 * area, bytes_accessed=queries.size, transcendentals=0
        ),
    )(*operands)


def per_device(queries, keys, values, lengths):
    count = lax.axis_size("dp") * lax.axis_size("ctx")
    rounds = lax.axis_size("ctx")
    size = 2 * keys.shape[0]

    def from_behind(block, r):
        by = 2 * (r + 1)
        pairs = [(i, i + by) for i in range(count - by)]
        if r == rounds - 1:
            pairs = [(i, j ^ 1) for i, j in pairs]
        return lax.ppermute(block, AXES, pairs)

    own = pack(keys, values)
    fetched = [from_behind(own, 0)]
    longer, bias, needed, own_bias, queries, *kept = own_part(lengths, queries, own, rounds)
    fetched += [from_behind(longer, r) for r in range(1, rounds)]
    kept = own_rest(own, own_bias, queries, kept)

    swap = [(i, i ^ 1) for i in range(count)]
    nearer = own
    for r, further in enumerate(fetched[:-1]):
        odd = kept[0]
        near = lax.ppermute(jnp.where(odd == 1, further[:size], nearer[:size]), AXES, swap)
        kept = behind_part(2 * r + 2, False, needed, bias, queries, further, kept)
        kept = behind_part(2 * r + 1, False, needed, bias, queries, near, kept)
        nearer = further
    to_odd = lax.ppermute(nearer[:size], AXES, [(i, i + 1) for i in range(0, count, 2)])
    odd = kept[0]
    sent = jnp.where(odd >= 0, fetched[-1][:size], nearer[:size])
    furthest = lax.ppermute(sent, AXES, swap)
    near = jnp.where(odd == 1, to_odd, sent)
    kept = behind_part(2 * rounds - 1, False, needed, bias, queries, near, kept)
    return behind_part(2 * rounds, True, needed, bias, queries, furthest, kept)


def solution(mesh):
    in_specs = (P(AXES, None), P(AXES, None), P(AXES, None), P())
    return jax.shard_map(
        per_device, mesh=mesh, in_specs=in_specs, out_specs=P(AXES, None), check_vma=False
    )
```

```python
import functools
import math

import jax
import jax.numpy as jnp
from jax import lax
from jax.experimental import pallas as pl
from jax.experimental.pallas import tpu as pltpu
from jax.sharding import PartitionSpec as P

HEAD_SIZE = 128
QUERY_HEADS = 32
KEY_VALUE_HEADS = 4
GROUP = QUERY_HEADS // KEY_VALUE_HEADS
HEADS_AT_ONCE = 8
EARLY_CHAINS = 2
EXCLUDED = -1e30
PAD = 16
AXES = ("dp", "ctx")


FACTOR = math.log2(math.e) / math.sqrt(HEAD_SIZE)


def head_columns(i):
    return slice(i * HEAD_SIZE, (i + 1) * HEAD_SIZE)


def stacked(ref, heads):
    return jnp.concatenate([ref[:, head_columns(i)] for i in heads], axis=0)


def spread(ref, heads, rows, value):
    for n, i in enumerate(heads):
        ref[:, head_columns(i)] = value[n * rows : (n + 1) * rows].astype(ref.dtype)


def with_ones(value):
    return jnp.concatenate([value, jnp.ones(value.shape, value.dtype)], axis=1)


def scores_of(q, key, bias):
    scores = lax.dot_general(
        q, key, (((1,), (1,)), ((), ())), preferred_element_type=jnp.float32
    )
    return scores + jnp.concatenate([bias] * (q.shape[0] // bias.shape[0]), axis=0)


def weights_of(scores, top):
    return jnp.exp2((scores - top) * jnp.float32(FACTOR)).astype(jnp.bfloat16)


def normalised(summed, total):
    inverse = pl.reciprocal(total, approx=True)
    return summed * (inverse * (2.0 - total * inverse))


def chains():
    return [
        (range(h, h + HEADS_AT_ONCE), h // GROUP) for h in range(0, QUERY_HEADS, HEADS_AT_ONCE)
    ]


def in_turn(runs, *stages):
    results = {}
    for turn in range(len(runs) + len(stages) - 1):
        for n, stage in enumerate(stages):
            i = turn - n
            if 0 <= i < len(runs):
                results[i] = stage(*runs[i], *results.pop(i, ()))


def pack_kernel(key_hbm, value_hbm, out_ref, sems):
    rows = key_hbm.shape[0]
    copies = [
        pltpu.make_async_copy(key_hbm, out_ref.at[:rows], sems.at[0]),
        pltpu.make_async_copy(value_hbm, out_ref.at[rows:], sems.at[1]),
    ]
    for copy in copies:
        copy.start()
    for copy in copies:
        copy.wait()


def pack(keys, values):
    rows, width = keys.shape
    return pl.pallas_call(
        pack_kernel,
        out_shape=pltpu.VMEM((2 * rows, width), keys.dtype),
        in_specs=[HBM, HBM],
        out_specs=VMEM,
        scratch_shapes=[pltpu.SemaphoreType.DMA((2,))],
        compiler_params=pltpu.CompilerParams(vmem_limit_bytes=1024 * 1024),
    )(*in_hbm(keys, values))


def attend_own(runs, rows, own_ref, own_bias_ref, q_ref, top_ref, total_ref, sum_ref, ready):
    def match(heads, g):
        ready(heads, g)
        key = own_ref[:rows, head_columns(g)]
        return (scores_of(stacked(q_ref, heads), key, own_bias_ref[...]),)

    def weigh(heads, g, scores):
        top = jnp.max(scores, axis=1, keepdims=True)
        spread(top_ref, heads, rows, jnp.broadcast_to(top, scores.shape))
        return (weights_of(scores, top),)

    def gather(heads, g, weights):
        value = with_ones(own_ref[rows:, head_columns(g)])
        summed = jnp.dot(weights, value, preferred_element_type=jnp.float32)
        spread(sum_ref, heads, rows, summed[:, :HEAD_SIZE])
        spread(total_ref, heads, rows, summed[:, HEAD_SIZE:])

    in_turn(runs, match, weigh, gather)


def own_kernel(
    rounds, rows, own_ref, lengths_hbm, q_hbm,
    longer_ref, bias_ref, needed_ref, own_bias_ref, q_ref, odd_ref, top_ref, total_ref, sum_ref,
    lengths_ref, lengths_sem, q_sems,
):
    lengths_copy = pltpu.make_async_copy(lengths_hbm, lengths_ref, lengths_sem)
    lengths_copy.start()
    width = GROUP * HEAD_SIZE
    q_copies = []
    for g in range(KEY_VALUE_HEADS):
        at = slice(g * width, (g + 1) * width)
        q_copies.append(pltpu.make_async_copy(q_hbm.at[:, at], q_ref.at[:, at], q_sems.at[g]))
        q_copies[g].start()
    me = lax.axis_index("dp") * lax.axis_size("ctx") + lax.axis_index("ctx")
    longer_ref[: 2 * rows, :] = own_ref[...]
    longer_ref[2 * rows :, :] = jnp.zeros((PAD, longer_ref.shape[1]), longer_ref.dtype)
    odd_ref[...] = jnp.full(odd_ref.shape, lax.rem(me, 2), jnp.int32)
    first = me * rows
    query_pos = first + lax.broadcasted_iota(jnp.int32, (rows, rows), 0)
    lengths_copy.wait()

    def later(doc, carried):
        bound, start, first_start = carried
        start = jnp.where(query_pos >= bound, bound, start)
        first_start = jnp.where(first >= bound, bound, first_start)
        return bound + lengths_ref[doc], start, first_start

    zero = jnp.int32(0)
    _, start, first_start = lax.fori_loop(
        0,
        lengths_ref.shape[0],
        later,
        (zero, jnp.zeros((rows, rows), jnp.int32), zero),
        unroll=8,
    )
    needed = lax.div(first - first_start + (rows - 1), jnp.int32(rows))
    needed_ref[...] = jnp.full(needed_ref.shape, needed, jnp.int32)
    lane = lax.broadcasted_iota(jnp.int32, (rows, rows), 1)

    def bias_of(allowed):
        return jnp.where(allowed, jnp.float32(0.0), jnp.float32(EXCLUDED))

    key_pos = first + lane
    own_bias_ref[...] = bias_of((key_pos >= start) & (key_pos <= query_pos))
    for b in range(2 * rounds):
        key_pos = first - (b + 1) * rows + lane
        bias_ref[:, b * rows : (b + 1) * rows] = bias_of(key_pos >= start)

    def ready(heads, g):
        if heads[0] % GROUP == 0:
            q_copies[g].wait()

    runs = chains()[:EARLY_CHAINS]
    attend_own(runs, rows, own_ref, own_bias_ref, q_ref, top_ref, total_ref, sum_ref, ready)
    for copy in q_copies[runs[-1][1] + 1 :]:
        copy.wait()


def own_rest_kernel(
    rows, own_ref, own_bias_ref, q_ref, odd_ref, *parts
):
    runs = chains()[EARLY_CHAINS:]
    parts = parts[4:]
    attend_own(runs, rows, own_ref, own_bias_ref, q_ref, *parts, lambda heads, g: None)


def in_vmem(*operands):
    return [pltpu.with_memory_space_constraint(x, pltpu.VMEM) for x in operands]


def in_hbm(*operands):
    return [pltpu.with_memory_space_constraint(x, pltpu.HBM) for x in operands]


SMEM = pl.BlockSpec(memory_space=pltpu.SMEM)
VMEM = pl.BlockSpec(memory_space=pltpu.VMEM)
HBM = pl.BlockSpec(memory_space=pltpu.HBM)


def own_part(lengths, queries, own, rounds):
    rows = queries.shape[0]
    part = pltpu.VMEM(queries.shape, jnp.float32)
    return pl.pallas_call(
        functools.partial(own_kernel, rounds, rows),
        out_shape=(
            pltpu.VMEM((2 * rows + PAD, own.shape[1]), own.dtype),
            pltpu.VMEM((rows, 2 * rounds * rows), jnp.float32),
            pltpu.VMEM((8, 128), jnp.int32),
            pltpu.VMEM((rows, rows), jnp.float32),
            pltpu.VMEM(queries.shape, queries.dtype),
            pltpu.VMEM((1, own.shape[1]), jnp.int32),
            part,
            part,
            part,
        ),
        in_specs=[VMEM, HBM, HBM],
        out_specs=(VMEM,) * 9,
        scratch_shapes=[
            pltpu.SMEM(lengths.shape, jnp.int32),
            pltpu.SemaphoreType.DMA,
            pltpu.SemaphoreType.DMA((KEY_VALUE_HEADS,)),
        ],
        compiler_params=pltpu.CompilerParams(vmem_limit_bytes=10 * 1024 * 1024),
        cost_estimate=pl.CostEstimate(
            flops=4 * 10**9, bytes_accessed=16 * 10**6, transcendentals=rows * queries.size
        ),
    )(*in_vmem(own), *in_hbm(lengths, queries))


def own_rest(own, own_bias, queries, kept):
    rows = queries.shape[0]
    operands = in_vmem(own, own_bias, queries, *kept)
    return pl.pallas_call(
        functools.partial(own_rest_kernel, rows),
        out_shape=tuple(pltpu.VMEM(x.shape, x.dtype) for x in kept),
        in_specs=[VMEM] * len(operands),
        out_specs=(VMEM,) * len(kept),
        input_output_aliases={3 + n: n for n in range(len(kept))},
        compiler_params=pltpu.CompilerParams(vmem_limit_bytes=10 * 1024 * 1024),
        cost_estimate=pl.CostEstimate(
            flops=4 * 10**9, bytes_accessed=16 * 10**6, transcendentals=rows * queries.size
        ),
    )(*operands)


def behind_kernel(
    before, last, rows, needed_ref, bias_ref, q_ref, near_ref, further_ref, top_ref, total_ref, sum_ref, *refs
):
    beyond = needed_ref[0, 0] - before
    pairs = [(ref.at[:rows], ref.at[rows : 2 * rows]) for ref in (near_ref, further_ref)]
    if last:
        out_hbm, out_ref, out_sems = refs

        def out_copy(n):
            width = HEADS_AT_ONCE * HEAD_SIZE
            at = slice(n * width, (n + 1) * width)
            return pltpu.make_async_copy(out_ref.at[:, at], out_hbm.at[:, at], out_sems.at[n])

    else:
        _, new_top_ref, new_total_ref, new_sum_ref = refs

    def finish(heads, g, summed, total):
        if last:
            spread(out_ref, heads, rows, normalised(summed, total))
            out_copy(heads[0] // HEADS_AT_ONCE).start()
        else:
            spread(new_sum_ref, heads, rows, summed)
            spread(new_total_ref, heads, rows, total)

    def attend(count):
        def match(heads, g):
            key = jnp.concatenate([key[:, head_columns(g)] for key, _ in pairs[:count]], axis=0)
            bias = bias_ref[:, before * rows : (before + count) * rows]
            return (scores_of(stacked(q_ref, heads), key, bias),)

        def weigh(heads, g, scores):
            old_top = stacked(top_ref, heads)
            top = jnp.maximum(old_top, jnp.max(scores, axis=1, keepdims=True))
            fade = jnp.exp2((old_top - top) * jnp.float32(FACTOR))
            if not last:
                spread(new_top_ref, heads, rows, top)
            return weights_of(scores, jnp.concatenate([top] * count, axis=1)), fade

        def gather(heads, g, weights, fade):
            value = jnp.concatenate([value[:, head_columns(g)] for _, value in pairs[:count]], axis=0)
            more = jnp.dot(weights, with_ones(value), preferred_element_type=jnp.float32)
            summed = stacked(sum_ref, heads) * fade + more[:, :HEAD_SIZE]
            total = stacked(total_ref, heads) * fade + more[:, HEAD_SIZE:]
            finish(heads, g, summed, total)

        in_turn(chains(), match, weigh, gather)

    @pl.when(beyond > 1)
    def _():
        attend(2)

    @pl.when(beyond == 1)
    def _():
        attend(1)

    if last:
        @pl.when(beyond < 1)
        def _():
            in_turn(
                chains(),
                lambda heads, g: finish(heads, g, stacked(sum_ref, heads), stacked(total_ref, heads)),
            )

        for n in range(len(chains())):
            out_copy(n).wait()


def behind_part(before, last, needed, bias, queries, near, further, parts):
    rows = queries.shape[0]
    area = rows * rows * 2 * QUERY_HEADS
    operands = in_vmem(needed, bias, queries, near, further, *parts)
    if last:
        out_shape = jax.ShapeDtypeStruct(queries.shape, queries.dtype)
        out_specs = HBM
        scratch = [
            pltpu.VMEM(queries.shape, queries.dtype),
            pltpu.SemaphoreType.DMA((len(chains()),)),
        ]
        aliases = {}
    else:
        kept = (further, *parts)
        out_shape = tuple(pltpu.VMEM(part.shape, part.dtype) for part in kept)
        out_specs = (VMEM,) * len(kept)
        scratch = []
        aliases = {4 + n: n for n in range(len(kept))}
    return pl.pallas_call(
        functools.partial(behind_kernel, before, last, rows),
        out_shape=out_shape,
        in_specs=[VMEM] * len(operands),
        out_specs=out_specs,
        scratch_shapes=scratch,
        input_output_aliases=aliases,
        compiler_params=pltpu.CompilerParams(vmem_limit_bytes=10 * 1024 * 1024),
        cost_estimate=pl.CostEstimate(
            flops=4 * area, bytes_accessed=queries.size, transcendentals=0
        ),
    )(*operands)


def per_device(queries, keys, values, lengths):
    count = lax.axis_size("dp") * lax.axis_size("ctx")
    rounds = lax.axis_size("ctx")

    def from_behind(block, r):
        by = 2 * (r + 1)
        return lax.ppermute(block, AXES, [(i, i + by) for i in range(count - by)])

    own = pack(keys, values)
    fetched = [from_behind(own, 0)]
    longer, bias, needed, own_bias, queries, *kept = own_part(lengths, queries, own, rounds)
    fetched += [from_behind(longer, r) for r in range(1, rounds)]
    odd, *parts = own_rest(own, own_bias, queries, kept)
    swap = [(i, i ^ 1) for i in range(count)]
    nearer = own
    size = 2 * keys.shape[0]
    for r, further in enumerate(fetched):
        last = r == rounds - 1
        near = lax.ppermute(jnp.where(odd == 1, further[:size], nearer[:size]), AXES, swap)
        result = behind_part(2 * r, last, needed, bias, queries, near, further, parts)
        if not last:
            nearer, *parts = result
    return result


def solution(mesh):
    in_specs = (P(AXES, None), P(AXES, None), P(AXES, None), P())
    return jax.shard_map(
        per_device, mesh=mesh, in_specs=in_specs, out_specs=P(AXES, None), check_vma=False
    )
```

```python
import functools
import math

import jax
import jax.numpy as jnp
from jax import lax
from jax.experimental import pallas as pl
from jax.experimental.pallas import tpu as pltpu
from jax.sharding import PartitionSpec as P

HEAD_SIZE = 128
QUERY_HEADS = 32
KEY_VALUE_HEADS = 4
GROUP = QUERY_HEADS // KEY_VALUE_HEADS
HEADS_AT_ONCE = 4
EARLY_CHAINS = 4
EXCLUDED = -1e30
PAD = 16
AXES = ("dp", "ctx")


FACTOR = math.log2(math.e) / math.sqrt(HEAD_SIZE)


def head_columns(i):
    return slice(i * HEAD_SIZE, (i + 1) * HEAD_SIZE)


def stacked(ref, heads):
    return jnp.concatenate([ref[:, head_columns(i)] for i in heads], axis=0)


def spread(ref, heads, rows, value):
    for n, i in enumerate(heads):
        ref[:, head_columns(i)] = value[n * rows : (n + 1) * rows].astype(ref.dtype)


def with_ones(value):
    return jnp.concatenate([value, jnp.ones(value.shape, value.dtype)], axis=1)


def scores_of(q, key, bias):
    scores = lax.dot_general(
        q, key, (((1,), (1,)), ((), ())), preferred_element_type=jnp.float32
    )
    return scores + jnp.concatenate([bias] * (q.shape[0] // bias.shape[0]), axis=0)


def weights_of(scores, top):
    return jnp.exp2((scores - top) * jnp.float32(FACTOR)).astype(jnp.bfloat16)


def normalised(summed, total):
    inverse = pl.reciprocal(total, approx=True)
    return summed * (inverse * (2.0 - total * inverse))


def level_of(top, total):
    return top + jnp.log(total) * jnp.float32(math.sqrt(HEAD_SIZE))


def chains():
    return [
        (range(h, h + HEADS_AT_ONCE), h // GROUP) for h in range(0, QUERY_HEADS, HEADS_AT_ONCE)
    ]


def in_turn(runs, *stages):
    results = {}
    for turn in range(len(runs) + len(stages) - 1):
        for n, stage in enumerate(stages):
            i = turn - n
            if 0 <= i < len(runs):
                results[i] = stage(*runs[i], *results.pop(i, ()))


def pack_kernel(key_hbm, value_hbm, out_ref, sems):
    rows = key_hbm.shape[0]
    copies = [
        pltpu.make_async_copy(key_hbm, out_ref.at[:rows], sems.at[0]),
        pltpu.make_async_copy(value_hbm, out_ref.at[rows:], sems.at[1]),
    ]
    for copy in copies:
        copy.start()
    for copy in copies:
        copy.wait()


def pack(keys, values):
    rows, width = keys.shape
    return pl.pallas_call(
        pack_kernel,
        out_shape=pltpu.VMEM((2 * rows, width), keys.dtype),
        in_specs=[HBM, HBM],
        out_specs=VMEM,
        scratch_shapes=[pltpu.SemaphoreType.DMA((2,))],
        compiler_params=pltpu.CompilerParams(vmem_limit_bytes=1024 * 1024),
    )(*in_hbm(keys, values))


def attend_own(runs, rows, own_ref, own_bias_ref, q_ref, level_ref, mean_ref, ready):
    def match(heads, g):
        ready(heads, g)
        key = own_ref[:rows, head_columns(g)]
        return (scores_of(stacked(q_ref, heads), key, own_bias_ref[...]),)

    def weigh(heads, g, scores):
        top = jnp.max(scores, axis=1, keepdims=True)
        return weights_of(scores, top), jnp.broadcast_to(top, scores.shape)

    def gather(heads, g, weights, top):
        value = with_ones(own_ref[rows:, head_columns(g)])
        more = jnp.dot(weights, value, preferred_element_type=jnp.float32)
        summed, total = more[:, :HEAD_SIZE], more[:, HEAD_SIZE:]
        spread(mean_ref, heads, rows, normalised(summed, total))
        spread(level_ref, heads, rows, level_of(top, total))

    in_turn(runs, match, weigh, gather)


def own_kernel(
    rounds, rows, own_ref, lengths_hbm, q_hbm,
    longer_ref, bias_ref, needed_ref, own_bias_ref, q_ref, odd_ref, level_ref, mean_ref,
    lengths_ref, lengths_sem, q_sems,
):
    lengths_copy = pltpu.make_async_copy(lengths_hbm, lengths_ref, lengths_sem)
    lengths_copy.start()
    width = GROUP * HEAD_SIZE
    q_copies = []
    for g in range(KEY_VALUE_HEADS):
        at = slice(g * width, (g + 1) * width)
        q_copies.append(pltpu.make_async_copy(q_hbm.at[:, at], q_ref.at[:, at], q_sems.at[g]))
        q_copies[g].start()
    me = lax.axis_index("dp") * lax.axis_size("ctx") + lax.axis_index("ctx")
    longer_ref[: 2 * rows, :] = own_ref[...]
    longer_ref[2 * rows :, :] = jnp.zeros((PAD, longer_ref.shape[1]), longer_ref.dtype)
    odd_ref[...] = jnp.full(odd_ref.shape, lax.rem(me, 2), jnp.int32)
    first = me * rows
    query_pos = first + lax.broadcasted_iota(jnp.int32, (rows, rows), 0)
    lengths_copy.wait()

    def later(doc, carried):
        bound, start, first_start = carried
        start = jnp.where(query_pos >= bound, bound, start)
        first_start = jnp.where(first >= bound, bound, first_start)
        return bound + lengths_ref[doc], start, first_start

    zero = jnp.int32(0)
    _, start, first_start = lax.fori_loop(
        0,
        lengths_ref.shape[0],
        later,
        (zero, jnp.zeros((rows, rows), jnp.int32), zero),
        unroll=8,
    )
    needed = lax.div(first - first_start + (rows - 1), jnp.int32(rows))
    needed_ref[...] = jnp.full(needed_ref.shape, needed, jnp.int32)
    lane = lax.broadcasted_iota(jnp.int32, (rows, rows), 1)

    def bias_of(allowed):
        return jnp.where(allowed, jnp.float32(0.0), jnp.float32(EXCLUDED))

    key_pos = first + lane
    own_bias_ref[...] = bias_of((key_pos >= start) & (key_pos <= query_pos))
    for b in range(2 * rounds):
        key_pos = first - (b + 1) * rows + lane
        bias_ref[:, b * rows : (b + 1) * rows] = bias_of(key_pos >= start)

    def ready(heads, g):
        if heads[0] % GROUP == 0:
            q_copies[g].wait()

    runs = chains()[:EARLY_CHAINS]
    attend_own(runs, rows, own_ref, own_bias_ref, q_ref, level_ref, mean_ref, ready)
    for copy in q_copies[runs[-1][1] + 1 :]:
        copy.wait()


def own_rest_kernel(
    rows, own_ref, own_bias_ref, q_ref, odd_ref, *parts
):
    runs = chains()[EARLY_CHAINS:]
    parts = parts[3:]
    attend_own(runs, rows, own_ref, own_bias_ref, q_ref, *parts, lambda heads, g: None)


def in_vmem(*operands):
    return [pltpu.with_memory_space_constraint(x, pltpu.VMEM) for x in operands]


def in_hbm(*operands):
    return [pltpu.with_memory_space_constraint(x, pltpu.HBM) for x in operands]


SMEM = pl.BlockSpec(memory_space=pltpu.SMEM)
VMEM = pl.BlockSpec(memory_space=pltpu.VMEM)
HBM = pl.BlockSpec(memory_space=pltpu.HBM)


def own_part(lengths, queries, own, rounds):
    rows = queries.shape[0]
    part = pltpu.VMEM(queries.shape, jnp.float32)
    return pl.pallas_call(
        functools.partial(own_kernel, rounds, rows),
        out_shape=(
            pltpu.VMEM((2 * rows + PAD, own.shape[1]), own.dtype),
            pltpu.VMEM((rows, 2 * rounds * rows), jnp.float32),
            pltpu.VMEM((8, 128), jnp.int32),
            pltpu.VMEM((rows, rows), jnp.float32),
            pltpu.VMEM(queries.shape, queries.dtype),
            pltpu.VMEM((1, own.shape[1]), jnp.int32),
            part,
            part,
        ),
        in_specs=[VMEM, HBM, HBM],
        out_specs=(VMEM,) * 8,
        scratch_shapes=[
            pltpu.SMEM(lengths.shape, jnp.int32),
            pltpu.SemaphoreType.DMA,
            pltpu.SemaphoreType.DMA((KEY_VALUE_HEADS,)),
        ],
        compiler_params=pltpu.CompilerParams(vmem_limit_bytes=10 * 1024 * 1024),
        cost_estimate=pl.CostEstimate(
            flops=4 * 10**9, bytes_accessed=16 * 10**6, transcendentals=rows * queries.size
        ),
    )(*in_vmem(own), *in_hbm(lengths, queries))


def own_rest(own, own_bias, queries, kept):
    rows = queries.shape[0]
    operands = in_vmem(own, own_bias, queries, *kept)
    return pl.pallas_call(
        functools.partial(own_rest_kernel, rows),
        out_shape=tuple(pltpu.VMEM(x.shape, x.dtype) for x in kept),
        in_specs=[VMEM] * len(operands),
        out_specs=(VMEM,) * len(kept),
        input_output_aliases={3 + n: n for n in range(len(kept))},
        compiler_params=pltpu.CompilerParams(vmem_limit_bytes=10 * 1024 * 1024),
        cost_estimate=pl.CostEstimate(
            flops=4 * 10**9, bytes_accessed=16 * 10**6, transcendentals=rows * queries.size
        ),
    )(*operands)


def behind_kernel(
    before, last, rows, needed_ref, bias_ref, q_ref, near_ref, further_ref, level_ref, mean_ref, *refs
):
    beyond = needed_ref[0, 0] - before
    pairs = [(ref.at[:rows], ref.at[rows : 2 * rows]) for ref in (near_ref, further_ref)]
    if last:
        out_hbm, out_ref, out_sems = refs

        def out_copy(n):
            width = HEADS_AT_ONCE * HEAD_SIZE
            at = slice(n * width, (n + 1) * width)
            return pltpu.make_async_copy(out_ref.at[:, at], out_hbm.at[:, at], out_sems.at[n])

    else:
        _, new_level_ref, new_mean_ref = refs

    def finish(heads, mean):
        spread(out_ref, heads, rows, mean)
        out_copy(heads[0] // HEADS_AT_ONCE).start()

    def attend(count):
        def match(heads, g):
            key = jnp.concatenate([key[:, head_columns(g)] for key, _ in pairs[:count]], axis=0)
            bias = bias_ref[:, before * rows : (before + count) * rows]
            return (scores_of(stacked(q_ref, heads), key, bias),)

        def weigh(heads, g, scores):
            level = stacked(level_ref, heads)
            top = jnp.maximum(level, jnp.max(scores, axis=1, keepdims=True))
            fade = jnp.exp2((level - top) * jnp.float32(FACTOR))
            return weights_of(scores, jnp.concatenate([top] * count, axis=1)), fade, top

        def gather(heads, g, weights, fade, top):
            value = jnp.concatenate([value[:, head_columns(g)] for _, value in pairs[:count]], axis=0)
            more = jnp.dot(weights, with_ones(value), preferred_element_type=jnp.float32)
            summed = stacked(mean_ref, heads) * fade + more[:, :HEAD_SIZE]
            total = fade + more[:, HEAD_SIZE:]
            if last:
                finish(heads, normalised(summed, total))
            else:
                spread(new_mean_ref, heads, rows, normalised(summed, total))
                spread(new_level_ref, heads, rows, level_of(top, total))

        in_turn(chains(), match, weigh, gather)

    @pl.when(beyond > 1)
    def _():
        attend(2)

    @pl.when(beyond == 1)
    def _():
        attend(1)

    if last:
        @pl.when(beyond < 1)
        def _():
            in_turn(
                chains(),
                lambda heads, g: finish(heads, stacked(mean_ref, heads)),
            )

        for n in range(len(chains())):
            out_copy(n).wait()


def behind_part(before, last, needed, bias, queries, near, further, parts):
    rows = queries.shape[0]
    area = rows * rows * 2 * QUERY_HEADS
    operands = in_vmem(needed, bias, queries, near, further, *parts)
    if last:
        out_shape = jax.ShapeDtypeStruct(queries.shape, queries.dtype)
        out_specs = HBM
        scratch = [
            pltpu.VMEM(queries.shape, queries.dtype),
            pltpu.SemaphoreType.DMA((len(chains()),)),
        ]
        aliases = {}
    else:
        kept = (further, *parts)
        out_shape = tuple(pltpu.VMEM(part.shape, part.dtype) for part in kept)
        out_specs = (VMEM,) * len(kept)
        scratch = []
        aliases = {4 + n: n for n in range(len(kept))}
    return pl.pallas_call(
        functools.partial(behind_kernel, before, last, rows),
        out_shape=out_shape,
        in_specs=[VMEM] * len(operands),
        out_specs=out_specs,
        scratch_shapes=scratch,
        input_output_aliases=aliases,
        compiler_params=pltpu.CompilerParams(vmem_limit_bytes=10 * 1024 * 1024),
        cost_estimate=pl.CostEstimate(
            flops=4 * area, bytes_accessed=queries.size, transcendentals=0
        ),
    )(*operands)


def per_device(queries, keys, values, lengths):
    count = lax.axis_size("dp") * lax.axis_size("ctx")
    rounds = lax.axis_size("ctx")

    def from_behind(block, r):
        by = 2 * (r + 1)
        return lax.ppermute(block, AXES, [(i, i + by) for i in range(count - by)])

    own = pack(keys, values)
    fetched = [from_behind(own, 0)]
    longer, bias, needed, own_bias, queries, *kept = own_part(lengths, queries, own, rounds)
    fetched += [from_behind(longer, r) for r in range(1, rounds)]
    odd, *parts = own_rest(own, own_bias, queries, kept)
    swap = [(i, i ^ 1) for i in range(count)]
    nearer = own
    size = 2 * keys.shape[0]
    for r, further in enumerate(fetched):
        last = r == rounds - 1
        near = lax.ppermute(jnp.where(odd == 1, further[:size], nearer[:size]), AXES, swap)
        result = behind_part(2 * r, last, needed, bias, queries, near, further, parts)
        if not last:
            nearer, *parts = result
    return result


def solution(mesh):
    in_specs = (P(AXES, None), P(AXES, None), P(AXES, None), P())
    return jax.shard_map(
        per_device, mesh=mesh, in_specs=in_specs, out_specs=P(AXES, None), check_vma=False
    )
```

```python
import functools
import math

import jax
import jax.numpy as jnp
from jax import lax
from jax.experimental import pallas as pl
from jax.experimental.pallas import tpu as pltpu
from jax.sharding import PartitionSpec as P

HEAD_SIZE = 128
QUERY_HEADS = 32
KEY_VALUE_HEADS = 4
GROUP = QUERY_HEADS // KEY_VALUE_HEADS
HEADS_AT_ONCE = 2
EARLY_CHAINS = 10
EXCLUDED = -1e30
PAD = 16
AXES = ("dp", "ctx")


FACTOR = math.log2(math.e) / math.sqrt(HEAD_SIZE)


def head_columns(i):
    return slice(i * HEAD_SIZE, (i + 1) * HEAD_SIZE)


def stacked(ref, heads):
    return jnp.concatenate([ref[:, head_columns(i)] for i in heads], axis=0)


def spread(ref, heads, rows, value):
    for n, i in enumerate(heads):
        ref[:, head_columns(i)] = value[n * rows : (n + 1) * rows].astype(ref.dtype)


def with_ones(value):
    return jnp.concatenate([value, jnp.ones(value.shape, value.dtype)], axis=1)


def scores_of(q, key, bias):
    scores = lax.dot_general(
        q, key, (((1,), (1,)), ((), ())), preferred_element_type=jnp.float32
    )
    return scores + jnp.concatenate([bias] * (q.shape[0] // bias.shape[0]), axis=0)


def weights_of(scores, top):
    return jnp.exp2((scores - top) * jnp.float32(FACTOR)).astype(jnp.bfloat16)


def normalised(summed, total):
    inverse = pl.reciprocal(total, approx=True)
    return summed * (inverse * (2.0 - total * inverse))


def level_of(top, total):
    return top + jnp.log(total) * jnp.float32(math.sqrt(HEAD_SIZE))


def chains():
    return [
        (range(h, h + HEADS_AT_ONCE), h // GROUP) for h in range(0, QUERY_HEADS, HEADS_AT_ONCE)
    ]


def in_turn(runs, *stages):
    results = {}
    for turn in range(len(runs) + len(stages) - 1):
        for n, stage in enumerate(stages):
            i = turn - n
            if 0 <= i < len(runs):
                results[i] = stage(*runs[i], *results.pop(i, ()))


def pack_kernel(key_hbm, value_hbm, out_ref, sems):
    rows = key_hbm.shape[0]
    copies = [
        pltpu.make_async_copy(key_hbm, out_ref.at[:rows], sems.at[0]),
        pltpu.make_async_copy(value_hbm, out_ref.at[rows:], sems.at[1]),
    ]
    for copy in copies:
        copy.start()
    for copy in copies:
        copy.wait()


def pack(keys, values):
    rows, width = keys.shape
    return pl.pallas_call(
        pack_kernel,
        out_shape=pltpu.VMEM((2 * rows, width), keys.dtype),
        in_specs=[HBM, HBM],
        out_specs=VMEM,
        scratch_shapes=[pltpu.SemaphoreType.DMA((2,))],
        compiler_params=pltpu.CompilerParams(vmem_limit_bytes=1024 * 1024),
    )(*in_hbm(keys, values))


def attend_own(runs, rows, own_ref, own_bias_ref, q_ref, level_ref, mean_ref, ready):
    def match(heads, g):
        ready(heads, g)
        key = own_ref[:rows, head_columns(g)]
        return (scores_of(stacked(q_ref, heads), key, own_bias_ref[...]),)

    def weigh(heads, g, scores):
        top = jnp.max(scores, axis=1, keepdims=True)
        return weights_of(scores, top), jnp.broadcast_to(top, scores.shape)

    def gather(heads, g, weights, top):
        value = with_ones(own_ref[rows:, head_columns(g)])
        more = jnp.dot(weights, value, preferred_element_type=jnp.float32)
        summed, total = more[:, :HEAD_SIZE], more[:, HEAD_SIZE:]
        spread(mean_ref, heads, rows, normalised(summed, total))
        spread(level_ref, heads, rows, level_of(top, total))

    in_turn(runs, match, weigh, gather)


def own_kernel(
    rounds, rows, own_ref, lengths_hbm, q_hbm,
    longer_ref, bias_ref, needed_ref, own_bias_ref, q_ref, odd_ref, level_ref, mean_ref,
    lengths_ref, lengths_sem, q_sems,
):
    lengths_copy = pltpu.make_async_copy(lengths_hbm, lengths_ref, lengths_sem)
    lengths_copy.start()
    width = GROUP * HEAD_SIZE
    q_copies = []
    for g in range(KEY_VALUE_HEADS):
        at = slice(g * width, (g + 1) * width)
        q_copies.append(pltpu.make_async_copy(q_hbm.at[:, at], q_ref.at[:, at], q_sems.at[g]))
        q_copies[g].start()
    me = lax.axis_index("dp") * lax.axis_size("ctx") + lax.axis_index("ctx")
    longer_ref[: 2 * rows, :] = own_ref[...]
    longer_ref[2 * rows :, :] = jnp.zeros((PAD, longer_ref.shape[1]), longer_ref.dtype)
    odd_ref[...] = jnp.full(odd_ref.shape, lax.rem(me, 2), jnp.int32)
    first = me * rows
    query_pos = first + lax.broadcasted_iota(jnp.int32, (rows, rows), 0)
    lengths_copy.wait()

    def later(doc, carried):
        bound, start, first_start = carried
        start = jnp.where(query_pos >= bound, bound, start)
        first_start = jnp.where(first >= bound, bound, first_start)
        return bound + lengths_ref[doc], start, first_start

    zero = jnp.int32(0)
    _, start, first_start = lax.fori_loop(
        0,
        lengths_ref.shape[0],
        later,
        (zero, jnp.zeros((rows, rows), jnp.int32), zero),
        unroll=8,
    )
    needed = lax.div(first - first_start + (rows - 1), jnp.int32(rows))
    needed_ref[...] = jnp.full(needed_ref.shape, needed, jnp.int32)
    lane = lax.broadcasted_iota(jnp.int32, (rows, rows), 1)

    def bias_of(allowed):
        return jnp.where(allowed, jnp.float32(0.0), jnp.float32(EXCLUDED))

    key_pos = first + lane
    own_bias_ref[...] = bias_of((key_pos >= start) & (key_pos <= query_pos))
    for b in range(2 * rounds):
        key_pos = first - (b + 1) * rows + lane
        bias_ref[:, b * rows : (b + 1) * rows] = bias_of(key_pos >= start)

    def ready(heads, g):
        if heads[0] % GROUP == 0:
            q_copies[g].wait()

    runs = chains()[:EARLY_CHAINS]
    attend_own(runs, rows, own_ref, own_bias_ref, q_ref, level_ref, mean_ref, ready)
    for copy in q_copies[runs[-1][1] + 1 :]:
        copy.wait()


def own_rest_kernel(
    rows, own_ref, own_bias_ref, q_ref, odd_ref, *parts
):
    runs = chains()[EARLY_CHAINS:]
    parts = parts[3:]
    attend_own(runs, rows, own_ref, own_bias_ref, q_ref, *parts, lambda heads, g: None)


def in_vmem(*operands):
    return [pltpu.with_memory_space_constraint(x, pltpu.VMEM) for x in operands]


def in_hbm(*operands):
    return [pltpu.with_memory_space_constraint(x, pltpu.HBM) for x in operands]


SMEM = pl.BlockSpec(memory_space=pltpu.SMEM)
VMEM = pl.BlockSpec(memory_space=pltpu.VMEM)
HBM = pl.BlockSpec(memory_space=pltpu.HBM)


def own_part(lengths, queries, own, rounds):
    rows = queries.shape[0]
    part = pltpu.VMEM(queries.shape, jnp.float32)
    return pl.pallas_call(
        functools.partial(own_kernel, rounds, rows),
        out_shape=(
            pltpu.VMEM((2 * rows + PAD, own.shape[1]), own.dtype),
            pltpu.VMEM((rows, 2 * rounds * rows), jnp.float32),
            pltpu.VMEM((8, 128), jnp.int32),
            pltpu.VMEM((rows, rows), jnp.float32),
            pltpu.VMEM(queries.shape, queries.dtype),
            pltpu.VMEM((1, own.shape[1]), jnp.int32),
            part,
            part,
        ),
        in_specs=[VMEM, HBM, HBM],
        out_specs=(VMEM,) * 8,
        scratch_shapes=[
            pltpu.SMEM(lengths.shape, jnp.int32),
            pltpu.SemaphoreType.DMA,
            pltpu.SemaphoreType.DMA((KEY_VALUE_HEADS,)),
        ],
        compiler_params=pltpu.CompilerParams(vmem_limit_bytes=10 * 1024 * 1024),
        cost_estimate=pl.CostEstimate(
            flops=4 * 10**9, bytes_accessed=16 * 10**6, transcendentals=rows * queries.size
        ),
    )(*in_vmem(own), *in_hbm(lengths, queries))


def own_rest(own, own_bias, queries, kept):
    rows = queries.shape[0]
    operands = in_vmem(own, own_bias, queries, *kept)
    return pl.pallas_call(
        functools.partial(own_rest_kernel, rows),
        out_shape=tuple(pltpu.VMEM(x.shape, x.dtype) for x in kept),
        in_specs=[VMEM] * len(operands),
        out_specs=(VMEM,) * len(kept),
        input_output_aliases={3 + n: n for n in range(len(kept))},
        compiler_params=pltpu.CompilerParams(vmem_limit_bytes=10 * 1024 * 1024),
        cost_estimate=pl.CostEstimate(
            flops=4 * 10**9, bytes_accessed=16 * 10**6, transcendentals=rows * queries.size
        ),
    )(*operands)


def behind_kernel(
    before, last, rows, needed_ref, bias_ref, q_ref, near_ref, further_ref, level_ref, mean_ref, *refs
):
    beyond = needed_ref[0, 0] - before
    pairs = [(ref.at[:rows], ref.at[rows : 2 * rows]) for ref in (near_ref, further_ref)]
    if last:
        out_hbm, out_ref, out_sems = refs

        def out_copy(n):
            width = HEADS_AT_ONCE * HEAD_SIZE
            at = slice(n * width, (n + 1) * width)
            return pltpu.make_async_copy(out_ref.at[:, at], out_hbm.at[:, at], out_sems.at[n])

    else:
        _, new_level_ref, new_mean_ref = refs

    def finish(heads, mean):
        spread(out_ref, heads, rows, mean)
        out_copy(heads[0] // HEADS_AT_ONCE).start()

    def attend(count):
        def match(heads, g):
            key = jnp.concatenate([key[:, head_columns(g)] for key, _ in pairs[:count]], axis=0)
            bias = bias_ref[:, before * rows : (before + count) * rows]
            return (scores_of(stacked(q_ref, heads), key, bias),)

        def weigh(heads, g, scores):
            level = stacked(level_ref, heads)
            top = jnp.maximum(level, jnp.max(scores, axis=1, keepdims=True))
            fade = jnp.exp2((level - top) * jnp.float32(FACTOR))
            return weights_of(scores, jnp.concatenate([top] * count, axis=1)), fade, top

        def gather(heads, g, weights, fade, top):
            value = jnp.concatenate([value[:, head_columns(g)] for _, value in pairs[:count]], axis=0)
            more = jnp.dot(weights, with_ones(value), preferred_element_type=jnp.float32)
            summed = stacked(mean_ref, heads) * fade + more[:, :HEAD_SIZE]
            total = fade + more[:, HEAD_SIZE:]
            if last:
                finish(heads, normalised(summed, total))
            else:
                spread(new_mean_ref, heads, rows, normalised(summed, total))
                spread(new_level_ref, heads, rows, level_of(top, total))

        in_turn(chains(), match, weigh, gather)

    @pl.when(beyond > 1)
    def _():
        attend(2)

    @pl.when(beyond == 1)
    def _():
        attend(1)

    if last:
        @pl.when(beyond < 1)
        def _():
            in_turn(
                chains(),
                lambda heads, g: finish(heads, stacked(mean_ref, heads)),
            )

        for n in range(len(chains())):
            out_copy(n).wait()


def behind_part(before, last, needed, bias, queries, near, further, parts):
    rows = queries.shape[0]
    area = rows * rows * 2 * QUERY_HEADS
    operands = in_vmem(needed, bias, queries, near, further, *parts)
    if last:
        out_shape = jax.ShapeDtypeStruct(queries.shape, queries.dtype)
        out_specs = HBM
        scratch = [
            pltpu.VMEM(queries.shape, queries.dtype),
            pltpu.SemaphoreType.DMA((len(chains()),)),
        ]
        aliases = {}
    else:
        kept = (further, *parts)
        out_shape = tuple(pltpu.VMEM(part.shape, part.dtype) for part in kept)
        out_specs = (VMEM,) * len(kept)
        scratch = []
        aliases = {4 + n: n for n in range(len(kept))}
    return pl.pallas_call(
        functools.partial(behind_kernel, before, last, rows),
        out_shape=out_shape,
        in_specs=[VMEM] * len(operands),
        out_specs=out_specs,
        scratch_shapes=scratch,
        input_output_aliases=aliases,
        compiler_params=pltpu.CompilerParams(vmem_limit_bytes=10 * 1024 * 1024),
        cost_estimate=pl.CostEstimate(
            flops=4 * area, bytes_accessed=queries.size, transcendentals=0
        ),
    )(*operands)


def per_device(queries, keys, values, lengths):
    count = lax.axis_size("dp") * lax.axis_size("ctx")
    rounds = lax.axis_size("ctx")

    def from_behind(block, r):
        by = 2 * (r + 1)
        return lax.ppermute(block, AXES, [(i, i + by) for i in range(count - by)])

    own = pack(keys, values)
    fetched = [from_behind(own, 0)]
    longer, bias, needed, own_bias, queries, *kept = own_part(lengths, queries, own, rounds)
    fetched += [from_behind(longer, r) for r in range(1, rounds)]
    odd, *parts = own_rest(own, own_bias, queries, kept)
    swap = [(i, i ^ 1) for i in range(count)]
    nearer = own
    size = 2 * keys.shape[0]
    for r, further in enumerate(fetched):
        last = r == rounds - 1
        near = lax.ppermute(jnp.where(odd == 1, further[:size], nearer[:size]), AXES, swap)
        result = behind_part(2 * r, last, needed, bias, queries, near, further, parts)
        if not last:
            nearer, *parts = result
    return result


def solution(mesh):
    in_specs = (P(AXES, None), P(AXES, None), P(AXES, None), P())
    return jax.shard_map(
        per_device, mesh=mesh, in_specs=in_specs, out_specs=P(AXES, None), check_vma=False
    )
```

```python
import functools
import math

import jax
import jax.numpy as jnp
from jax import lax
from jax.experimental import pallas as pl
from jax.experimental.pallas import tpu as pltpu
from jax.sharding import PartitionSpec as P

HEAD_SIZE = 128
QUERY_HEADS = 32
KEY_VALUE_HEADS = 4
GROUP = QUERY_HEADS // KEY_VALUE_HEADS
HEADS_AT_ONCE = 4
EARLY_CHAINS = 4
EXCLUDED = -1e30
TURNS = 2
PAD = 16
AXES = ("dp", "ctx")


FACTOR = math.log2(math.e) / math.sqrt(HEAD_SIZE)


def head_columns(i):
    return pl.ds(pl.multiple_of(i * HEAD_SIZE, HEAD_SIZE), HEAD_SIZE)


def stacked(ref, heads):
    return jnp.concatenate([ref[:, head_columns(i)] for i in heads], axis=0)


def spread(ref, heads, rows, value):
    for n, i in enumerate(heads):
        ref[:, head_columns(i)] = value[n * rows : (n + 1) * rows].astype(ref.dtype)


def with_ones(value):
    return jnp.concatenate([value, jnp.ones(value.shape, value.dtype)], axis=1)


def scores_of(q, key, bias):
    scores = lax.dot_general(
        q, key, (((1,), (1,)), ((), ())), preferred_element_type=jnp.float32
    )
    return scores + jnp.concatenate([bias] * (q.shape[0] // bias.shape[0]), axis=0)


def weights_of(scores, top):
    return jnp.exp2((scores - top) * jnp.float32(FACTOR)).astype(jnp.bfloat16)


def normalised(summed, total):
    inverse = pl.reciprocal(total, approx=True)
    return summed * (inverse * (2.0 - total * inverse))


def level_of(top, total):
    return top + jnp.log(total) * jnp.float32(math.sqrt(HEAD_SIZE))


def chains():
    return [
        (range(h, h + HEADS_AT_ONCE), h // GROUP) for h in range(0, QUERY_HEADS, HEADS_AT_ONCE)
    ]


def in_loop(*stages):
    runs = chains()[: len(chains()) // TURNS]

    def step(turn, _):
        first = turn * (QUERY_HEADS // TURNS)
        group = turn * (KEY_VALUE_HEADS // TURNS)
        in_turn([([first + i for i in heads], group + g) for heads, g in runs], *stages)
        return 0

    lax.fori_loop(0, TURNS, step, 0)


def in_turn(runs, *stages):
    results = {}
    for turn in range(len(runs) + len(stages) - 1):
        for n, stage in enumerate(stages):
            i = turn - n
            if 0 <= i < len(runs):
                results[i] = stage(*runs[i], *results.pop(i, ()))


def pack_kernel(key_hbm, value_hbm, out_ref, sems):
    rows = key_hbm.shape[0]
    copies = [
        pltpu.make_async_copy(key_hbm, out_ref.at[:rows], sems.at[0]),
        pltpu.make_async_copy(value_hbm, out_ref.at[rows:], sems.at[1]),
    ]
    for copy in copies:
        copy.start()
    for copy in copies:
        copy.wait()


def pack(keys, values):
    rows, width = keys.shape
    return pl.pallas_call(
        pack_kernel,
        out_shape=pltpu.VMEM((2 * rows, width), keys.dtype),
        in_specs=[HBM, HBM],
        out_specs=VMEM,
        scratch_shapes=[pltpu.SemaphoreType.DMA((2,))],
        compiler_params=pltpu.CompilerParams(vmem_limit_bytes=1024 * 1024),
    )(*in_hbm(keys, values))


def attend_own(runs, rows, own_ref, own_bias_ref, q_ref, level_ref, mean_ref, ready):
    def match(heads, g):
        ready(heads, g)
        key = own_ref[:rows, head_columns(g)]
        return (scores_of(stacked(q_ref, heads), key, own_bias_ref[...]),)

    def weigh(heads, g, scores):
        top = jnp.max(scores, axis=1, keepdims=True)
        return weights_of(scores, top), jnp.broadcast_to(top, scores.shape)

    def gather(heads, g, weights, top):
        value = with_ones(own_ref[rows:, head_columns(g)])
        more = jnp.dot(weights, value, preferred_element_type=jnp.float32)
        summed, total = more[:, :HEAD_SIZE], more[:, HEAD_SIZE:]
        spread(mean_ref, heads, rows, normalised(summed, total))
        spread(level_ref, heads, rows, level_of(top, total))

    in_turn(runs, match, weigh, gather)


def own_kernel(
    rounds, rows, own_ref, lengths_hbm, q_hbm,
    longer_ref, bias_ref, needed_ref, own_bias_ref, q_ref, odd_ref, level_ref, mean_ref,
    lengths_ref, lengths_sem, q_sems,
):
    lengths_copy = pltpu.make_async_copy(lengths_hbm, lengths_ref, lengths_sem)
    lengths_copy.start()
    width = GROUP * HEAD_SIZE
    q_copies = []
    for g in range(KEY_VALUE_HEADS):
        at = slice(g * width, (g + 1) * width)
        q_copies.append(pltpu.make_async_copy(q_hbm.at[:, at], q_ref.at[:, at], q_sems.at[g]))
        q_copies[g].start()
    me = lax.axis_index("dp") * lax.axis_size("ctx") + lax.axis_index("ctx")
    longer_ref[: 2 * rows, :] = own_ref[...]
    longer_ref[2 * rows :, :] = jnp.zeros((PAD, longer_ref.shape[1]), longer_ref.dtype)
    odd_ref[...] = jnp.full(odd_ref.shape, lax.rem(me, 2), jnp.int32)
    first = me * rows
    query_pos = first + lax.broadcasted_iota(jnp.int32, (rows, rows), 0)
    lengths_copy.wait()

    def later(doc, carried):
        bound, start, first_start = carried
        start = jnp.where(query_pos >= bound, bound, start)
        first_start = jnp.where(first >= bound, bound, first_start)
        return bound + lengths_ref[doc], start, first_start

    zero = jnp.int32(0)
    _, start, first_start = lax.fori_loop(
        0,
        lengths_ref.shape[0],
        later,
        (zero, jnp.zeros((rows, rows), jnp.int32), zero),
        unroll=8,
    )
    needed = lax.div(first - first_start + (rows - 1), jnp.int32(rows))
    needed_ref[...] = jnp.full(needed_ref.shape, needed, jnp.int32)
    lane = lax.broadcasted_iota(jnp.int32, (rows, rows), 1)

    def bias_of(allowed):
        return jnp.where(allowed, jnp.float32(0.0), jnp.float32(EXCLUDED))

    key_pos = first + lane
    own_bias_ref[...] = bias_of((key_pos >= start) & (key_pos <= query_pos))
    for b in range(2 * rounds):
        key_pos = first - (b + 1) * rows + lane
        bias_ref[:, b * rows : (b + 1) * rows] = bias_of(key_pos >= start)

    def ready(heads, g):
        if heads[0] % GROUP == 0:
            q_copies[g].wait()

    runs = chains()[:EARLY_CHAINS]
    attend_own(runs, rows, own_ref, own_bias_ref, q_ref, level_ref, mean_ref, ready)
    for copy in q_copies[runs[-1][1] + 1 :]:
        copy.wait()


def own_rest_kernel(
    rows, own_ref, own_bias_ref, q_ref, odd_ref, *parts
):
    runs = chains()[EARLY_CHAINS:]
    parts = parts[3:]
    attend_own(runs, rows, own_ref, own_bias_ref, q_ref, *parts, lambda heads, g: None)


def in_vmem(*operands):
    return [pltpu.with_memory_space_constraint(x, pltpu.VMEM) for x in operands]


def in_hbm(*operands):
    return [pltpu.with_memory_space_constraint(x, pltpu.HBM) for x in operands]


SMEM = pl.BlockSpec(memory_space=pltpu.SMEM)
VMEM = pl.BlockSpec(memory_space=pltpu.VMEM)
HBM = pl.BlockSpec(memory_space=pltpu.HBM)


def own_part(lengths, queries, own, rounds):
    rows = queries.shape[0]
    part = pltpu.VMEM(queries.shape, jnp.float32)
    return pl.pallas_call(
        functools.partial(own_kernel, rounds, rows),
        out_shape=(
            pltpu.VMEM((2 * rows + PAD, own.shape[1]), own.dtype),
            pltpu.VMEM((rows, 2 * rounds * rows), jnp.float32),
            pltpu.VMEM((8, 128), jnp.int32),
            pltpu.VMEM((rows, rows), jnp.float32),
            pltpu.VMEM(queries.shape, queries.dtype),
            pltpu.VMEM((1, own.shape[1]), jnp.int32),
            part,
            part,
        ),
        in_specs=[VMEM, HBM, HBM],
        out_specs=(VMEM,) * 8,
        scratch_shapes=[
            pltpu.SMEM(lengths.shape, jnp.int32),
            pltpu.SemaphoreType.DMA,
            pltpu.SemaphoreType.DMA((KEY_VALUE_HEADS,)),
        ],
        compiler_params=pltpu.CompilerParams(vmem_limit_bytes=10 * 1024 * 1024),
        cost_estimate=pl.CostEstimate(
            flops=4 * 10**9, bytes_accessed=16 * 10**6, transcendentals=rows * queries.size
        ),
    )(*in_vmem(own), *in_hbm(lengths, queries))


def own_rest(own, own_bias, queries, kept):
    rows = queries.shape[0]
    operands = in_vmem(own, own_bias, queries, *kept)
    return pl.pallas_call(
        functools.partial(own_rest_kernel, rows),
        out_shape=tuple(pltpu.VMEM(x.shape, x.dtype) for x in kept),
        in_specs=[VMEM] * len(operands),
        out_specs=(VMEM,) * len(kept),
        input_output_aliases={3 + n: n for n in range(len(kept))},
        compiler_params=pltpu.CompilerParams(vmem_limit_bytes=10 * 1024 * 1024),
        cost_estimate=pl.CostEstimate(
            flops=4 * 10**9, bytes_accessed=16 * 10**6, transcendentals=rows * queries.size
        ),
    )(*operands)


def behind_kernel(
    before, last, rows, needed_ref, bias_ref, q_ref, near_ref, further_ref, level_ref, mean_ref, *refs
):
    beyond = needed_ref[0, 0] - before
    pairs = [(ref.at[:rows], ref.at[rows : 2 * rows]) for ref in (near_ref, further_ref)]
    if last:
        out_hbm, out_ref, out_sems = refs

        def out_copy(n):
            width = HEADS_AT_ONCE * HEAD_SIZE
            at = pl.ds(pl.multiple_of(n * width, width), width)
            return pltpu.make_async_copy(out_ref.at[:, at], out_hbm.at[:, at], out_sems.at[n])

    else:
        _, new_level_ref, new_mean_ref = refs

    def finish(heads, mean):
        spread(out_ref, heads, rows, mean)
        out_copy(lax.div(heads[0], HEADS_AT_ONCE)).start()

    def attend(count):
        def match(heads, g):
            key = jnp.concatenate([key[:, head_columns(g)] for key, _ in pairs[:count]], axis=0)
            bias = bias_ref[:, before * rows : (before + count) * rows]
            return (scores_of(stacked(q_ref, heads), key, bias),)

        def weigh(heads, g, scores):
            level = stacked(level_ref, heads)
            top = jnp.maximum(level, jnp.max(scores, axis=1, keepdims=True))
            fade = jnp.exp2((level - top) * jnp.float32(FACTOR))
            return weights_of(scores, jnp.concatenate([top] * count, axis=1)), fade, top

        def gather(heads, g, weights, fade, top):
            value = jnp.concatenate([value[:, head_columns(g)] for _, value in pairs[:count]], axis=0)
            more = jnp.dot(weights, with_ones(value), preferred_element_type=jnp.float32)
            summed = stacked(mean_ref, heads) * fade + more[:, :HEAD_SIZE]
            total = fade + more[:, HEAD_SIZE:]
            if last:
                finish(heads, normalised(summed, total))
            else:
                spread(new_mean_ref, heads, rows, normalised(summed, total))
                spread(new_level_ref, heads, rows, level_of(top, total))

        in_loop(match, weigh, gather)

    @pl.when(beyond > 1)
    def _():
        attend(2)

    @pl.when(beyond == 1)
    def _():
        attend(1)

    if last:
        @pl.when(beyond < 1)
        def _():
            in_loop(lambda heads, g: finish(heads, stacked(mean_ref, heads)))

        for n in range(len(chains())):
            out_copy(n).wait()


def behind_part(before, last, needed, bias, queries, near, further, parts):
    rows = queries.shape[0]
    area = rows * rows * 2 * QUERY_HEADS
    operands = in_vmem(needed, bias, queries, near, further, *parts)
    if last:
        out_shape = jax.ShapeDtypeStruct(queries.shape, queries.dtype)
        out_specs = HBM
        scratch = [
            pltpu.VMEM(queries.shape, queries.dtype),
            pltpu.SemaphoreType.DMA((len(chains()),)),
        ]
        aliases = {}
    else:
        kept = (further, *parts)
        out_shape = tuple(pltpu.VMEM(part.shape, part.dtype) for part in kept)
        out_specs = (VMEM,) * len(kept)
        scratch = []
        aliases = {4 + n: n for n in range(len(kept))}
    return pl.pallas_call(
        functools.partial(behind_kernel, before, last, rows),
        out_shape=out_shape,
        in_specs=[VMEM] * len(operands),
        out_specs=out_specs,
        scratch_shapes=scratch,
        input_output_aliases=aliases,
        compiler_params=pltpu.CompilerParams(vmem_limit_bytes=10 * 1024 * 1024),
        cost_estimate=pl.CostEstimate(
            flops=4 * area, bytes_accessed=queries.size, transcendentals=0
        ),
    )(*operands)


def per_device(queries, keys, values, lengths):
    count = lax.axis_size("dp") * lax.axis_size("ctx")
    rounds = lax.axis_size("ctx")

    def from_behind(block, r):
        by = 2 * (r + 1)
        return lax.ppermute(block, AXES, [(i, i + by) for i in range(count - by)])

    own = pack(keys, values)
    fetched = [from_behind(own, 0)]
    longer, bias, needed, own_bias, queries, *kept = own_part(lengths, queries, own, rounds)
    fetched += [from_behind(longer, r) for r in range(1, rounds)]
    odd, *parts = own_rest(own, own_bias, queries, kept)
    swap = [(i, i ^ 1) for i in range(count)]
    nearer = own
    size = 2 * keys.shape[0]
    for r, further in enumerate(fetched):
        last = r == rounds - 1
        near = lax.ppermute(jnp.where(odd == 1, further[:size], nearer[:size]), AXES, swap)
        result = behind_part(2 * r, last, needed, bias, queries, near, further, parts)
        if not last:
            nearer, *parts = result
    return result


def solution(mesh):
    in_specs = (P(AXES, None), P(AXES, None), P(AXES, None), P())
    return jax.shard_map(
        per_device, mesh=mesh, in_specs=in_specs, out_specs=P(AXES, None), check_vma=False
    )
```

```python
import functools
import math

import jax
import jax.numpy as jnp
from jax import lax
from jax.experimental import pallas as pl
from jax.experimental.pallas import tpu as pltpu
from jax.sharding import PartitionSpec as P

HEAD_SIZE = 128
QUERY_HEADS = 32
KEY_VALUE_HEADS = 4
GROUP = QUERY_HEADS // KEY_VALUE_HEADS
HEADS_AT_ONCE = 2
EARLY_CHAINS = 8
EXCLUDED = -1e30
PAD = 16
AXES = ("dp", "ctx")


FACTOR = math.log2(math.e) / math.sqrt(HEAD_SIZE)


def head_columns(i):
    return slice(i * HEAD_SIZE, (i + 1) * HEAD_SIZE)


def stacked(ref, heads):
    return jnp.concatenate([ref[:, head_columns(i)] for i in heads], axis=0)


def spread(ref, heads, rows, value):
    for n, i in enumerate(heads):
        ref[:, head_columns(i)] = value[n * rows : (n + 1) * rows].astype(ref.dtype)


def with_ones(value):
    return jnp.concatenate([value, jnp.ones(value.shape, value.dtype)], axis=1)


def scores_of(q, key, bias):
    scores = lax.dot_general(
        q, key, (((1,), (1,)), ((), ())), preferred_element_type=jnp.float32
    )
    return scores + jnp.concatenate([bias] * (q.shape[0] // bias.shape[0]), axis=0)


def weights_of(scores, top):
    return jnp.exp2((scores - top) * jnp.float32(FACTOR)).astype(jnp.bfloat16)


def normalised(summed, total):
    inverse = pl.reciprocal(total, approx=True)
    return summed * (inverse * (2.0 - total * inverse))


def level_of(top, total):
    return top + jnp.log(total) * jnp.float32(math.sqrt(HEAD_SIZE))


def chains():
    return [
        (range(h, h + HEADS_AT_ONCE), h // GROUP) for h in range(0, QUERY_HEADS, HEADS_AT_ONCE)
    ]


def in_turn(runs, *stages):
    results = {}
    for turn in range(len(runs) + len(stages) - 1):
        for n, stage in enumerate(stages):
            i = turn - n
            if 0 <= i < len(runs):
                results[i] = stage(*runs[i], *results.pop(i, ()))


def pack_kernel(key_hbm, value_hbm, out_ref, sems):
    rows = key_hbm.shape[0]
    copies = [
        pltpu.make_async_copy(key_hbm, out_ref.at[:rows], sems.at[0]),
        pltpu.make_async_copy(value_hbm, out_ref.at[rows:], sems.at[1]),
    ]
    for copy in copies:
        copy.start()
    for copy in copies:
        copy.wait()


def pack(keys, values):
    rows, width = keys.shape
    return pl.pallas_call(
        pack_kernel,
        out_shape=pltpu.VMEM((2 * rows, width), keys.dtype),
        in_specs=[HBM, HBM],
        out_specs=VMEM,
        scratch_shapes=[pltpu.SemaphoreType.DMA((2,))],
        compiler_params=pltpu.CompilerParams(vmem_limit_bytes=1024 * 1024),
    )(*in_hbm(keys, values))


def attend_own(runs, rows, own_ref, own_bias_ref, q_ref, level_ref, mean_ref, ready):
    def match(heads, g):
        ready(heads, g)
        key = own_ref[:rows, head_columns(g)]
        return (scores_of(stacked(q_ref, heads), key, own_bias_ref[...]),)

    def crest(heads, g, scores):
        return scores, jnp.max(scores, axis=1, keepdims=True)

    def weigh(heads, g, scores, top):
        return weights_of(scores, top), jnp.broadcast_to(top, scores.shape)

    def gather(heads, g, weights, top):
        value = with_ones(own_ref[rows:, head_columns(g)])
        return jnp.dot(weights, value, preferred_element_type=jnp.float32), top

    def settle(heads, g, more, top):
        summed, total = more[:, :HEAD_SIZE], more[:, HEAD_SIZE:]
        spread(mean_ref, heads, rows, normalised(summed, total))
        spread(level_ref, heads, rows, level_of(top, total))

    in_turn(runs, match, crest, weigh, gather, settle)


def own_kernel(
    rounds, rows, own_ref, lengths_hbm, q_hbm,
    longer_ref, bias_ref, needed_ref, own_bias_ref, q_ref, odd_ref, level_ref, mean_ref,
    lengths_ref, lengths_sem, q_sems,
):
    lengths_copy = pltpu.make_async_copy(lengths_hbm, lengths_ref, lengths_sem)
    lengths_copy.start()
    width = GROUP * HEAD_SIZE
    q_copies = []
    for g in range(KEY_VALUE_HEADS):
        at = slice(g * width, (g + 1) * width)
        q_copies.append(pltpu.make_async_copy(q_hbm.at[:, at], q_ref.at[:, at], q_sems.at[g]))
        q_copies[g].start()
    me = lax.axis_index("dp") * lax.axis_size("ctx") + lax.axis_index("ctx")
    longer_ref[: 2 * rows, :] = own_ref[...]
    longer_ref[2 * rows :, :] = jnp.zeros((PAD, longer_ref.shape[1]), longer_ref.dtype)
    odd_ref[...] = jnp.full(odd_ref.shape, lax.rem(me, 2), jnp.int32)
    first = me * rows
    query_pos = first + lax.broadcasted_iota(jnp.int32, (rows, rows), 0)
    lengths_copy.wait()

    def later(doc, carried):
        bound, start, first_start = carried
        start = jnp.where(query_pos >= bound, bound, start)
        first_start = jnp.where(first >= bound, bound, first_start)
        return bound + lengths_ref[doc], start, first_start

    zero = jnp.int32(0)
    _, start, first_start = lax.fori_loop(
        0,
        lengths_ref.shape[0],
        later,
        (zero, jnp.zeros((rows, rows), jnp.int32), zero),
        unroll=8,
    )
    needed = lax.div(first - first_start + (rows - 1), jnp.int32(rows))
    needed_ref[...] = jnp.full(needed_ref.shape, needed, jnp.int32)
    lane = lax.broadcasted_iota(jnp.int32, (rows, rows), 1)

    def bias_of(allowed):
        return jnp.where(allowed, jnp.float32(0.0), jnp.float32(EXCLUDED))

    key_pos = first + lane
    own_bias_ref[...] = bias_of((key_pos >= start) & (key_pos <= query_pos))
    for b in range(2 * rounds):
        key_pos = first - (b + 1) * rows + lane
        bias_ref[:, b * rows : (b + 1) * rows] = bias_of(key_pos >= start)

    def ready(heads, g):
        if heads[0] % GROUP == 0:
            q_copies[g].wait()

    runs = chains()[:EARLY_CHAINS]
    attend_own(runs, rows, own_ref, own_bias_ref, q_ref, level_ref, mean_ref, ready)
    for copy in q_copies[runs[-1][1] + 1 :]:
        copy.wait()


def own_rest_kernel(
    rows, own_ref, own_bias_ref, q_ref, odd_ref, *parts
):
    runs = chains()[EARLY_CHAINS:]
    parts = parts[3:]
    attend_own(runs, rows, own_ref, own_bias_ref, q_ref, *parts, lambda heads, g: None)


def in_vmem(*operands):
    return [pltpu.with_memory_space_constraint(x, pltpu.VMEM) for x in operands]


def in_hbm(*operands):
    return [pltpu.with_memory_space_constraint(x, pltpu.HBM) for x in operands]


SMEM = pl.BlockSpec(memory_space=pltpu.SMEM)
VMEM = pl.BlockSpec(memory_space=pltpu.VMEM)
HBM = pl.BlockSpec(memory_space=pltpu.HBM)


def own_part(lengths, queries, own, rounds):
    rows = queries.shape[0]
    part = pltpu.VMEM(queries.shape, jnp.float32)
    return pl.pallas_call(
        functools.partial(own_kernel, rounds, rows),
        out_shape=(
            pltpu.VMEM((2 * rows + PAD, own.shape[1]), own.dtype),
            pltpu.VMEM((rows, 2 * rounds * rows), jnp.float32),
            pltpu.VMEM((8, 128), jnp.int32),
            pltpu.VMEM((rows, rows), jnp.float32),
            pltpu.VMEM(queries.shape, queries.dtype),
            pltpu.VMEM((1, own.shape[1]), jnp.int32),
            part,
            part,
        ),
        in_specs=[VMEM, HBM, HBM],
        out_specs=(VMEM,) * 8,
        scratch_shapes=[
            pltpu.SMEM(lengths.shape, jnp.int32),
            pltpu.SemaphoreType.DMA,
            pltpu.SemaphoreType.DMA((KEY_VALUE_HEADS,)),
        ],
        compiler_params=pltpu.CompilerParams(vmem_limit_bytes=10 * 1024 * 1024),
        cost_estimate=pl.CostEstimate(
            flops=4 * 10**9, bytes_accessed=16 * 10**6, transcendentals=rows * queries.size
        ),
    )(*in_vmem(own), *in_hbm(lengths, queries))


def own_rest(own, own_bias, queries, kept):
    rows = queries.shape[0]
    operands = in_vmem(own, own_bias, queries, *kept)
    return pl.pallas_call(
        functools.partial(own_rest_kernel, rows),
        out_shape=tuple(pltpu.VMEM(x.shape, x.dtype) for x in kept),
        in_specs=[VMEM] * len(operands),
        out_specs=(VMEM,) * len(kept),
        input_output_aliases={3 + n: n for n in range(len(kept))},
        compiler_params=pltpu.CompilerParams(vmem_limit_bytes=10 * 1024 * 1024),
        cost_estimate=pl.CostEstimate(
            flops=4 * 10**9, bytes_accessed=16 * 10**6, transcendentals=rows * queries.size
        ),
    )(*operands)


def behind_kernel(
    before, last, rows, needed_ref, bias_ref, q_ref, near_ref, further_ref, level_ref, mean_ref, *refs
):
    beyond = needed_ref[0, 0] - before
    pairs = [(ref.at[:rows], ref.at[rows : 2 * rows]) for ref in (near_ref, further_ref)]
    if last:
        out_hbm, out_ref, out_sems = refs

        def out_copy(n):
            width = HEADS_AT_ONCE * HEAD_SIZE
            at = slice(n * width, (n + 1) * width)
            return pltpu.make_async_copy(out_ref.at[:, at], out_hbm.at[:, at], out_sems.at[n])

    else:
        _, new_level_ref, new_mean_ref = refs

    def finish(heads, mean):
        spread(out_ref, heads, rows, mean)
        out_copy(heads[0] // HEADS_AT_ONCE).start()

    def attend(count):
        def match(heads, g):
            key = jnp.concatenate([key[:, head_columns(g)] for key, _ in pairs[:count]], axis=0)
            bias = bias_ref[:, before * rows : (before + count) * rows]
            return (scores_of(stacked(q_ref, heads), key, bias),)

        def crest(heads, g, scores):
            level = stacked(level_ref, heads)
            top = jnp.maximum(level, jnp.max(scores, axis=1, keepdims=True))
            return scores, top, jnp.exp2((level - top) * jnp.float32(FACTOR))

        def weigh(heads, g, scores, top, fade):
            return weights_of(scores, jnp.concatenate([top] * count, axis=1)), top, fade

        def gather(heads, g, weights, top, fade):
            value = jnp.concatenate([value[:, head_columns(g)] for _, value in pairs[:count]], axis=0)
            return jnp.dot(weights, with_ones(value), preferred_element_type=jnp.float32), top, fade

        def settle(heads, g, more, top, fade):
            summed = stacked(mean_ref, heads) * fade + more[:, :HEAD_SIZE]
            total = fade + more[:, HEAD_SIZE:]
            if last:
                finish(heads, normalised(summed, total))
            else:
                spread(new_mean_ref, heads, rows, normalised(summed, total))
                spread(new_level_ref, heads, rows, level_of(top, total))

        in_turn(chains(), match, crest, weigh, gather, settle)

    @pl.when(beyond > 1)
    def _():
        attend(2)

    @pl.when(beyond == 1)
    def _():
        attend(1)

    if last:
        @pl.when(beyond < 1)
        def _():
            in_turn(
                chains(),
                lambda heads, g: finish(heads, stacked(mean_ref, heads)),
            )

        for n in range(len(chains())):
            out_copy(n).wait()


def behind_part(before, last, needed, bias, queries, near, further, parts):
    rows = queries.shape[0]
    area = rows * rows * 2 * QUERY_HEADS
    operands = in_vmem(needed, bias, queries, near, further, *parts)
    if last:
        out_shape = jax.ShapeDtypeStruct(queries.shape, queries.dtype)
        out_specs = HBM
        scratch = [
            pltpu.VMEM(queries.shape, queries.dtype),
            pltpu.SemaphoreType.DMA((len(chains()),)),
        ]
        aliases = {}
    else:
        kept = (further, *parts)
        out_shape = tuple(pltpu.VMEM(part.shape, part.dtype) for part in kept)
        out_specs = (VMEM,) * len(kept)
        scratch = []
        aliases = {4 + n: n for n in range(len(kept))}
    return pl.pallas_call(
        functools.partial(behind_kernel, before, last, rows),
        out_shape=out_shape,
        in_specs=[VMEM] * len(operands),
        out_specs=out_specs,
        scratch_shapes=scratch,
        input_output_aliases=aliases,
        compiler_params=pltpu.CompilerParams(vmem_limit_bytes=10 * 1024 * 1024),
        cost_estimate=pl.CostEstimate(
            flops=4 * area, bytes_accessed=queries.size, transcendentals=0
        ),
    )(*operands)


def per_device(queries, keys, values, lengths):
    count = lax.axis_size("dp") * lax.axis_size("ctx")
    rounds = lax.axis_size("ctx")

    def from_behind(block, r):
        by = 2 * (r + 1)
        return lax.ppermute(block, AXES, [(i, i + by) for i in range(count - by)])

    own = pack(keys, values)
    fetched = [from_behind(own, 0)]
    longer, bias, needed, own_bias, queries, *kept = own_part(lengths, queries, own, rounds)
    fetched += [from_behind(longer, r) for r in range(1, rounds)]
    odd, *parts = own_rest(own, own_bias, queries, kept)
    swap = [(i, i ^ 1) for i in range(count)]
    nearer = own
    size = 2 * keys.shape[0]
    for r, further in enumerate(fetched):
        last = r == rounds - 1
        near = lax.ppermute(jnp.where(odd == 1, further[:size], nearer[:size]), AXES, swap)
        result = behind_part(2 * r, last, needed, bias, queries, near, further, parts)
        if not last:
            nearer, *parts = result
    return result


def solution(mesh):
    in_specs = (P(AXES, None), P(AXES, None), P(AXES, None), P())
    return jax.shard_map(
        per_device, mesh=mesh, in_specs=in_specs, out_specs=P(AXES, None), check_vma=False
    )
```

```python
import functools
import math

import jax
import jax.numpy as jnp
from jax import lax
from jax.experimental import pallas as pl
from jax.experimental.pallas import tpu as pltpu
from jax.sharding import PartitionSpec as P

HEAD_SIZE = 128
QUERY_HEADS = 32
KEY_VALUE_HEADS = 4
GROUP = QUERY_HEADS // KEY_VALUE_HEADS
HEADS_AT_ONCE = 4
EARLY_CHAINS = 4
EXCLUDED = -1e30
PAD = 16
AXES = ("dp", "ctx")


FACTOR = math.log2(math.e) / math.sqrt(HEAD_SIZE)


def head_columns(i):
    return slice(i * HEAD_SIZE, (i + 1) * HEAD_SIZE)


def stacked(ref, heads, rows):
    return jnp.concatenate([ref[:rows, head_columns(i)] for i in heads], axis=0)


def spread(ref, heads, rows, value):
    for n, i in enumerate(heads):
        ref[:rows, head_columns(i)] = value[n * rows : (n + 1) * rows].astype(ref.dtype)


def with_ones(value):
    return jnp.concatenate([value, jnp.ones(value.shape, value.dtype)], axis=1)


def scores_of(q, key, bias):
    scores = lax.dot_general(
        q, key, (((1,), (1,)), ((), ())), preferred_element_type=jnp.float32
    )
    return scores + jnp.concatenate([bias] * (q.shape[0] // bias.shape[0]), axis=0)


def weights_of(scores, top):
    return jnp.exp2((scores - top) * jnp.float32(FACTOR)).astype(jnp.bfloat16)


def normalised(summed, total):
    inverse = pl.reciprocal(total, approx=True)
    return summed * (inverse * (2.0 - total * inverse))


def level_of(top, total):
    return top + jnp.log(total) * jnp.float32(math.sqrt(HEAD_SIZE))


def chains(size=HEADS_AT_ONCE):
    return [(range(h, h + size), h // GROUP) for h in range(0, QUERY_HEADS, size)]


def in_turn(runs, *stages):
    results = {}
    for turn in range(len(runs) + len(stages) - 1):
        for n, stage in enumerate(stages):
            i = turn - n
            if 0 <= i < len(runs):
                results[i] = stage(*runs[i], *results.pop(i, ()))


def pack_kernel(key_hbm, value_hbm, out_ref, sems):
    rows = key_hbm.shape[0]
    copies = [
        pltpu.make_async_copy(key_hbm, out_ref.at[:rows], sems.at[0]),
        pltpu.make_async_copy(value_hbm, out_ref.at[rows:], sems.at[1]),
    ]
    for copy in copies:
        copy.start()
    for copy in copies:
        copy.wait()


def pack(keys, values):
    rows, width = keys.shape
    return pl.pallas_call(
        pack_kernel,
        out_shape=pltpu.VMEM((2 * rows, width), keys.dtype),
        in_specs=[HBM, HBM],
        out_specs=VMEM,
        scratch_shapes=[pltpu.SemaphoreType.DMA((2,))],
        compiler_params=pltpu.CompilerParams(vmem_limit_bytes=1024 * 1024),
    )(*in_hbm(keys, values))


def attend_own(runs, rows, own_ref, own_bias_ref, q_ref, level_ref, mean_ref, ready):
    def match(heads, g):
        ready(heads, g)
        key = own_ref[:rows, head_columns(g)]
        return (scores_of(stacked(q_ref, heads, rows), key, own_bias_ref[...]),)

    def weigh(heads, g, scores):
        top = jnp.max(scores, axis=1, keepdims=True)
        return weights_of(scores, top), jnp.broadcast_to(top, scores.shape)

    def gather(heads, g, weights, top):
        value = with_ones(own_ref[rows:, head_columns(g)])
        more = jnp.dot(weights, value, preferred_element_type=jnp.float32)
        summed, total = more[:, :HEAD_SIZE], more[:, HEAD_SIZE:]
        spread(mean_ref, heads, rows, normalised(summed, total))
        spread(level_ref, heads, rows, level_of(top, total))

    in_turn(runs, match, weigh, gather)


def own_kernel(
    rounds, rows, own_ref, lengths_hbm, q_hbm,
    longer_ref, bias_ref, needed_ref, own_bias_ref, q_ref, odd_ref, level_ref, mean_ref,
    lengths_ref, lengths_sem, q_sems,
):
    lengths_copy = pltpu.make_async_copy(lengths_hbm, lengths_ref, lengths_sem)
    lengths_copy.start()
    width = GROUP * HEAD_SIZE
    q_copies = []
    for g in range(KEY_VALUE_HEADS):
        at = slice(g * width, (g + 1) * width)
        q_copies.append(pltpu.make_async_copy(q_hbm.at[:, at], q_ref.at[:, at], q_sems.at[g]))
        q_copies[g].start()
    me = lax.axis_index("dp") * lax.axis_size("ctx") + lax.axis_index("ctx")
    longer_ref[: 2 * rows, :] = own_ref[...]
    longer_ref[2 * rows :, :] = jnp.zeros((PAD, longer_ref.shape[1]), longer_ref.dtype)
    odd_ref[...] = jnp.full(odd_ref.shape, lax.rem(me, 2), jnp.int32)
    first = me * rows
    query_pos = first + lax.broadcasted_iota(jnp.int32, (rows, rows), 0)
    lengths_copy.wait()

    def later(doc, carried):
        bound, start, first_start, first_end = carried
        following = bound + lengths_ref[doc]
        start = jnp.where(query_pos >= bound, bound, start)
        first_start = jnp.where(first >= bound, bound, first_start)
        first_end = jnp.where(first >= bound, following, first_end)
        return following, start, first_start, first_end

    zero = jnp.int32(0)
    _, start, first_start, first_end = lax.fori_loop(
        0,
        lengths_ref.shape[0],
        later,
        (zero, jnp.zeros((rows, rows), jnp.int32), zero, zero),
        unroll=8,
    )
    needed = lax.div(first - first_start + (rows - 1), jnp.int32(rows))
    needed_ref[:4, :] = jnp.full((4, needed_ref.shape[1]), needed, jnp.int32)
    needed_ref[4:, :] = jnp.full((4, needed_ref.shape[1]), first_end - first, jnp.int32)
    lane = lax.broadcasted_iota(jnp.int32, (rows, rows), 1)

    def bias_of(allowed):
        return jnp.where(allowed, jnp.float32(0.0), jnp.float32(EXCLUDED))

    key_pos = first + lane
    own_bias_ref[...] = bias_of((key_pos >= start) & (key_pos <= query_pos))
    for b in range(2 * rounds):
        key_pos = first - (b + 1) * rows + lane
        bias_ref[:, b * rows : (b + 1) * rows] = bias_of(key_pos >= start)

    def ready(heads, g):
        if heads[0] % GROUP == 0:
            q_copies[g].wait()

    runs = chains()[:EARLY_CHAINS]
    attend_own(runs, rows, own_ref, own_bias_ref, q_ref, level_ref, mean_ref, ready)
    for copy in q_copies[runs[-1][1] + 1 :]:
        copy.wait()


def own_rest_kernel(
    rows, own_ref, own_bias_ref, q_ref, odd_ref, *parts
):
    runs = chains()[EARLY_CHAINS:]
    parts = parts[3:]
    attend_own(runs, rows, own_ref, own_bias_ref, q_ref, *parts, lambda heads, g: None)


def in_vmem(*operands):
    return [pltpu.with_memory_space_constraint(x, pltpu.VMEM) for x in operands]


def in_hbm(*operands):
    return [pltpu.with_memory_space_constraint(x, pltpu.HBM) for x in operands]


SMEM = pl.BlockSpec(memory_space=pltpu.SMEM)
VMEM = pl.BlockSpec(memory_space=pltpu.VMEM)
HBM = pl.BlockSpec(memory_space=pltpu.HBM)


def own_part(lengths, queries, own, rounds):
    rows = queries.shape[0]
    part = pltpu.VMEM(queries.shape, jnp.float32)
    return pl.pallas_call(
        functools.partial(own_kernel, rounds, rows),
        out_shape=(
            pltpu.VMEM((2 * rows + PAD, own.shape[1]), own.dtype),
            pltpu.VMEM((rows, 2 * rounds * rows), jnp.float32),
            pltpu.VMEM((8, 128), jnp.int32),
            pltpu.VMEM((rows, rows), jnp.float32),
            pltpu.VMEM(queries.shape, queries.dtype),
            pltpu.VMEM((1, own.shape[1]), jnp.int32),
            part,
            part,
        ),
        in_specs=[VMEM, HBM, HBM],
        out_specs=(VMEM,) * 8,
        scratch_shapes=[
            pltpu.SMEM(lengths.shape, jnp.int32),
            pltpu.SemaphoreType.DMA,
            pltpu.SemaphoreType.DMA((KEY_VALUE_HEADS,)),
        ],
        compiler_params=pltpu.CompilerParams(vmem_limit_bytes=10 * 1024 * 1024),
        cost_estimate=pl.CostEstimate(
            flops=4 * 10**9, bytes_accessed=16 * 10**6, transcendentals=rows * queries.size
        ),
    )(*in_vmem(own), *in_hbm(lengths, queries))


def own_rest(own, own_bias, queries, kept):
    rows = queries.shape[0]
    operands = in_vmem(own, own_bias, queries, *kept)
    return pl.pallas_call(
        functools.partial(own_rest_kernel, rows),
        out_shape=tuple(pltpu.VMEM(x.shape, x.dtype) for x in kept),
        in_specs=[VMEM] * len(operands),
        out_specs=(VMEM,) * len(kept),
        input_output_aliases={3 + n: n for n in range(len(kept))},
        compiler_params=pltpu.CompilerParams(vmem_limit_bytes=10 * 1024 * 1024),
        cost_estimate=pl.CostEstimate(
            flops=4 * 10**9, bytes_accessed=16 * 10**6, transcendentals=rows * queries.size
        ),
    )(*operands)


def behind_kernel(
    before, last, rows, needed_ref, bias_ref, q_ref, near_ref, further_ref, level_ref, mean_ref, *refs
):
    beyond = needed_ref[0, 0] - before
    crossing = needed_ref[4, 0]
    pairs = [(ref.at[:rows], ref.at[rows : 2 * rows]) for ref in (near_ref, further_ref)]
    if last:
        out_hbm, out_ref, out_sems = refs

        def out_copy(n):
            width = HEADS_AT_ONCE * HEAD_SIZE
            at = slice(n * width, (n + 1) * width)
            return pltpu.make_async_copy(out_ref.at[:, at], out_hbm.at[:, at], out_sems.at[n])

    else:
        _, new_level_ref, new_mean_ref = refs

    def finish(heads, upto, mean):
        if upto:
            spread(out_ref, heads, upto, mean)
        if upto < rows:
            at = slice(heads[0] * HEAD_SIZE, (heads[-1] + 1) * HEAD_SIZE)
            out_ref[upto:, at] = mean_ref[upto:, at].astype(out_ref.dtype)
        for i in heads[::HEADS_AT_ONCE]:
            out_copy(i // HEADS_AT_ONCE).start()

    def attend(count, upto):
        def match(heads, g):
            key = jnp.concatenate([key[:, head_columns(g)] for key, _ in pairs[:count]], axis=0)
            bias = bias_ref[:upto, before * rows : (before + count) * rows]
            return (scores_of(stacked(q_ref, heads, upto), key, bias),)

        def weigh(heads, g, scores):
            level = stacked(level_ref, heads, upto)
            top = jnp.maximum(level, jnp.max(scores, axis=1, keepdims=True))
            fade = jnp.exp2((level - top) * jnp.float32(FACTOR))
            return weights_of(scores, jnp.concatenate([top] * count, axis=1)), fade, top

        def gather(heads, g, weights, fade, top):
            value = jnp.concatenate([value[:, head_columns(g)] for _, value in pairs[:count]], axis=0)
            more = jnp.dot(weights, with_ones(value), preferred_element_type=jnp.float32)
            summed = stacked(mean_ref, heads, upto) * fade + more[:, :HEAD_SIZE]
            total = fade + more[:, HEAD_SIZE:]
            if last:
                finish(heads, upto, normalised(summed, total))
            else:
                spread(new_mean_ref, heads, upto, normalised(summed, total))
                spread(new_level_ref, heads, upto, level_of(top, total))

        runs = chains() if upto == rows else chains(GROUP)
        in_turn(runs, match, weigh, gather)

    sizes = [0, rows // 4, rows // 2, rows]
    for count, enough in ((2, beyond > 1), (1, beyond == 1)):
        for low, upto in zip(sizes, sizes[1:]):
            fits = crossing > low if upto == rows else (crossing > low) & (crossing <= upto)
            pl.when(enough & fits)(functools.partial(attend, count, upto))

    if last:
        @pl.when(beyond < 1)
        def _():
            in_turn(chains(), lambda heads, g: finish(heads, 0, None))

        for n in range(len(chains())):
            out_copy(n).wait()


def behind_part(before, last, needed, bias, queries, near, further, parts):
    rows = queries.shape[0]
    area = rows * rows * 2 * QUERY_HEADS
    operands = in_vmem(needed, bias, queries, near, further, *parts)
    if last:
        out_shape = jax.ShapeDtypeStruct(queries.shape, queries.dtype)
        out_specs = HBM
        scratch = [
            pltpu.VMEM(queries.shape, queries.dtype),
            pltpu.SemaphoreType.DMA((len(chains()),)),
        ]
        aliases = {}
    else:
        kept = (further, *parts)
        out_shape = tuple(pltpu.VMEM(part.shape, part.dtype) for part in kept)
        out_specs = (VMEM,) * len(kept)
        scratch = []
        aliases = {4 + n: n for n in range(len(kept))}
    return pl.pallas_call(
        functools.partial(behind_kernel, before, last, rows),
        out_shape=out_shape,
        in_specs=[VMEM] * len(operands),
        out_specs=out_specs,
        scratch_shapes=scratch,
        input_output_aliases=aliases,
        compiler_params=pltpu.CompilerParams(vmem_limit_bytes=10 * 1024 * 1024),
        cost_estimate=pl.CostEstimate(
            flops=4 * area, bytes_accessed=queries.size, transcendentals=0
        ),
    )(*operands)


def per_device(queries, keys, values, lengths):
    count = lax.axis_size("dp") * lax.axis_size("ctx")
    rounds = lax.axis_size("ctx")

    def from_behind(block, r):
        by = 2 * (r + 1)
        return lax.ppermute(block, AXES, [(i, i + by) for i in range(count - by)])

    own = pack(keys, values)
    fetched = [from_behind(own, 0)]
    longer, bias, needed, own_bias, queries, *kept = own_part(lengths, queries, own, rounds)
    fetched += [from_behind(longer, r) for r in range(1, rounds)]
    odd, *parts = own_rest(own, own_bias, queries, kept)
    swap = [(i, i ^ 1) for i in range(count)]
    nearer = own
    size = 2 * keys.shape[0]
    for r, further in enumerate(fetched):
        last = r == rounds - 1
        near = lax.ppermute(jnp.where(odd == 1, further[:size], nearer[:size]), AXES, swap)
        result = behind_part(2 * r, last, needed, bias, queries, near, further, parts)
        if not last:
            nearer, *parts = result
    return result


def solution(mesh):
    in_specs = (P(AXES, None), P(AXES, None), P(AXES, None), P())
    return jax.shard_map(
        per_device, mesh=mesh, in_specs=in_specs, out_specs=P(AXES, None), check_vma=False
    )
```

```python
import functools
import math

import jax
import jax.numpy as jnp
from jax import lax
from jax.experimental import pallas as pl
from jax.experimental.pallas import tpu as pltpu
from jax.sharding import PartitionSpec as P

HEAD_SIZE = 128
QUERY_HEADS = 32
KEY_VALUE_HEADS = 4
GROUP = QUERY_HEADS // KEY_VALUE_HEADS
HEADS_AT_ONCE = 4
EARLY_CHAINS = 4
EXCLUDED = -1e30
PAD = 16
AXES = ("dp", "ctx")


FACTOR = math.log2(math.e) / math.sqrt(HEAD_SIZE)


def head_columns(i):
    return slice(i * HEAD_SIZE, (i + 1) * HEAD_SIZE)


def stacked(ref, heads, rows):
    return jnp.concatenate([ref[:rows, head_columns(i)] for i in heads], axis=0)


def spread(ref, heads, rows, value):
    for n, i in enumerate(heads):
        ref[:rows, head_columns(i)] = value[n * rows : (n + 1) * rows].astype(ref.dtype)


def with_ones(value):
    return jnp.concatenate([value, jnp.ones(value.shape, value.dtype)], axis=1)


def scores_of(q, key, bias):
    scores = lax.dot_general(
        q, key, (((1,), (1,)), ((), ())), preferred_element_type=jnp.float32
    )
    return scores + jnp.concatenate([bias] * (q.shape[0] // bias.shape[0]), axis=0)


def weights_of(scores, top):
    return jnp.exp2((scores - top) * jnp.float32(FACTOR)).astype(jnp.bfloat16)


def normalised(summed, total):
    inverse = pl.reciprocal(total, approx=True)
    return summed * (inverse * (2.0 - total * inverse))


def level_of(top, total):
    return top + jnp.log(total) * jnp.float32(math.sqrt(HEAD_SIZE))


def chains(size=HEADS_AT_ONCE):
    return [(range(h, h + size), h // GROUP) for h in range(0, QUERY_HEADS, size)]


def in_turn(runs, *stages):
    results = {}
    for turn in range(len(runs) + len(stages) - 1):
        for n, stage in enumerate(stages):
            i = turn - n
            if 0 <= i < len(runs):
                results[i] = stage(*runs[i], *results.pop(i, ()))


def pack_kernel(key_hbm, value_hbm, out_ref, sems):
    rows = key_hbm.shape[0]
    copies = [
        pltpu.make_async_copy(key_hbm, out_ref.at[:rows], sems.at[0]),
        pltpu.make_async_copy(value_hbm, out_ref.at[rows:], sems.at[1]),
    ]
    for copy in copies:
        copy.start()
    for copy in copies:
        copy.wait()


def pack(keys, values):
    rows, width = keys.shape
    return pl.pallas_call(
        pack_kernel,
        out_shape=pltpu.VMEM((2 * rows, width), keys.dtype),
        in_specs=[HBM, HBM],
        out_specs=VMEM,
        scratch_shapes=[pltpu.SemaphoreType.DMA((2,))],
        compiler_params=pltpu.CompilerParams(vmem_limit_bytes=1024 * 1024),
    )(*in_hbm(keys, values))


def attend_own(runs, rows, own_ref, own_bias_ref, q_ref, level_ref, mean_ref, ready):
    def match(heads, g):
        ready(heads, g)
        key = own_ref[:rows, head_columns(g)]
        return (scores_of(stacked(q_ref, heads, rows), key, own_bias_ref[...]),)

    def weigh(heads, g, scores):
        top = jnp.max(scores, axis=1, keepdims=True)
        return weights_of(scores, top), jnp.broadcast_to(top, scores.shape)

    def gather(heads, g, weights, top):
        value = with_ones(own_ref[rows:, head_columns(g)])
        more = jnp.dot(weights, value, preferred_element_type=jnp.float32)
        summed, total = more[:, :HEAD_SIZE], more[:, HEAD_SIZE:]
        spread(mean_ref, heads, rows, normalised(summed, total))
        spread(level_ref, heads, rows, level_of(top, total))

    in_turn(runs, match, weigh, gather)


def own_kernel(
    rounds, rows, own_ref, lengths_hbm, q_hbm,
    longer_ref, bias_ref, needed_ref, own_bias_ref, q_ref, odd_ref, level_ref, mean_ref,
    lengths_ref, lengths_sem, q_sems,
):
    lengths_copy = pltpu.make_async_copy(lengths_hbm, lengths_ref, lengths_sem)
    lengths_copy.start()
    width = GROUP * HEAD_SIZE
    q_copies = []
    for g in range(KEY_VALUE_HEADS):
        at = slice(g * width, (g + 1) * width)
        q_copies.append(pltpu.make_async_copy(q_hbm.at[:, at], q_ref.at[:, at], q_sems.at[g]))
        q_copies[g].start()
    me = lax.axis_index("dp") * lax.axis_size("ctx") + lax.axis_index("ctx")
    longer_ref[: 2 * rows, :] = own_ref[...]
    longer_ref[2 * rows :, :] = jnp.zeros((PAD, longer_ref.shape[1]), longer_ref.dtype)
    odd_ref[...] = jnp.full(odd_ref.shape, lax.rem(me, 2), jnp.int32)
    first = me * rows
    query_pos = first + lax.broadcasted_iota(jnp.int32, (rows, rows), 0)
    lengths_copy.wait()

    def later(doc, carried):
        bound, start, first_start, first_end = carried
        following = bound + lengths_ref[doc]
        start = jnp.where(query_pos >= bound, bound, start)
        first_start = jnp.where(first >= bound, bound, first_start)
        first_end = jnp.where(first >= bound, following, first_end)
        return following, start, first_start, first_end

    zero = jnp.int32(0)
    _, start, first_start, first_end = lax.fori_loop(
        0,
        lengths_ref.shape[0],
        later,
        (zero, jnp.zeros((rows, rows), jnp.int32), zero, zero),
        unroll=8,
    )
    needed = lax.div(first - first_start + (rows - 1), jnp.int32(rows))
    needed_ref[:4, :] = jnp.full((4, needed_ref.shape[1]), needed, jnp.int32)
    needed_ref[4:, :] = jnp.full((4, needed_ref.shape[1]), first_end - first, jnp.int32)
    lane = lax.broadcasted_iota(jnp.int32, (rows, rows), 1)

    def bias_of(allowed):
        return jnp.where(allowed, jnp.float32(0.0), jnp.float32(EXCLUDED))

    key_pos = first + lane
    own_bias_ref[...] = bias_of((key_pos >= start) & (key_pos <= query_pos))
    for b in range(2 * rounds):
        key_pos = first - (b + 1) * rows + lane
        bias_ref[:, b * rows : (b + 1) * rows] = bias_of(key_pos >= start)

    def ready(heads, g):
        if heads[0] % GROUP == 0:
            q_copies[g].wait()

    runs = chains()[:EARLY_CHAINS]
    attend_own(runs, rows, own_ref, own_bias_ref, q_ref, level_ref, mean_ref, ready)
    for copy in q_copies[runs[-1][1] + 1 :]:
        copy.wait()


def own_rest_kernel(
    rows, own_ref, own_bias_ref, q_ref, odd_ref, *parts
):
    runs = chains()[EARLY_CHAINS:]
    parts = parts[3:]
    attend_own(runs, rows, own_ref, own_bias_ref, q_ref, *parts, lambda heads, g: None)


def in_vmem(*operands):
    return [pltpu.with_memory_space_constraint(x, pltpu.VMEM) for x in operands]


def in_hbm(*operands):
    return [pltpu.with_memory_space_constraint(x, pltpu.HBM) for x in operands]


SMEM = pl.BlockSpec(memory_space=pltpu.SMEM)
VMEM = pl.BlockSpec(memory_space=pltpu.VMEM)
HBM = pl.BlockSpec(memory_space=pltpu.HBM)


def own_part(lengths, queries, own, rounds):
    rows = queries.shape[0]
    part = pltpu.VMEM(queries.shape, jnp.float32)
    return pl.pallas_call(
        functools.partial(own_kernel, rounds, rows),
        out_shape=(
            pltpu.VMEM((2 * rows + PAD, own.shape[1]), own.dtype),
            pltpu.VMEM((rows, 2 * rounds * rows), jnp.float32),
            pltpu.VMEM((8, 128), jnp.int32),
            pltpu.VMEM((rows, rows), jnp.float32),
            pltpu.VMEM(queries.shape, queries.dtype),
            pltpu.VMEM((1, own.shape[1]), jnp.int32),
            part,
            part,
        ),
        in_specs=[VMEM, HBM, HBM],
        out_specs=(VMEM,) * 8,
        scratch_shapes=[
            pltpu.SMEM(lengths.shape, jnp.int32),
            pltpu.SemaphoreType.DMA,
            pltpu.SemaphoreType.DMA((KEY_VALUE_HEADS,)),
        ],
        compiler_params=pltpu.CompilerParams(vmem_limit_bytes=10 * 1024 * 1024),
        cost_estimate=pl.CostEstimate(
            flops=4 * 10**9, bytes_accessed=16 * 10**6, transcendentals=rows * queries.size
        ),
    )(*in_vmem(own), *in_hbm(lengths, queries))


def own_rest(own, own_bias, queries, kept):
    rows = queries.shape[0]
    operands = in_vmem(own, own_bias, queries, *kept)
    return pl.pallas_call(
        functools.partial(own_rest_kernel, rows),
        out_shape=tuple(pltpu.VMEM(x.shape, x.dtype) for x in kept),
        in_specs=[VMEM] * len(operands),
        out_specs=(VMEM,) * len(kept),
        input_output_aliases={3 + n: n for n in range(len(kept))},
        compiler_params=pltpu.CompilerParams(vmem_limit_bytes=10 * 1024 * 1024),
        cost_estimate=pl.CostEstimate(
            flops=4 * 10**9, bytes_accessed=16 * 10**6, transcendentals=rows * queries.size
        ),
    )(*operands)


def behind_kernel(
    before, last, rows, needed_ref, bias_ref, q_ref, near_ref, further_ref, level_ref, mean_ref, *refs
):
    beyond = needed_ref[0, 0] - before
    crossing = needed_ref[4, 0]
    pairs = [(ref.at[:rows], ref.at[rows : 2 * rows]) for ref in (near_ref, further_ref)]
    if last:
        out_hbm, out_ref, out_sems = refs

        def out_copy(n):
            width = HEADS_AT_ONCE * HEAD_SIZE
            at = slice(n * width, (n + 1) * width)
            return pltpu.make_async_copy(out_ref.at[:, at], out_hbm.at[:, at], out_sems.at[n])

    else:
        _, new_level_ref, new_mean_ref = refs

    def finish(heads, upto, mean):
        spread(out_ref, heads, upto, mean)
        if upto < rows:
            for i in heads:
                out_ref[upto:, head_columns(i)] = mean_ref[upto:, head_columns(i)].astype(
                    out_ref.dtype
                )
        for i in heads[::HEADS_AT_ONCE]:
            out_copy(i // HEADS_AT_ONCE).start()

    def attend(count, upto):
        def match(heads, g):
            key = jnp.concatenate([key[:, head_columns(g)] for key, _ in pairs[:count]], axis=0)
            bias = bias_ref[:upto, before * rows : (before + count) * rows]
            return (scores_of(stacked(q_ref, heads, upto), key, bias),)

        def weigh(heads, g, scores):
            level = stacked(level_ref, heads, upto)
            top = jnp.maximum(level, jnp.max(scores, axis=1, keepdims=True))
            fade = jnp.exp2((level - top) * jnp.float32(FACTOR))
            return weights_of(scores, jnp.concatenate([top] * count, axis=1)), fade, top

        def gather(heads, g, weights, fade, top):
            value = jnp.concatenate([value[:, head_columns(g)] for _, value in pairs[:count]], axis=0)
            more = jnp.dot(weights, with_ones(value), preferred_element_type=jnp.float32)
            summed = stacked(mean_ref, heads, upto) * fade + more[:, :HEAD_SIZE]
            total = fade + more[:, HEAD_SIZE:]
            if last:
                finish(heads, upto, normalised(summed, total))
            else:
                spread(new_mean_ref, heads, upto, normalised(summed, total))
                spread(new_level_ref, heads, upto, level_of(top, total))

        runs = chains() if upto == rows else chains(GROUP)
        in_turn(runs, match, weigh, gather)

    sizes = [0, rows // 2, rows]
    for count, enough in ((2, beyond > 1), (1, beyond == 1)):
        for low, upto in zip(sizes, sizes[1:]):
            fits = crossing > low if upto == rows else (crossing > low) & (crossing <= upto)
            pl.when(enough & fits)(functools.partial(attend, count, upto))

    if last:
        @pl.when(beyond < 1)
        def _():
            in_turn(
                chains(),
                lambda heads, g: finish(heads, rows, stacked(mean_ref, heads, rows)),
            )

        for n in range(len(chains())):
            out_copy(n).wait()


def behind_part(before, last, needed, bias, queries, near, further, parts):
    rows = queries.shape[0]
    area = rows * rows * 2 * QUERY_HEADS
    operands = in_vmem(needed, bias, queries, near, further, *parts)
    if last:
        out_shape = jax.ShapeDtypeStruct(queries.shape, queries.dtype)
        out_specs = HBM
        scratch = [
            pltpu.VMEM(queries.shape, queries.dtype),
            pltpu.SemaphoreType.DMA((len(chains()),)),
        ]
        aliases = {}
    else:
        kept = (further, *parts)
        out_shape = tuple(pltpu.VMEM(part.shape, part.dtype) for part in kept)
        out_specs = (VMEM,) * len(kept)
        scratch = []
        aliases = {4 + n: n for n in range(len(kept))}
    return pl.pallas_call(
        functools.partial(behind_kernel, before, last, rows),
        out_shape=out_shape,
        in_specs=[VMEM] * len(operands),
        out_specs=out_specs,
        scratch_shapes=scratch,
        input_output_aliases=aliases,
        compiler_params=pltpu.CompilerParams(vmem_limit_bytes=10 * 1024 * 1024),
        cost_estimate=pl.CostEstimate(
            flops=4 * area, bytes_accessed=queries.size, transcendentals=0
        ),
    )(*operands)


def per_device(queries, keys, values, lengths):
    count = lax.axis_size("dp") * lax.axis_size("ctx")
    rounds = lax.axis_size("ctx")

    def from_behind(block, r):
        by = 2 * (r + 1)
        return lax.ppermute(block, AXES, [(i, i + by) for i in range(count - by)])

    own = pack(keys, values)
    fetched = [from_behind(own, 0)]
    longer, bias, needed, own_bias, queries, *kept = own_part(lengths, queries, own, rounds)
    fetched += [from_behind(longer, r) for r in range(1, rounds)]
    odd, *parts = own_rest(own, own_bias, queries, kept)
    swap = [(i, i ^ 1) for i in range(count)]
    nearer = own
    size = 2 * keys.shape[0]
    for r, further in enumerate(fetched):
        last = r == rounds - 1
        near = lax.ppermute(jnp.where(odd == 1, further[:size], nearer[:size]), AXES, swap)
        result = behind_part(2 * r, last, needed, bias, queries, near, further, parts)
        if not last:
            nearer, *parts = result
    return result


def solution(mesh):
    in_specs = (P(AXES, None), P(AXES, None), P(AXES, None), P())
    return jax.shard_map(
        per_device, mesh=mesh, in_specs=in_specs, out_specs=P(AXES, None), check_vma=False
    )
```

```python
import functools
import math

import jax
import jax.numpy as jnp
from jax import lax
from jax.experimental import pallas as pl
from jax.experimental.pallas import tpu as pltpu
from jax.sharding import PartitionSpec as P

HEAD_SIZE = 128
QUERY_HEADS = 32
KEY_VALUE_HEADS = 4
GROUP = QUERY_HEADS // KEY_VALUE_HEADS
HEADS_AT_ONCE = 4
EARLY_CHAINS = 4
EXCLUDED = -1e30
PAD = 16
AXES = ("dp", "ctx")


FACTOR = math.log2(math.e) / math.sqrt(HEAD_SIZE)


def head_columns(i):
    return slice(i * HEAD_SIZE, (i + 1) * HEAD_SIZE)


def stacked(ref, heads, rows):
    return jnp.concatenate([ref[:rows, head_columns(i)] for i in heads], axis=0)


def spread(ref, heads, rows, value):
    for n, i in enumerate(heads):
        ref[:rows, head_columns(i)] = value[n * rows : (n + 1) * rows].astype(ref.dtype)


def with_ones(value):
    return jnp.concatenate([value, jnp.ones(value.shape, value.dtype)], axis=1)


def scores_of(q, key, bias):
    scores = lax.dot_general(
        q, key, (((1,), (1,)), ((), ())), preferred_element_type=jnp.float32
    )
    return scores + jnp.concatenate([bias] * (q.shape[0] // bias.shape[0]), axis=0)


def weights_of(scores, top):
    return jnp.exp2((scores - top) * jnp.float32(FACTOR)).astype(jnp.bfloat16)


def normalised(summed, total):
    inverse = pl.reciprocal(total, approx=True)
    return summed * (inverse * (2.0 - total * inverse))


def level_of(top, total):
    return top + jnp.log(total) * jnp.float32(math.sqrt(HEAD_SIZE))


def chains(size=HEADS_AT_ONCE):
    return [(range(h, h + size), h // GROUP) for h in range(0, QUERY_HEADS, size)]


def in_turn(runs, *stages):
    results = {}
    for turn in range(len(runs) + len(stages) - 1):
        for n, stage in enumerate(stages):
            i = turn - n
            if 0 <= i < len(runs):
                results[i] = stage(*runs[i], *results.pop(i, ()))


def pack_kernel(key_hbm, value_hbm, out_ref, sems):
    rows = key_hbm.shape[0]
    copies = [
        pltpu.make_async_copy(key_hbm, out_ref.at[:rows], sems.at[0]),
        pltpu.make_async_copy(value_hbm, out_ref.at[rows:], sems.at[1]),
    ]
    for copy in copies:
        copy.start()
    for copy in copies:
        copy.wait()


def pack(keys, values):
    rows, width = keys.shape
    return pl.pallas_call(
        pack_kernel,
        out_shape=pltpu.VMEM((2 * rows, width), keys.dtype),
        in_specs=[HBM, HBM],
        out_specs=VMEM,
        scratch_shapes=[pltpu.SemaphoreType.DMA((2,))],
        compiler_params=pltpu.CompilerParams(vmem_limit_bytes=1024 * 1024),
    )(*in_hbm(keys, values))


def attend_own(runs, rows, own_ref, own_bias_ref, q_ref, level_ref, mean_ref, ready):
    def match(heads, g):
        ready(heads, g)
        key = own_ref[:rows, head_columns(g)]
        return (scores_of(stacked(q_ref, heads, rows), key, own_bias_ref[...]),)

    def weigh(heads, g, scores):
        top = jnp.max(scores, axis=1, keepdims=True)
        return weights_of(scores, top), jnp.broadcast_to(top, scores.shape)

    def gather(heads, g, weights, top):
        value = with_ones(own_ref[rows:, head_columns(g)])
        more = jnp.dot(weights, value, preferred_element_type=jnp.float32)
        summed, total = more[:, :HEAD_SIZE], more[:, HEAD_SIZE:]
        spread(mean_ref, heads, rows, normalised(summed, total))
        spread(level_ref, heads, rows, level_of(top, total))

    in_turn(runs, match, weigh, gather)


def own_kernel(
    rounds, rows, own_ref, lengths_hbm, q_hbm,
    longer_ref, bias_ref, needed_ref, own_bias_ref, q_ref, odd_ref, level_ref, mean_ref,
    lengths_ref, lengths_sem, q_sems,
):
    lengths_copy = pltpu.make_async_copy(lengths_hbm, lengths_ref, lengths_sem)
    lengths_copy.start()
    width = GROUP * HEAD_SIZE
    q_copies = []
    for g in range(KEY_VALUE_HEADS):
        at = slice(g * width, (g + 1) * width)
        q_copies.append(pltpu.make_async_copy(q_hbm.at[:, at], q_ref.at[:, at], q_sems.at[g]))
        q_copies[g].start()
    me = lax.axis_index("dp") * lax.axis_size("ctx") + lax.axis_index("ctx")
    longer_ref[: 2 * rows, :] = own_ref[...]
    longer_ref[2 * rows :, :] = jnp.zeros((PAD, longer_ref.shape[1]), longer_ref.dtype)
    odd_ref[...] = jnp.full(odd_ref.shape, lax.rem(me, 2), jnp.int32)
    first = me * rows
    query_pos = first + lax.broadcasted_iota(jnp.int32, (rows, rows), 0)
    lengths_copy.wait()

    def later(doc, carried):
        bound, start, first_start, first_end = carried
        following = bound + lengths_ref[doc]
        start = jnp.where(query_pos >= bound, bound, start)
        first_start = jnp.where(first >= bound, bound, first_start)
        first_end = jnp.where(first >= bound, following, first_end)
        return following, start, first_start, first_end

    zero = jnp.int32(0)
    _, start, first_start, first_end = lax.fori_loop(
        0,
        lengths_ref.shape[0],
        later,
        (zero, jnp.zeros((rows, rows), jnp.int32), zero, zero),
        unroll=8,
    )
    needed = lax.div(first - first_start + (rows - 1), jnp.int32(rows))
    crossing = jnp.minimum(first_end - first, rows)
    needed_ref[...] = jnp.full(needed_ref.shape, needed * (rows + 1) + crossing, jnp.int32)
    lane = lax.broadcasted_iota(jnp.int32, (rows, rows), 1)

    def bias_of(allowed):
        return jnp.where(allowed, jnp.float32(0.0), jnp.float32(EXCLUDED))

    key_pos = first + lane
    own_bias_ref[...] = bias_of((key_pos >= start) & (key_pos <= query_pos))
    for b in range(2 * rounds):
        key_pos = first - (b + 1) * rows + lane
        bias_ref[:, b * rows : (b + 1) * rows] = bias_of(key_pos >= start)

    def ready(heads, g):
        if heads[0] % GROUP == 0:
            q_copies[g].wait()

    runs = chains()[:EARLY_CHAINS]
    attend_own(runs, rows, own_ref, own_bias_ref, q_ref, level_ref, mean_ref, ready)
    for copy in q_copies[runs[-1][1] + 1 :]:
        copy.wait()


def own_rest_kernel(
    rows, own_ref, own_bias_ref, q_ref, odd_ref, *parts
):
    runs = chains()[EARLY_CHAINS:]
    parts = parts[3:]
    attend_own(runs, rows, own_ref, own_bias_ref, q_ref, *parts, lambda heads, g: None)


def in_vmem(*operands):
    return [pltpu.with_memory_space_constraint(x, pltpu.VMEM) for x in operands]


def in_hbm(*operands):
    return [pltpu.with_memory_space_constraint(x, pltpu.HBM) for x in operands]


SMEM = pl.BlockSpec(memory_space=pltpu.SMEM)
VMEM = pl.BlockSpec(memory_space=pltpu.VMEM)
HBM = pl.BlockSpec(memory_space=pltpu.HBM)


def own_part(lengths, queries, own, rounds):
    rows = queries.shape[0]
    part = pltpu.VMEM(queries.shape, jnp.float32)
    return pl.pallas_call(
        functools.partial(own_kernel, rounds, rows),
        out_shape=(
            pltpu.VMEM((2 * rows + PAD, own.shape[1]), own.dtype),
            pltpu.VMEM((rows, 2 * rounds * rows), jnp.float32),
            pltpu.VMEM((8, 128), jnp.int32),
            pltpu.VMEM((rows, rows), jnp.float32),
            pltpu.VMEM(queries.shape, queries.dtype),
            pltpu.VMEM((1, own.shape[1]), jnp.int32),
            part,
            part,
        ),
        in_specs=[VMEM, HBM, HBM],
        out_specs=(VMEM,) * 8,
        scratch_shapes=[
            pltpu.SMEM(lengths.shape, jnp.int32),
            pltpu.SemaphoreType.DMA,
            pltpu.SemaphoreType.DMA((KEY_VALUE_HEADS,)),
        ],
        compiler_params=pltpu.CompilerParams(vmem_limit_bytes=10 * 1024 * 1024),
        cost_estimate=pl.CostEstimate(
            flops=4 * 10**9, bytes_accessed=16 * 10**6, transcendentals=rows * queries.size
        ),
    )(*in_vmem(own), *in_hbm(lengths, queries))


def own_rest(own, own_bias, queries, kept):
    rows = queries.shape[0]
    operands = in_vmem(own, own_bias, queries, *kept)
    return pl.pallas_call(
        functools.partial(own_rest_kernel, rows),
        out_shape=tuple(pltpu.VMEM(x.shape, x.dtype) for x in kept),
        in_specs=[VMEM] * len(operands),
        out_specs=(VMEM,) * len(kept),
        input_output_aliases={3 + n: n for n in range(len(kept))},
        compiler_params=pltpu.CompilerParams(vmem_limit_bytes=10 * 1024 * 1024),
        cost_estimate=pl.CostEstimate(
            flops=4 * 10**9, bytes_accessed=16 * 10**6, transcendentals=rows * queries.size
        ),
    )(*operands)


def behind_kernel(
    before, last, rows, needed_ref, bias_ref, q_ref, near_ref, further_ref, level_ref, mean_ref, *refs
):
    both = needed_ref[0, 0]
    beyond = lax.div(both, rows + 1) - before
    crossing = lax.rem(both, rows + 1)
    pairs = [(ref.at[:rows], ref.at[rows : 2 * rows]) for ref in (near_ref, further_ref)]
    if last:
        out_hbm, out_ref, out_sems = refs

        def out_copy(n):
            width = HEADS_AT_ONCE * HEAD_SIZE
            at = slice(n * width, (n + 1) * width)
            return pltpu.make_async_copy(out_ref.at[:, at], out_hbm.at[:, at], out_sems.at[n])

    else:
        _, new_level_ref, new_mean_ref = refs

    def finish(heads, upto, mean):
        spread(out_ref, heads, upto, mean)
        if upto < rows:
            for i in heads:
                out_ref[upto:, head_columns(i)] = mean_ref[upto:, head_columns(i)].astype(
                    out_ref.dtype
                )
        for i in heads[::HEADS_AT_ONCE]:
            out_copy(i // HEADS_AT_ONCE).start()

    def attend(count, upto):
        def match(heads, g):
            key = jnp.concatenate([key[:, head_columns(g)] for key, _ in pairs[:count]], axis=0)
            bias = bias_ref[:upto, before * rows : (before + count) * rows]
            return (scores_of(stacked(q_ref, heads, upto), key, bias),)

        def weigh(heads, g, scores):
            level = stacked(level_ref, heads, upto)
            top = jnp.maximum(level, jnp.max(scores, axis=1, keepdims=True))
            fade = jnp.exp2((level - top) * jnp.float32(FACTOR))
            return weights_of(scores, jnp.concatenate([top] * count, axis=1)), fade, top

        def gather(heads, g, weights, fade, top):
            value = jnp.concatenate([value[:, head_columns(g)] for _, value in pairs[:count]], axis=0)
            more = jnp.dot(weights, with_ones(value), preferred_element_type=jnp.float32)
            summed = stacked(mean_ref, heads, upto) * fade + more[:, :HEAD_SIZE]
            total = fade + more[:, HEAD_SIZE:]
            if last:
                finish(heads, upto, normalised(summed, total))
            else:
                spread(new_mean_ref, heads, upto, normalised(summed, total))
                spread(new_level_ref, heads, upto, level_of(top, total))

        runs = chains() if upto == rows else chains(GROUP)
        in_turn(runs, match, weigh, gather)

    short = crossing <= rows // 2
    pl.when((beyond > 0) & short)(functools.partial(attend, 2, rows // 2))
    pl.when((beyond > 1) & jnp.logical_not(short))(functools.partial(attend, 2, rows))
    pl.when((beyond == 1) & jnp.logical_not(short))(functools.partial(attend, 1, rows))

    if last:
        @pl.when(beyond < 1)
        def _():
            in_turn(
                chains(),
                lambda heads, g: finish(heads, rows, stacked(mean_ref, heads, rows)),
            )

        for n in range(len(chains())):
            out_copy(n).wait()


def behind_part(before, last, needed, bias, queries, near, further, parts):
    rows = queries.shape[0]
    area = rows * rows * 2 * QUERY_HEADS
    operands = in_vmem(needed, bias, queries, near, further, *parts)
    if last:
        out_shape = jax.ShapeDtypeStruct(queries.shape, queries.dtype)
        out_specs = HBM
        scratch = [
            pltpu.VMEM(queries.shape, queries.dtype),
            pltpu.SemaphoreType.DMA((len(chains()),)),
        ]
        aliases = {}
    else:
        kept = (further, *parts)
        out_shape = tuple(pltpu.VMEM(part.shape, part.dtype) for part in kept)
        out_specs = (VMEM,) * len(kept)
        scratch = []
        aliases = {4 + n: n for n in range(len(kept))}
    return pl.pallas_call(
        functools.partial(behind_kernel, before, last, rows),
        out_shape=out_shape,
        in_specs=[VMEM] * len(operands),
        out_specs=out_specs,
        scratch_shapes=scratch,
        input_output_aliases=aliases,
        compiler_params=pltpu.CompilerParams(vmem_limit_bytes=10 * 1024 * 1024),
        cost_estimate=pl.CostEstimate(
            flops=4 * area, bytes_accessed=queries.size, transcendentals=0
        ),
    )(*operands)


def per_device(queries, keys, values, lengths):
    count = lax.axis_size("dp") * lax.axis_size("ctx")
    rounds = lax.axis_size("ctx")

    def from_behind(block, r):
        by = 2 * (r + 1)
        return lax.ppermute(block, AXES, [(i, i + by) for i in range(count - by)])

    own = pack(keys, values)
    fetched = [from_behind(own, 0)]
    longer, bias, needed, own_bias, queries, *kept = own_part(lengths, queries, own, rounds)
    fetched += [from_behind(longer, r) for r in range(1, rounds)]
    odd, *parts = own_rest(own, own_bias, queries, kept)
    swap = [(i, i ^ 1) for i in range(count)]
    nearer = own
    size = 2 * keys.shape[0]
    for r, further in enumerate(fetched):
        last = r == rounds - 1
        near = lax.ppermute(jnp.where(odd == 1, further[:size], nearer[:size]), AXES, swap)
        result = behind_part(2 * r, last, needed, bias, queries, near, further, parts)
        if not last:
            nearer, *parts = result
    return result


def solution(mesh):
    in_specs = (P(AXES, None), P(AXES, None), P(AXES, None), P())
    return jax.shard_map(
        per_device, mesh=mesh, in_specs=in_specs, out_specs=P(AXES, None), check_vma=False
    )
```

```python
import functools
import math

import jax
import jax.numpy as jnp
from jax import lax
from jax.experimental import pallas as pl
from jax.experimental.pallas import tpu as pltpu
from jax.sharding import PartitionSpec as P

HEAD_SIZE = 128
QUERY_HEADS = 32
KEY_VALUE_HEADS = 4
GROUP = QUERY_HEADS // KEY_VALUE_HEADS
HEADS_AT_ONCE = 4
EARLY_CHAINS = 4
EXCLUDED = -1e30
PAD = 16
AXES = ("dp", "ctx")


FACTOR = math.log2(math.e) / math.sqrt(HEAD_SIZE)


def head_columns(i):
    return slice(i * HEAD_SIZE, (i + 1) * HEAD_SIZE)


def stacked(ref, heads, rows):
    return jnp.concatenate([ref[:rows, head_columns(i)] for i in heads], axis=0)


def spread(ref, heads, rows, value):
    for n, i in enumerate(heads):
        ref[:rows, head_columns(i)] = value[n * rows : (n + 1) * rows].astype(ref.dtype)


def scores_of(q, key, bias):
    scores = lax.dot_general(
        q, key, (((1,), (1,)), ((), ())), preferred_element_type=jnp.float32
    )
    return scores + jnp.concatenate([bias] * (q.shape[0] // bias.shape[0]), axis=0)


def weights_of(scores, top):
    weights = jnp.exp2((scores - top) * jnp.float32(FACTOR))
    total = jnp.sum(weights, axis=1, keepdims=True)
    return weights.astype(jnp.bfloat16), jnp.broadcast_to(total, (scores.shape[0], HEAD_SIZE))


def normalised(summed, total):
    inverse = pl.reciprocal(total, approx=True)
    return summed * (inverse * (2.0 - total * inverse))


def level_of(top, total):
    return top + jnp.log(total) * jnp.float32(math.sqrt(HEAD_SIZE))


def chains(size=HEADS_AT_ONCE):
    return [(range(h, h + size), h // GROUP) for h in range(0, QUERY_HEADS, size)]


def in_turn(runs, *stages):
    results = {}
    for turn in range(len(runs) + len(stages) - 1):
        for n, stage in enumerate(stages):
            i = turn - n
            if 0 <= i < len(runs):
                results[i] = stage(*runs[i], *results.pop(i, ()))


def pack_kernel(key_hbm, value_hbm, out_ref, sems):
    rows = key_hbm.shape[0]
    copies = [
        pltpu.make_async_copy(key_hbm, out_ref.at[:rows], sems.at[0]),
        pltpu.make_async_copy(value_hbm, out_ref.at[rows:], sems.at[1]),
    ]
    for copy in copies:
        copy.start()
    for copy in copies:
        copy.wait()


def pack(keys, values):
    rows, width = keys.shape
    return pl.pallas_call(
        pack_kernel,
        out_shape=pltpu.VMEM((2 * rows, width), keys.dtype),
        in_specs=[HBM, HBM],
        out_specs=VMEM,
        scratch_shapes=[pltpu.SemaphoreType.DMA((2,))],
        compiler_params=pltpu.CompilerParams(vmem_limit_bytes=1024 * 1024),
    )(*in_hbm(keys, values))


def attend_own(runs, rows, own_ref, own_bias_ref, q_ref, level_ref, mean_ref, ready):
    def match(heads, g):
        ready(heads, g)
        key = own_ref[:rows, head_columns(g)]
        return (scores_of(stacked(q_ref, heads, rows), key, own_bias_ref[...]),)

    def weigh(heads, g, scores):
        top = jnp.max(scores, axis=1, keepdims=True)
        return *weights_of(scores, top), jnp.broadcast_to(top, scores.shape)

    def gather(heads, g, weights, total, top):
        value = own_ref[rows:, head_columns(g)]
        summed = jnp.dot(weights, value, preferred_element_type=jnp.float32)
        spread(mean_ref, heads, rows, normalised(summed, total))
        spread(level_ref, heads, rows, level_of(top, total))

    in_turn(runs, match, weigh, gather)


def own_kernel(
    rounds, rows, own_ref, lengths_hbm, q_hbm,
    longer_ref, bias_ref, needed_ref, own_bias_ref, q_ref, odd_ref, level_ref, mean_ref,
    lengths_ref, lengths_sem, q_sems,
):
    lengths_copy = pltpu.make_async_copy(lengths_hbm, lengths_ref, lengths_sem)
    lengths_copy.start()
    width = GROUP * HEAD_SIZE
    q_copies = []
    for g in range(KEY_VALUE_HEADS):
        at = slice(g * width, (g + 1) * width)
        q_copies.append(pltpu.make_async_copy(q_hbm.at[:, at], q_ref.at[:, at], q_sems.at[g]))
        q_copies[g].start()
    me = lax.axis_index("dp") * lax.axis_size("ctx") + lax.axis_index("ctx")
    longer_ref[: 2 * rows, :] = own_ref[...]
    longer_ref[2 * rows :, :] = jnp.zeros((PAD, longer_ref.shape[1]), longer_ref.dtype)
    odd_ref[...] = jnp.full(odd_ref.shape, lax.rem(me, 2), jnp.int32)
    first = me * rows
    query_pos = first + lax.broadcasted_iota(jnp.int32, (rows, rows), 0)
    lengths_copy.wait()

    def later(doc, carried):
        bound, start, first_start, first_end = carried
        following = bound + lengths_ref[doc]
        start = jnp.where(query_pos >= bound, bound, start)
        first_start = jnp.where(first >= bound, bound, first_start)
        first_end = jnp.where(first >= bound, following, first_end)
        return following, start, first_start, first_end

    zero = jnp.int32(0)
    _, start, first_start, first_end = lax.fori_loop(
        0,
        lengths_ref.shape[0],
        later,
        (zero, jnp.zeros((rows, rows), jnp.int32), zero, zero),
        unroll=8,
    )
    needed = lax.div(first - first_start + (rows - 1), jnp.int32(rows))
    crossing = jnp.minimum(first_end - first, rows)
    needed_ref[...] = jnp.full(needed_ref.shape, needed * (rows + 1) + crossing, jnp.int32)
    lane = lax.broadcasted_iota(jnp.int32, (rows, rows), 1)

    def bias_of(allowed):
        return jnp.where(allowed, jnp.float32(0.0), jnp.float32(EXCLUDED))

    key_pos = first + lane
    own_bias_ref[...] = bias_of((key_pos >= start) & (key_pos <= query_pos))
    for b in range(2 * rounds):
        key_pos = first - (b + 1) * rows + lane
        bias_ref[:, b * rows : (b + 1) * rows] = bias_of(key_pos >= start)

    def ready(heads, g):
        if heads[0] % GROUP == 0:
            q_copies[g].wait()

    runs = chains()[:EARLY_CHAINS]
    attend_own(runs, rows, own_ref, own_bias_ref, q_ref, level_ref, mean_ref, ready)
    for copy in q_copies[runs[-1][1] + 1 :]:
        copy.wait()


def own_rest_kernel(
    rows, own_ref, own_bias_ref, q_ref, odd_ref, *parts
):
    runs = chains()[EARLY_CHAINS:]
    parts = parts[3:]
    attend_own(runs, rows, own_ref, own_bias_ref, q_ref, *parts, lambda heads, g: None)


def in_vmem(*operands):
    return [pltpu.with_memory_space_constraint(x, pltpu.VMEM) for x in operands]


def in_hbm(*operands):
    return [pltpu.with_memory_space_constraint(x, pltpu.HBM) for x in operands]


SMEM = pl.BlockSpec(memory_space=pltpu.SMEM)
VMEM = pl.BlockSpec(memory_space=pltpu.VMEM)
HBM = pl.BlockSpec(memory_space=pltpu.HBM)


def own_part(lengths, queries, own, rounds):
    rows = queries.shape[0]
    part = pltpu.VMEM(queries.shape, jnp.float32)
    return pl.pallas_call(
        functools.partial(own_kernel, rounds, rows),
        out_shape=(
            pltpu.VMEM((2 * rows + PAD, own.shape[1]), own.dtype),
            pltpu.VMEM((rows, 2 * rounds * rows), jnp.float32),
            pltpu.VMEM((8, 128), jnp.int32),
            pltpu.VMEM((rows, rows), jnp.float32),
            pltpu.VMEM(queries.shape, queries.dtype),
            pltpu.VMEM((1, own.shape[1]), jnp.int32),
            part,
            part,
        ),
        in_specs=[VMEM, HBM, HBM],
        out_specs=(VMEM,) * 8,
        scratch_shapes=[
            pltpu.SMEM(lengths.shape, jnp.int32),
            pltpu.SemaphoreType.DMA,
            pltpu.SemaphoreType.DMA((KEY_VALUE_HEADS,)),
        ],
        compiler_params=pltpu.CompilerParams(vmem_limit_bytes=10 * 1024 * 1024),
        cost_estimate=pl.CostEstimate(
            flops=4 * 10**9, bytes_accessed=16 * 10**6, transcendentals=rows * queries.size
        ),
    )(*in_vmem(own), *in_hbm(lengths, queries))


def own_rest(own, own_bias, queries, kept):
    rows = queries.shape[0]
    operands = in_vmem(own, own_bias, queries, *kept)
    return pl.pallas_call(
        functools.partial(own_rest_kernel, rows),
        out_shape=tuple(pltpu.VMEM(x.shape, x.dtype) for x in kept),
        in_specs=[VMEM] * len(operands),
        out_specs=(VMEM,) * len(kept),
        input_output_aliases={3 + n: n for n in range(len(kept))},
        compiler_params=pltpu.CompilerParams(vmem_limit_bytes=10 * 1024 * 1024),
        cost_estimate=pl.CostEstimate(
            flops=4 * 10**9, bytes_accessed=16 * 10**6, transcendentals=rows * queries.size
        ),
    )(*operands)


def behind_kernel(
    before, last, rows, needed_ref, bias_ref, q_ref, near_ref, further_ref, level_ref, mean_ref, *refs
):
    both = needed_ref[0, 0]
    beyond = lax.div(both, rows + 1) - before
    crossing = lax.rem(both, rows + 1)
    pairs = [(ref.at[:rows], ref.at[rows : 2 * rows]) for ref in (near_ref, further_ref)]
    if last:
        out_hbm, out_ref, out_sems = refs

        def out_copy(n):
            width = HEADS_AT_ONCE * HEAD_SIZE
            at = slice(n * width, (n + 1) * width)
            return pltpu.make_async_copy(out_ref.at[:, at], out_hbm.at[:, at], out_sems.at[n])

    else:
        _, new_level_ref, new_mean_ref = refs

    def finish(heads, upto, mean):
        spread(out_ref, heads, upto, mean)
        if upto < rows:
            for i in heads:
                out_ref[upto:, head_columns(i)] = mean_ref[upto:, head_columns(i)].astype(
                    out_ref.dtype
                )
        for i in heads[::HEADS_AT_ONCE]:
            out_copy(i // HEADS_AT_ONCE).start()

    def attend(count, upto):
        def match(heads, g):
            key = jnp.concatenate([key[:, head_columns(g)] for key, _ in pairs[:count]], axis=0)
            bias = bias_ref[:upto, before * rows : (before + count) * rows]
            return (scores_of(stacked(q_ref, heads, upto), key, bias),)

        def weigh(heads, g, scores):
            level = stacked(level_ref, heads, upto)
            top = jnp.maximum(level, jnp.max(scores, axis=1, keepdims=True))
            fade = jnp.exp2((level - top) * jnp.float32(FACTOR))
            return *weights_of(scores, jnp.concatenate([top] * count, axis=1)), fade, top

        def gather(heads, g, weights, total, fade, top):
            value = jnp.concatenate([value[:, head_columns(g)] for _, value in pairs[:count]], axis=0)
            more = jnp.dot(weights, value, preferred_element_type=jnp.float32)
            summed = stacked(mean_ref, heads, upto) * fade + more
            total = fade + total
            if last:
                finish(heads, upto, normalised(summed, total))
            else:
                spread(new_mean_ref, heads, upto, normalised(summed, total))
                spread(new_level_ref, heads, upto, level_of(top, total))

        runs = chains() if upto == rows else chains(GROUP)
        in_turn(runs, match, weigh, gather)

    short = crossing <= rows // 2
    pl.when((beyond > 0) & short)(functools.partial(attend, 2, rows // 2))
    pl.when((beyond > 1) & jnp.logical_not(short))(functools.partial(attend, 2, rows))
    pl.when((beyond == 1) & jnp.logical_not(short))(functools.partial(attend, 1, rows))

    if last:
        @pl.when(beyond < 1)
        def _():
            in_turn(
                chains(),
                lambda heads, g: finish(heads, rows, stacked(mean_ref, heads, rows)),
            )

        for n in range(len(chains())):
            out_copy(n).wait()


def behind_part(before, last, needed, bias, queries, near, further, parts):
    rows = queries.shape[0]
    area = rows * rows * 2 * QUERY_HEADS
    operands = in_vmem(needed, bias, queries, near, further, *parts)
    if last:
        out_shape = jax.ShapeDtypeStruct(queries.shape, queries.dtype)
        out_specs = HBM
        scratch = [
            pltpu.VMEM(queries.shape, queries.dtype),
            pltpu.SemaphoreType.DMA((len(chains()),)),
        ]
        aliases = {}
    else:
        kept = (further, *parts)
        out_shape = tuple(pltpu.VMEM(part.shape, part.dtype) for part in kept)
        out_specs = (VMEM,) * len(kept)
        scratch = []
        aliases = {4 + n: n for n in range(len(kept))}
    return pl.pallas_call(
        functools.partial(behind_kernel, before, last, rows),
        out_shape=out_shape,
        in_specs=[VMEM] * len(operands),
        out_specs=out_specs,
        scratch_shapes=scratch,
        input_output_aliases=aliases,
        compiler_params=pltpu.CompilerParams(vmem_limit_bytes=10 * 1024 * 1024),
        cost_estimate=pl.CostEstimate(
            flops=4 * area, bytes_accessed=queries.size, transcendentals=0
        ),
    )(*operands)


def per_device(queries, keys, values, lengths):
    count = lax.axis_size("dp") * lax.axis_size("ctx")
    rounds = lax.axis_size("ctx")

    def from_behind(block, r):
        by = 2 * (r + 1)
        return lax.ppermute(block, AXES, [(i, i + by) for i in range(count - by)])

    own = pack(keys, values)
    fetched = [from_behind(own, 0)]
    longer, bias, needed, own_bias, queries, *kept = own_part(lengths, queries, own, rounds)
    fetched += [from_behind(longer, r) for r in range(1, rounds)]
    odd, *parts = own_rest(own, own_bias, queries, kept)
    swap = [(i, i ^ 1) for i in range(count)]
    nearer = own
    size = 2 * keys.shape[0]
    for r, further in enumerate(fetched):
        last = r == rounds - 1
        near = lax.ppermute(jnp.where(odd == 1, further[:size], nearer[:size]), AXES, swap)
        result = behind_part(2 * r, last, needed, bias, queries, near, further, parts)
        if not last:
            nearer, *parts = result
    return result


def solution(mesh):
    in_specs = (P(AXES, None), P(AXES, None), P(AXES, None), P())
    return jax.shard_map(
        per_device, mesh=mesh, in_specs=in_specs, out_specs=P(AXES, None), check_vma=False
    )
```

```python
import functools
import math

import jax
import jax.numpy as jnp
from jax import lax
from jax.experimental import pallas as pl
from jax.experimental.pallas import tpu as pltpu
from jax.sharding import PartitionSpec as P

HEAD_SIZE = 128
QUERY_HEADS = 32
KEY_VALUE_HEADS = 4
GROUP = QUERY_HEADS // KEY_VALUE_HEADS
HEADS_AT_ONCE = 4
EARLY_CHAINS = 5
EXCLUDED = -1e30
PAD = 16
AXES = ("dp", "ctx")


FACTOR = math.log2(math.e) / math.sqrt(HEAD_SIZE)


def head_columns(i):
    return slice(i * HEAD_SIZE, (i + 1) * HEAD_SIZE)


def stacked(ref, heads, rows):
    return jnp.concatenate([ref[:rows, head_columns(i)] for i in heads], axis=0)


def spread(ref, heads, rows, value):
    for n, i in enumerate(heads):
        ref[:rows, head_columns(i)] = value[n * rows : (n + 1) * rows].astype(ref.dtype)


def with_ones(value):
    return jnp.concatenate([value, jnp.ones(value.shape, value.dtype)], axis=1)


def scores_of(q, key, bias):
    scores = lax.dot_general(
        q, key, (((1,), (1,)), ((), ())), preferred_element_type=jnp.float32
    )
    return scores + jnp.concatenate([bias] * (q.shape[0] // bias.shape[0]), axis=0)


def weights_of(scores, top):
    return jnp.exp2((scores - top) * jnp.float32(FACTOR)).astype(jnp.bfloat16)


def normalised(summed, total):
    inverse = pl.reciprocal(total, approx=True)
    return summed * (inverse * (2.0 - total * inverse))


def level_of(top, total):
    return top + jnp.log(total) * jnp.float32(math.sqrt(HEAD_SIZE))


def chains(size=HEADS_AT_ONCE):
    return [(range(h, h + size), h // GROUP) for h in range(0, QUERY_HEADS, size)]


def in_turn(runs, *stages):
    results = {}
    for turn in range(len(runs) + len(stages) - 1):
        for n, stage in enumerate(stages):
            i = turn - n
            if 0 <= i < len(runs):
                results[i] = stage(*runs[i], *results.pop(i, ()))


def pack_kernel(key_hbm, value_hbm, out_ref, sems):
    rows = key_hbm.shape[0]
    copies = [
        pltpu.make_async_copy(key_hbm, out_ref.at[:rows], sems.at[0]),
        pltpu.make_async_copy(value_hbm, out_ref.at[rows:], sems.at[1]),
    ]
    for copy in copies:
        copy.start()
    for copy in copies:
        copy.wait()


def pack(keys, values):
    rows, width = keys.shape
    return pl.pallas_call(
        pack_kernel,
        out_shape=pltpu.VMEM((2 * rows, width), keys.dtype),
        in_specs=[HBM, HBM],
        out_specs=VMEM,
        scratch_shapes=[pltpu.SemaphoreType.DMA((2,))],
        compiler_params=pltpu.CompilerParams(vmem_limit_bytes=1024 * 1024),
    )(*in_hbm(keys, values))


def attend_own(runs, rows, own_ref, own_bias_ref, q_ref, level_ref, mean_ref, ready):
    def match(heads, g):
        ready(heads, g)
        key = own_ref[:rows, head_columns(g)]
        return (scores_of(stacked(q_ref, heads, rows), key, own_bias_ref[...]),)

    def weigh(heads, g, scores):
        top = jnp.max(scores, axis=1, keepdims=True)
        return weights_of(scores, top), jnp.broadcast_to(top, scores.shape)

    def gather(heads, g, weights, top):
        value = with_ones(own_ref[rows:, head_columns(g)])
        more = jnp.dot(weights, value, preferred_element_type=jnp.float32)
        summed, total = more[:, :HEAD_SIZE], more[:, HEAD_SIZE:]
        spread(mean_ref, heads, rows, normalised(summed, total))
        spread(level_ref, heads, rows, level_of(top, total))

    in_turn(runs, match, weigh, gather)


def own_kernel(
    rounds, rows, own_ref, lengths_hbm, q_hbm,
    longer_ref, bias_ref, needed_ref, own_bias_ref, q_ref, odd_ref, level_ref, mean_ref,
    lengths_ref, lengths_sem, q_sems,
):
    lengths_copy = pltpu.make_async_copy(lengths_hbm, lengths_ref, lengths_sem)
    lengths_copy.start()
    width = GROUP * HEAD_SIZE
    q_copies = []
    for g in range(KEY_VALUE_HEADS):
        at = slice(g * width, (g + 1) * width)
        q_copies.append(pltpu.make_async_copy(q_hbm.at[:, at], q_ref.at[:, at], q_sems.at[g]))
        q_copies[g].start()
    me = lax.axis_index("dp") * lax.axis_size("ctx") + lax.axis_index("ctx")
    longer_ref[: 2 * rows, :] = own_ref[...]
    longer_ref[2 * rows :, :] = jnp.zeros((PAD, longer_ref.shape[1]), longer_ref.dtype)
    odd_ref[...] = jnp.full(odd_ref.shape, lax.rem(me, 2), jnp.int32)
    first = me * rows
    query_pos = first + lax.broadcasted_iota(jnp.int32, (rows, rows), 0)
    lengths_copy.wait()

    def later(doc, carried):
        bound, start, first_start, first_end = carried
        following = bound + lengths_ref[doc]
        start = jnp.where(query_pos >= bound, bound, start)
        first_start = jnp.where(first >= bound, bound, first_start)
        first_end = jnp.where(first >= bound, following, first_end)
        return following, start, first_start, first_end

    zero = jnp.int32(0)
    _, start, first_start, first_end = lax.fori_loop(
        0,
        lengths_ref.shape[0],
        later,
        (zero, jnp.zeros((rows, rows), jnp.int32), zero, zero),
        unroll=8,
    )
    needed = lax.div(first - first_start + (rows - 1), jnp.int32(rows))
    crossing = jnp.minimum(first_end - first, rows)
    needed_ref[...] = jnp.full(needed_ref.shape, needed * (rows + 1) + crossing, jnp.int32)
    lane = lax.broadcasted_iota(jnp.int32, (rows, rows), 1)

    def bias_of(allowed):
        return jnp.where(allowed, jnp.float32(0.0), jnp.float32(EXCLUDED))

    key_pos = first + lane
    own_bias_ref[...] = bias_of((key_pos >= start) & (key_pos <= query_pos))
    for b in range(2 * rounds):
        key_pos = first - (b + 1) * rows + lane
        bias_ref[:, b * rows : (b + 1) * rows] = bias_of(key_pos >= start)

    def ready(heads, g):
        if heads[0] % GROUP == 0:
            q_copies[g].wait()

    runs = chains()[:EARLY_CHAINS]
    attend_own(runs, rows, own_ref, own_bias_ref, q_ref, level_ref, mean_ref, ready)
    for copy in q_copies[runs[-1][1] + 1 :]:
        copy.wait()


def own_rest_kernel(
    rows, own_ref, own_bias_ref, q_ref, odd_ref, *parts
):
    runs = chains()[EARLY_CHAINS:]
    parts = parts[3:]
    attend_own(runs, rows, own_ref, own_bias_ref, q_ref, *parts, lambda heads, g: None)


def in_vmem(*operands):
    return [pltpu.with_memory_space_constraint(x, pltpu.VMEM) for x in operands]


def in_hbm(*operands):
    return [pltpu.with_memory_space_constraint(x, pltpu.HBM) for x in operands]


SMEM = pl.BlockSpec(memory_space=pltpu.SMEM)
VMEM = pl.BlockSpec(memory_space=pltpu.VMEM)
HBM = pl.BlockSpec(memory_space=pltpu.HBM)


def own_part(lengths, queries, own, rounds):
    rows = queries.shape[0]
    part = pltpu.VMEM(queries.shape, jnp.float32)
    return pl.pallas_call(
        functools.partial(own_kernel, rounds, rows),
        out_shape=(
            pltpu.VMEM((2 * rows + PAD, own.shape[1]), own.dtype),
            pltpu.VMEM((rows, 2 * rounds * rows), jnp.float32),
            pltpu.VMEM((8, 128), jnp.int32),
            pltpu.VMEM((rows, rows), jnp.float32),
            pltpu.VMEM(queries.shape, queries.dtype),
            pltpu.VMEM((1, own.shape[1]), jnp.int32),
            part,
            part,
        ),
        in_specs=[VMEM, HBM, HBM],
        out_specs=(VMEM,) * 8,
        scratch_shapes=[
            pltpu.SMEM(lengths.shape, jnp.int32),
            pltpu.SemaphoreType.DMA,
            pltpu.SemaphoreType.DMA((KEY_VALUE_HEADS,)),
        ],
        compiler_params=pltpu.CompilerParams(vmem_limit_bytes=10 * 1024 * 1024),
        cost_estimate=pl.CostEstimate(
            flops=4 * 10**9, bytes_accessed=16 * 10**6, transcendentals=rows * queries.size
        ),
    )(*in_vmem(own), *in_hbm(lengths, queries))


def own_rest(own, own_bias, queries, kept):
    rows = queries.shape[0]
    operands = in_vmem(own, own_bias, queries, *kept)
    return pl.pallas_call(
        functools.partial(own_rest_kernel, rows),
        out_shape=tuple(pltpu.VMEM(x.shape, x.dtype) for x in kept),
        in_specs=[VMEM] * len(operands),
        out_specs=(VMEM,) * len(kept),
        input_output_aliases={3 + n: n for n in range(len(kept))},
        compiler_params=pltpu.CompilerParams(vmem_limit_bytes=10 * 1024 * 1024),
        cost_estimate=pl.CostEstimate(
            flops=4 * 10**9, bytes_accessed=16 * 10**6, transcendentals=rows * queries.size
        ),
    )(*operands)


def behind_kernel(
    before, last, rows, needed_ref, bias_ref, q_ref, near_ref, further_ref, level_ref, mean_ref, *refs
):
    both = needed_ref[0, 0]
    beyond = lax.div(both, rows + 1) - before
    crossing = lax.rem(both, rows + 1)
    pairs = [(ref.at[:rows], ref.at[rows : 2 * rows]) for ref in (near_ref, further_ref)]
    if last:
        out_hbm, out_ref, out_sems = refs

        def out_copy(n):
            width = HEADS_AT_ONCE * HEAD_SIZE
            at = slice(n * width, (n + 1) * width)
            return pltpu.make_async_copy(out_ref.at[:, at], out_hbm.at[:, at], out_sems.at[n])

    else:
        _, new_level_ref, new_mean_ref = refs

    def finish(heads, upto, mean):
        spread(out_ref, heads, upto, mean)
        if upto < rows:
            for i in heads:
                out_ref[upto:, head_columns(i)] = mean_ref[upto:, head_columns(i)].astype(
                    out_ref.dtype
                )
        for i in heads[::HEADS_AT_ONCE]:
            out_copy(i // HEADS_AT_ONCE).start()

    def attend(count, upto):
        def match(heads, g):
            key = jnp.concatenate([key[:, head_columns(g)] for key, _ in pairs[:count]], axis=0)
            bias = bias_ref[:upto, before * rows : (before + count) * rows]
            return (scores_of(stacked(q_ref, heads, upto), key, bias),)

        def weigh(heads, g, scores):
            level = stacked(level_ref, heads, upto)
            top = jnp.maximum(level, jnp.max(scores, axis=1, keepdims=True))
            fade = jnp.exp2((level - top) * jnp.float32(FACTOR))
            return weights_of(scores, jnp.concatenate([top] * count, axis=1)), fade, top

        def gather(heads, g, weights, fade, top):
            value = jnp.concatenate([value[:, head_columns(g)] for _, value in pairs[:count]], axis=0)
            more = jnp.dot(weights, with_ones(value), preferred_element_type=jnp.float32)
            summed = stacked(mean_ref, heads, upto) * fade + more[:, :HEAD_SIZE]
            total = fade + more[:, HEAD_SIZE:]
            if last:
                finish(heads, upto, normalised(summed, total))
            else:
                spread(new_mean_ref, heads, upto, normalised(summed, total))
                spread(new_level_ref, heads, upto, level_of(top, total))

        runs = chains() if upto == rows else chains(GROUP)
        in_turn(runs, match, weigh, gather)

    short = crossing <= rows // 2
    pl.when((beyond > 0) & short)(functools.partial(attend, 2, rows // 2))
    pl.when((beyond > 1) & jnp.logical_not(short))(functools.partial(attend, 2, rows))
    pl.when((beyond == 1) & jnp.logical_not(short))(functools.partial(attend, 1, rows))

    if last:
        @pl.when(beyond < 1)
        def _():
            in_turn(
                chains(),
                lambda heads, g: finish(heads, rows, stacked(mean_ref, heads, rows)),
            )

        for n in range(len(chains())):
            out_copy(n).wait()


def behind_part(before, last, needed, bias, queries, near, further, parts):
    rows = queries.shape[0]
    area = rows * rows * 2 * QUERY_HEADS
    operands = in_vmem(needed, bias, queries, near, further, *parts)
    if last:
        out_shape = jax.ShapeDtypeStruct(queries.shape, queries.dtype)
        out_specs = HBM
        scratch = [
            pltpu.VMEM(queries.shape, queries.dtype),
            pltpu.SemaphoreType.DMA((len(chains()),)),
        ]
        aliases = {}
    else:
        kept = (further, *parts)
        out_shape = tuple(pltpu.VMEM(part.shape, part.dtype) for part in kept)
        out_specs = (VMEM,) * len(kept)
        scratch = []
        aliases = {4 + n: n for n in range(len(kept))}
    return pl.pallas_call(
        functools.partial(behind_kernel, before, last, rows),
        out_shape=out_shape,
        in_specs=[VMEM] * len(operands),
        out_specs=out_specs,
        scratch_shapes=scratch,
        input_output_aliases=aliases,
        compiler_params=pltpu.CompilerParams(vmem_limit_bytes=10 * 1024 * 1024),
        cost_estimate=pl.CostEstimate(
            flops=4 * area, bytes_accessed=queries.size, transcendentals=0
        ),
    )(*operands)


def per_device(queries, keys, values, lengths):
    count = lax.axis_size("dp") * lax.axis_size("ctx")
    rounds = lax.axis_size("ctx")

    def from_behind(block, r):
        by = 2 * (r + 1)
        return lax.ppermute(block, AXES, [(i, i + by) for i in range(count - by)])

    own = pack(keys, values)
    fetched = [from_behind(own, 0)]
    longer, bias, needed, own_bias, queries, *kept = own_part(lengths, queries, own, rounds)
    fetched += [from_behind(longer, r) for r in range(1, rounds)]
    odd, *parts = own_rest(own, own_bias, queries, kept)
    swap = [(i, i ^ 1) for i in range(count)]
    nearer = own
    size = 2 * keys.shape[0]
    for r, further in enumerate(fetched):
        last = r == rounds - 1
        near = lax.ppermute(jnp.where(odd == 1, further[:size], nearer[:size]), AXES, swap)
        result = behind_part(2 * r, last, needed, bias, queries, near, further, parts)
        if not last:
            nearer, *parts = result
    return result


def solution(mesh):
    in_specs = (P(AXES, None), P(AXES, None), P(AXES, None), P())
    return jax.shard_map(
        per_device, mesh=mesh, in_specs=in_specs, out_specs=P(AXES, None), check_vma=False
    )
```

```python
import functools
import math

import jax
import jax.numpy as jnp
from jax import lax
from jax.experimental import pallas as pl
from jax.experimental.pallas import tpu as pltpu
from jax.sharding import PartitionSpec as P

HEAD_SIZE = 128
QUERY_HEADS = 32
KEY_VALUE_HEADS = 4
GROUP = QUERY_HEADS // KEY_VALUE_HEADS
HEADS_AT_ONCE = 4
EARLY_CHAINS = 4
EXCLUDED = -1e30
PAD = 16
AXES = ("dp", "ctx")


FACTOR = math.log2(math.e) / math.sqrt(HEAD_SIZE)


def head_columns(i):
    return slice(i * HEAD_SIZE, (i + 1) * HEAD_SIZE)


def stacked(ref, heads, rows):
    return jnp.concatenate([ref[:rows, head_columns(i)] for i in heads], axis=0)


def spread(ref, heads, rows, value):
    for n, i in enumerate(heads):
        ref[:rows, head_columns(i)] = value[n * rows : (n + 1) * rows].astype(ref.dtype)


def with_ones(value):
    return jnp.concatenate([value, jnp.ones(value.shape, value.dtype)], axis=1)


def scores_of(q, key, bias):
    scores = lax.dot_general(
        q, key, (((1,), (1,)), ((), ())), preferred_element_type=jnp.float32
    )
    return scores + jnp.concatenate([bias] * (q.shape[0] // bias.shape[0]), axis=0)


def weights_of(scores, top):
    return jnp.exp2((scores - top) * jnp.float32(FACTOR)).astype(jnp.bfloat16)


def normalised(summed, total):
    inverse = pl.reciprocal(total, approx=True)
    return summed * (inverse * (2.0 - total * inverse))


def level_of(top, total):
    return top + jnp.log(total) * jnp.float32(math.sqrt(HEAD_SIZE))


def chains(size=HEADS_AT_ONCE):
    return [(range(h, h + size), h // GROUP) for h in range(0, QUERY_HEADS, size)]


def in_turn(runs, *stages):
    results = {}
    for turn in range(len(runs) + len(stages) - 1):
        for n, stage in enumerate(stages):
            i = turn - n
            if 0 <= i < len(runs):
                results[i] = stage(*runs[i], *results.pop(i, ()))


def pack_kernel(key_hbm, value_hbm, out_ref, sems):
    rows = key_hbm.shape[0]
    copies = [
        pltpu.make_async_copy(key_hbm, out_ref.at[:rows], sems.at[0]),
        pltpu.make_async_copy(value_hbm, out_ref.at[rows:], sems.at[1]),
    ]
    for copy in copies:
        copy.start()
    for copy in copies:
        copy.wait()


def pack(keys, values):
    rows, width = keys.shape
    return pl.pallas_call(
        pack_kernel,
        out_shape=pltpu.VMEM((2 * rows, width), keys.dtype),
        in_specs=[HBM, HBM],
        out_specs=VMEM,
        scratch_shapes=[pltpu.SemaphoreType.DMA((2,))],
        compiler_params=pltpu.CompilerParams(vmem_limit_bytes=1024 * 1024),
    )(*in_hbm(keys, values))


def attend_own(runs, rows, own_ref, own_bias_ref, q_ref, level_ref, mean_ref, ready):
    def match(heads, g):
        ready(heads, g)
        key = own_ref[:rows, head_columns(g)]
        return (scores_of(stacked(q_ref, heads, rows), key, own_bias_ref[...]),)

    def weigh(heads, g, scores):
        top = jnp.max(scores, axis=1, keepdims=True)
        return weights_of(scores, top), jnp.broadcast_to(top, scores.shape)

    def gather(heads, g, weights, top):
        value = with_ones(own_ref[rows:, head_columns(g)])
        more = jnp.dot(weights, value, preferred_element_type=jnp.float32)
        summed, total = more[:, :HEAD_SIZE], more[:, HEAD_SIZE:]
        spread(mean_ref, heads, rows, normalised(summed, total))
        spread(level_ref, heads, rows, level_of(top, total))

    in_turn(runs, match, weigh, gather)


def own_kernel(
    rounds, rows, own_ref, lengths_hbm, q_hbm,
    longer_ref, bias_ref, needed_ref, own_bias_ref, q_ref, odd_ref, level_ref, mean_ref,
    lengths_ref, lengths_sem, q_sems,
):
    lengths_copy = pltpu.make_async_copy(lengths_hbm, lengths_ref, lengths_sem)
    lengths_copy.start()
    width = GROUP * HEAD_SIZE
    q_copies = []
    for g in range(KEY_VALUE_HEADS):
        at = slice(g * width, (g + 1) * width)
        q_copies.append(pltpu.make_async_copy(q_hbm.at[:, at], q_ref.at[:, at], q_sems.at[g]))
        q_copies[g].start()
    me = lax.axis_index("dp") * lax.axis_size("ctx") + lax.axis_index("ctx")
    longer_ref[: 2 * rows, :] = own_ref[...]
    longer_ref[2 * rows :, :] = jnp.zeros((PAD, longer_ref.shape[1]), longer_ref.dtype)
    odd_ref[...] = jnp.full(odd_ref.shape, lax.rem(me, 2), jnp.int32)
    first = me * rows
    query_pos = first + lax.broadcasted_iota(jnp.int32, (rows, rows), 0)
    lengths_copy.wait()

    def later(doc, carried):
        bound, start, first_start, first_end = carried
        following = bound + lengths_ref[doc]
        start = jnp.where(query_pos >= bound, bound, start)
        first_start = jnp.where(first >= bound, bound, first_start)
        first_end = jnp.where(first >= bound, following, first_end)
        return following, start, first_start, first_end

    zero = jnp.int32(0)
    _, start, first_start, first_end = lax.fori_loop(
        0,
        lengths_ref.shape[0],
        later,
        (zero, jnp.zeros((rows, rows), jnp.int32), zero, zero),
        unroll=8,
    )
    needed = lax.div(first - first_start + (rows - 1), jnp.int32(rows))
    crossing = jnp.minimum(first_end - first, rows)
    needed_ref[...] = jnp.full(needed_ref.shape, needed * (rows + 1) + crossing, jnp.int32)
    lane = lax.broadcasted_iota(jnp.int32, (rows, rows), 1)

    def bias_of(allowed):
        return jnp.where(allowed, jnp.float32(0.0), jnp.float32(EXCLUDED))

    key_pos = first + lane
    own_bias_ref[...] = bias_of((key_pos >= start) & (key_pos <= query_pos))
    for b in range(2 * rounds):
        key_pos = first - (b + 1) * rows + lane
        bias_ref[:, b * rows : (b + 1) * rows] = bias_of(key_pos >= start)

    def ready(heads, g):
        if heads[0] % GROUP == 0:
            q_copies[g].wait()

    runs = chains()[:EARLY_CHAINS]
    attend_own(runs, rows, own_ref, own_bias_ref, q_ref, level_ref, mean_ref, ready)
    for copy in q_copies[runs[-1][1] + 1 :]:
        copy.wait()


def own_rest_kernel(
    rows, own_ref, own_bias_ref, q_ref, odd_ref, *parts
):
    runs = chains()[EARLY_CHAINS:]
    parts = parts[3:]
    attend_own(runs, rows, own_ref, own_bias_ref, q_ref, *parts, lambda heads, g: None)


def in_vmem(*operands):
    return [pltpu.with_memory_space_constraint(x, pltpu.VMEM) for x in operands]


def in_hbm(*operands):
    return [pltpu.with_memory_space_constraint(x, pltpu.HBM) for x in operands]


SMEM = pl.BlockSpec(memory_space=pltpu.SMEM)
VMEM = pl.BlockSpec(memory_space=pltpu.VMEM)
HBM = pl.BlockSpec(memory_space=pltpu.HBM)


def own_part(lengths, queries, own, rounds):
    rows = queries.shape[0]
    part = pltpu.VMEM(queries.shape, jnp.float32)
    return pl.pallas_call(
        functools.partial(own_kernel, rounds, rows),
        out_shape=(
            pltpu.VMEM((2 * rows + PAD, own.shape[1]), own.dtype),
            pltpu.VMEM((rows, 2 * rounds * rows), jnp.float32),
            pltpu.VMEM((8, 128), jnp.int32),
            pltpu.VMEM((rows, rows), jnp.float32),
            pltpu.VMEM(queries.shape, queries.dtype),
            pltpu.VMEM((1, own.shape[1]), jnp.int32),
            part,
            part,
        ),
        in_specs=[VMEM, HBM, HBM],
        out_specs=(VMEM,) * 8,
        scratch_shapes=[
            pltpu.SMEM(lengths.shape, jnp.int32),
            pltpu.SemaphoreType.DMA,
            pltpu.SemaphoreType.DMA((KEY_VALUE_HEADS,)),
        ],
        compiler_params=pltpu.CompilerParams(vmem_limit_bytes=10 * 1024 * 1024),
        cost_estimate=pl.CostEstimate(
            flops=4 * 10**9, bytes_accessed=16 * 10**6, transcendentals=rows * queries.size
        ),
    )(*in_vmem(own), *in_hbm(lengths, queries))


def own_rest(own, own_bias, queries, kept):
    rows = queries.shape[0]
    operands = in_vmem(own, own_bias, queries, *kept)
    return pl.pallas_call(
        functools.partial(own_rest_kernel, rows),
        out_shape=tuple(pltpu.VMEM(x.shape, x.dtype) for x in kept),
        in_specs=[VMEM] * len(operands),
        out_specs=(VMEM,) * len(kept),
        input_output_aliases={3 + n: n for n in range(len(kept))},
        compiler_params=pltpu.CompilerParams(vmem_limit_bytes=10 * 1024 * 1024),
        cost_estimate=pl.CostEstimate(
            flops=4 * 10**9, bytes_accessed=16 * 10**6, transcendentals=rows * queries.size
        ),
    )(*operands)


def behind_kernel(
    before, last, rows, needed_ref, bias_ref, q_ref, near_ref, further_ref, level_ref, mean_ref, *refs
):
    both = needed_ref[0, 0]
    beyond = lax.div(both, rows + 1) - before
    crossing = lax.rem(both, rows + 1)
    pairs = [(ref.at[:rows], ref.at[rows : 2 * rows]) for ref in (near_ref, further_ref)]
    if last:
        out_hbm, out_ref, out_sems = refs

        def out_copy(n):
            width = HEADS_AT_ONCE * HEAD_SIZE
            at = slice(n * width, (n + 1) * width)
            return pltpu.make_async_copy(out_ref.at[:, at], out_hbm.at[:, at], out_sems.at[n])

    else:
        _, new_level_ref, new_mean_ref = refs

    def finish(heads, upto, mean):
        spread(out_ref, heads, upto, mean)
        if upto < rows:
            for i in heads:
                out_ref[upto:, head_columns(i)] = mean_ref[upto:, head_columns(i)].astype(
                    out_ref.dtype
                )
        for i in heads[::HEADS_AT_ONCE]:
            out_copy(i // HEADS_AT_ONCE).start()

    def attend(count, upto):
        def match(heads, g):
            key = jnp.concatenate([key[:, head_columns(g)] for key, _ in pairs[:count]], axis=0)
            bias = bias_ref[:upto, before * rows : (before + count) * rows]
            return (scores_of(stacked(q_ref, heads, upto), key, bias),)

        def weigh(heads, g, scores):
            level = stacked(level_ref, heads, upto)
            top = jnp.maximum(level, jnp.max(scores, axis=1, keepdims=True))
            fade = jnp.exp2((level - top) * jnp.float32(FACTOR))
            return weights_of(scores, jnp.concatenate([top] * count, axis=1)), fade, top

        def gather(heads, g, weights, fade, top):
            value = jnp.concatenate([value[:, head_columns(g)] for _, value in pairs[:count]], axis=0)
            more = jnp.dot(weights, with_ones(value), preferred_element_type=jnp.float32)
            summed = stacked(mean_ref, heads, upto) * fade + more[:, :HEAD_SIZE]
            total = fade + more[:, HEAD_SIZE:]
            if last:
                finish(heads, upto, normalised(summed, total))
            else:
                spread(new_mean_ref, heads, upto, normalised(summed, total))
                spread(new_level_ref, heads, upto, level_of(top, total))

        runs = chains() if upto == rows else chains(GROUP)
        in_turn(runs, match, weigh, gather)

    some = beyond > 0
    quarter, half = crossing <= rows // 4, crossing <= rows // 2
    pl.when(some & quarter)(functools.partial(attend, 2, rows // 4))
    pl.when(some & half & jnp.logical_not(quarter))(functools.partial(attend, 2, rows // 2))
    full = jnp.logical_not(half)
    if last:
        pl.when((beyond > 1) & full)(functools.partial(attend, 2, rows))
        pl.when((beyond == 1) & full)(functools.partial(attend, 1, rows))
    else:
        pl.when(some & full)(functools.partial(attend, 2, rows))

    if last:
        @pl.when(beyond < 1)
        def _():
            in_turn(
                chains(),
                lambda heads, g: finish(heads, rows, stacked(mean_ref, heads, rows)),
            )

        for n in range(len(chains())):
            out_copy(n).wait()


def behind_part(before, last, needed, bias, queries, near, further, parts):
    rows = queries.shape[0]
    area = rows * rows * 2 * QUERY_HEADS
    operands = in_vmem(needed, bias, queries, near, further, *parts)
    if last:
        out_shape = jax.ShapeDtypeStruct(queries.shape, queries.dtype)
        out_specs = HBM
        scratch = [
            pltpu.VMEM(queries.shape, queries.dtype),
            pltpu.SemaphoreType.DMA((len(chains()),)),
        ]
        aliases = {}
    else:
        kept = (further, *parts)
        out_shape = tuple(pltpu.VMEM(part.shape, part.dtype) for part in kept)
        out_specs = (VMEM,) * len(kept)
        scratch = []
        aliases = {4 + n: n for n in range(len(kept))}
    return pl.pallas_call(
        functools.partial(behind_kernel, before, last, rows),
        out_shape=out_shape,
        in_specs=[VMEM] * len(operands),
        out_specs=out_specs,
        scratch_shapes=scratch,
        input_output_aliases=aliases,
        compiler_params=pltpu.CompilerParams(vmem_limit_bytes=10 * 1024 * 1024),
        cost_estimate=pl.CostEstimate(
            flops=4 * area, bytes_accessed=queries.size, transcendentals=0
        ),
    )(*operands)


def per_device(queries, keys, values, lengths):
    count = lax.axis_size("dp") * lax.axis_size("ctx")
    rounds = lax.axis_size("ctx")

    def from_behind(block, r):
        by = 2 * (r + 1)
        return lax.ppermute(block, AXES, [(i, i + by) for i in range(count - by)])

    own = pack(keys, values)
    fetched = [from_behind(own, 0)]
    longer, bias, needed, own_bias, queries, *kept = own_part(lengths, queries, own, rounds)
    fetched += [from_behind(longer, r) for r in range(1, rounds)]
    odd, *parts = own_rest(own, own_bias, queries, kept)
    swap = [(i, i ^ 1) for i in range(count)]
    nearer = own
    size = 2 * keys.shape[0]
    for r, further in enumerate(fetched):
        last = r == rounds - 1
        near = lax.ppermute(jnp.where(odd == 1, further[:size], nearer[:size]), AXES, swap)
        result = behind_part(2 * r, last, needed, bias, queries, near, further, parts)
        if not last:
            nearer, *parts = result
    return result


def solution(mesh):
    in_specs = (P(AXES, None), P(AXES, None), P(AXES, None), P())
    return jax.shard_map(
        per_device, mesh=mesh, in_specs=in_specs, out_specs=P(AXES, None), check_vma=False
    )
```

```python
import functools
import math

import jax
import jax.numpy as jnp
from jax import lax
from jax.experimental import pallas as pl
from jax.experimental.pallas import tpu as pltpu
from jax.sharding import PartitionSpec as P

HEAD_SIZE = 128
QUERY_HEADS = 32
KEY_VALUE_HEADS = 4
GROUP = QUERY_HEADS // KEY_VALUE_HEADS
HEADS_AT_ONCE = 4
EARLY_CHAINS = 3
EXCLUDED = -1e30
PAD = 16
AXES = ("dp", "ctx")


FACTOR = math.log2(math.e) / math.sqrt(HEAD_SIZE)


def head_columns(i):
    return slice(i * HEAD_SIZE, (i + 1) * HEAD_SIZE)


def stacked(ref, heads, rows):
    return jnp.concatenate([ref[:rows, head_columns(i)] for i in heads], axis=0)


def spread(ref, heads, rows, value):
    for n, i in enumerate(heads):
        ref[:rows, head_columns(i)] = value[n * rows : (n + 1) * rows].astype(ref.dtype)


def with_ones(value):
    return jnp.concatenate([value, jnp.ones(value.shape, value.dtype)], axis=1)


def scores_of(q, key, bias):
    scores = lax.dot_general(
        q, key, (((1,), (1,)), ((), ())), preferred_element_type=jnp.float32
    )
    return scores + jnp.concatenate([bias] * (q.shape[0] // bias.shape[0]), axis=0)


def weights_of(scores, top):
    return jnp.exp2((scores - top) * jnp.float32(FACTOR)).astype(jnp.bfloat16)


def normalised(summed, total):
    inverse = pl.reciprocal(total, approx=True)
    return summed * (inverse * (2.0 - total * inverse))


def level_of(top, total):
    return top + jnp.log(total) * jnp.float32(math.sqrt(HEAD_SIZE))


def chains(size=HEADS_AT_ONCE):
    return [(range(h, h + size), h // GROUP) for h in range(0, QUERY_HEADS, size)]


def in_turn(runs, *stages):
    results = {}
    for turn in range(len(runs) + len(stages) - 1):
        for n, stage in enumerate(stages):
            i = turn - n
            if 0 <= i < len(runs):
                results[i] = stage(*runs[i], *results.pop(i, ()))


def pack_kernel(key_hbm, value_hbm, out_ref, sems):
    rows = key_hbm.shape[0]
    copies = [
        pltpu.make_async_copy(key_hbm, out_ref.at[:rows], sems.at[0]),
        pltpu.make_async_copy(value_hbm, out_ref.at[rows:], sems.at[1]),
    ]
    for copy in copies:
        copy.start()
    for copy in copies:
        copy.wait()


def pack(keys, values):
    rows, width = keys.shape
    return pl.pallas_call(
        pack_kernel,
        out_shape=pltpu.VMEM((2 * rows, width), keys.dtype),
        in_specs=[HBM, HBM],
        out_specs=VMEM,
        scratch_shapes=[pltpu.SemaphoreType.DMA((2,))],
        compiler_params=pltpu.CompilerParams(vmem_limit_bytes=1024 * 1024),
    )(*in_hbm(keys, values))


def attend_own(runs, rows, own_ref, own_bias_ref, q_ref, level_ref, mean_ref, ready):
    def match(heads, g):
        ready(heads, g)
        key = own_ref[:rows, head_columns(g)]
        return (scores_of(stacked(q_ref, heads, rows), key, own_bias_ref[...]),)

    def weigh(heads, g, scores):
        top = jnp.max(scores, axis=1, keepdims=True)
        return weights_of(scores, top), jnp.broadcast_to(top, scores.shape)

    def gather(heads, g, weights, top):
        value = with_ones(own_ref[rows:, head_columns(g)])
        more = jnp.dot(weights, value, preferred_element_type=jnp.float32)
        summed, total = more[:, :HEAD_SIZE], more[:, HEAD_SIZE:]
        spread(mean_ref, heads, rows, normalised(summed, total))
        spread(level_ref, heads, rows, level_of(top, total))

    in_turn(runs, match, weigh, gather)


def own_kernel(
    rounds, rows, own_ref, lengths_hbm, q_hbm,
    longer_ref, bias_ref, needed_ref, own_bias_ref, q_ref, odd_ref, level_ref, mean_ref,
    lengths_ref, lengths_sem, q_sems,
):
    lengths_copy = pltpu.make_async_copy(lengths_hbm, lengths_ref, lengths_sem)
    lengths_copy.start()
    width = GROUP * HEAD_SIZE
    q_copies = []
    for g in range(KEY_VALUE_HEADS):
        at = slice(g * width, (g + 1) * width)
        q_copies.append(pltpu.make_async_copy(q_hbm.at[:, at], q_ref.at[:, at], q_sems.at[g]))
        q_copies[g].start()
    me = lax.axis_index("dp") * lax.axis_size("ctx") + lax.axis_index("ctx")
    longer_ref[: 2 * rows, :] = own_ref[...]
    longer_ref[2 * rows :, :] = jnp.zeros((PAD, longer_ref.shape[1]), longer_ref.dtype)
    odd_ref[...] = jnp.full(odd_ref.shape, lax.rem(me, 2), jnp.int32)
    first = me * rows
    query_pos = first + lax.broadcasted_iota(jnp.int32, (rows, rows), 0)
    lengths_copy.wait()

    def later(doc, carried):
        bound, start, first_start, first_end = carried
        following = bound + lengths_ref[doc]
        start = jnp.where(query_pos >= bound, bound, start)
        first_start = jnp.where(first >= bound, bound, first_start)
        first_end = jnp.where(first >= bound, following, first_end)
        return following, start, first_start, first_end

    zero = jnp.int32(0)
    _, start, first_start, first_end = lax.fori_loop(
        0,
        lengths_ref.shape[0],
        later,
        (zero, jnp.zeros((rows, rows), jnp.int32), zero, zero),
        unroll=8,
    )
    needed = lax.div(first - first_start + (rows - 1), jnp.int32(rows))
    crossing = jnp.minimum(first_end - first, rows)
    needed_ref[...] = jnp.full(needed_ref.shape, needed * (rows + 1) + crossing, jnp.int32)
    lane = lax.broadcasted_iota(jnp.int32, (rows, rows), 1)

    def bias_of(allowed):
        return jnp.where(allowed, jnp.float32(0.0), jnp.float32(EXCLUDED))

    key_pos = first + lane
    own_bias_ref[...] = bias_of((key_pos >= start) & (key_pos <= query_pos))
    for b in range(2 * rounds):
        key_pos = first - (b + 1) * rows + lane
        bias_ref[:, b * rows : (b + 1) * rows] = bias_of(key_pos >= start)

    def ready(heads, g):
        if heads[0] % GROUP == 0:
            q_copies[g].wait()

    runs = chains()[:EARLY_CHAINS]
    attend_own(runs, rows, own_ref, own_bias_ref, q_ref, level_ref, mean_ref, ready)
    for copy in q_copies[runs[-1][1] + 1 :]:
        copy.wait()


def own_rest_kernel(
    rows, own_ref, own_bias_ref, q_ref, odd_ref, *parts
):
    runs = chains()[EARLY_CHAINS:]
    parts = parts[3:]
    attend_own(runs, rows, own_ref, own_bias_ref, q_ref, *parts, lambda heads, g: None)


def in_vmem(*operands):
    return [pltpu.with_memory_space_constraint(x, pltpu.VMEM) for x in operands]


def in_hbm(*operands):
    return [pltpu.with_memory_space_constraint(x, pltpu.HBM) for x in operands]


SMEM = pl.BlockSpec(memory_space=pltpu.SMEM)
VMEM = pl.BlockSpec(memory_space=pltpu.VMEM)
HBM = pl.BlockSpec(memory_space=pltpu.HBM)


def own_part(lengths, queries, own, rounds):
    rows = queries.shape[0]
    part = pltpu.VMEM(queries.shape, jnp.float32)
    return pl.pallas_call(
        functools.partial(own_kernel, rounds, rows),
        out_shape=(
            pltpu.VMEM((2 * rows + PAD, own.shape[1]), own.dtype),
            pltpu.VMEM((rows, 2 * rounds * rows), jnp.float32),
            pltpu.VMEM((8, 128), jnp.int32),
            pltpu.VMEM((rows, rows), jnp.float32),
            pltpu.VMEM(queries.shape, queries.dtype),
            pltpu.VMEM((1, own.shape[1]), jnp.int32),
            part,
            part,
        ),
        in_specs=[VMEM, HBM, HBM],
        out_specs=(VMEM,) * 8,
        scratch_shapes=[
            pltpu.SMEM(lengths.shape, jnp.int32),
            pltpu.SemaphoreType.DMA,
            pltpu.SemaphoreType.DMA((KEY_VALUE_HEADS,)),
        ],
        compiler_params=pltpu.CompilerParams(vmem_limit_bytes=10 * 1024 * 1024),
        cost_estimate=pl.CostEstimate(
            flops=4 * 10**9, bytes_accessed=16 * 10**6, transcendentals=rows * queries.size
        ),
    )(*in_vmem(own), *in_hbm(lengths, queries))


def own_rest(own, own_bias, queries, kept):
    rows = queries.shape[0]
    operands = in_vmem(own, own_bias, queries, *kept)
    return pl.pallas_call(
        functools.partial(own_rest_kernel, rows),
        out_shape=tuple(pltpu.VMEM(x.shape, x.dtype) for x in kept),
        in_specs=[VMEM] * len(operands),
        out_specs=(VMEM,) * len(kept),
        input_output_aliases={3 + n: n for n in range(len(kept))},
        compiler_params=pltpu.CompilerParams(vmem_limit_bytes=10 * 1024 * 1024),
        cost_estimate=pl.CostEstimate(
            flops=4 * 10**9, bytes_accessed=16 * 10**6, transcendentals=rows * queries.size
        ),
    )(*operands)


def behind_kernel(
    before, last, rows, needed_ref, bias_ref, q_ref, near_ref, further_ref, level_ref, mean_ref, *refs
):
    both = needed_ref[0, 0]
    beyond = lax.div(both, rows + 1) - before
    crossing = lax.rem(both, rows + 1)
    pairs = [(ref.at[:rows], ref.at[rows : 2 * rows]) for ref in (near_ref, further_ref)]
    if last:
        out_hbm, out_ref, out_sems = refs

        def out_copy(n):
            width = HEADS_AT_ONCE * HEAD_SIZE
            at = slice(n * width, (n + 1) * width)
            return pltpu.make_async_copy(out_ref.at[:, at], out_hbm.at[:, at], out_sems.at[n])

    else:
        _, new_level_ref, new_mean_ref = refs

    def finish(heads, upto, mean):
        spread(out_ref, heads, upto, mean)
        if upto < rows:
            for i in heads:
                out_ref[upto:, head_columns(i)] = mean_ref[upto:, head_columns(i)].astype(
                    out_ref.dtype
                )
        for i in heads[::HEADS_AT_ONCE]:
            out_copy(i // HEADS_AT_ONCE).start()

    def attend(count, upto):
        def match(heads, g):
            key = jnp.concatenate([key[:, head_columns(g)] for key, _ in pairs[:count]], axis=0)
            bias = bias_ref[:upto, before * rows : (before + count) * rows]
            return (scores_of(stacked(q_ref, heads, upto), key, bias),)

        def weigh(heads, g, scores):
            level = stacked(level_ref, heads, upto)
            top = jnp.maximum(level, jnp.max(scores, axis=1, keepdims=True))
            fade = jnp.exp2((level - top) * jnp.float32(FACTOR))
            return weights_of(scores, jnp.concatenate([top] * count, axis=1)), fade, top

        def gather(heads, g, weights, fade, top):
            value = jnp.concatenate([value[:, head_columns(g)] for _, value in pairs[:count]], axis=0)
            more = jnp.dot(weights, with_ones(value), preferred_element_type=jnp.float32)
            summed = stacked(mean_ref, heads, upto) * fade + more[:, :HEAD_SIZE]
            total = fade + more[:, HEAD_SIZE:]
            if last:
                finish(heads, upto, normalised(summed, total))
            else:
                spread(new_mean_ref, heads, upto, normalised(summed, total))
                spread(new_level_ref, heads, upto, level_of(top, total))

        runs = chains() if upto == rows else chains(GROUP)
        in_turn(runs, match, weigh, gather)

    some = beyond > 0
    quarter, half = crossing <= rows // 4, crossing <= rows // 2
    pl.when(some & quarter)(functools.partial(attend, 2, rows // 4))
    pl.when(some & half & jnp.logical_not(quarter))(functools.partial(attend, 2, rows // 2))
    full = jnp.logical_not(half)
    if last:
        pl.when((beyond > 1) & full)(functools.partial(attend, 2, rows))
        pl.when((beyond == 1) & full)(functools.partial(attend, 1, rows))
    else:
        pl.when(some & full)(functools.partial(attend, 2, rows))

    if last:
        @pl.when(beyond < 1)
        def _():
            in_turn(
                chains(),
                lambda heads, g: finish(heads, rows, stacked(mean_ref, heads, rows)),
            )

        for n in range(len(chains())):
            out_copy(n).wait()


def behind_part(before, last, needed, bias, queries, near, further, parts):
    rows = queries.shape[0]
    area = rows * rows * 2 * QUERY_HEADS
    operands = in_vmem(needed, bias, queries, near, further, *parts)
    if last:
        out_shape = jax.ShapeDtypeStruct(queries.shape, queries.dtype)
        out_specs = HBM
        scratch = [
            pltpu.VMEM(queries.shape, queries.dtype),
            pltpu.SemaphoreType.DMA((len(chains()),)),
        ]
        aliases = {}
    else:
        kept = (further, *parts)
        out_shape = tuple(pltpu.VMEM(part.shape, part.dtype) for part in kept)
        out_specs = (VMEM,) * len(kept)
        scratch = []
        aliases = {4 + n: n for n in range(len(kept))}
    return pl.pallas_call(
        functools.partial(behind_kernel, before, last, rows),
        out_shape=out_shape,
        in_specs=[VMEM] * len(operands),
        out_specs=out_specs,
        scratch_shapes=scratch,
        input_output_aliases=aliases,
        compiler_params=pltpu.CompilerParams(vmem_limit_bytes=10 * 1024 * 1024),
        cost_estimate=pl.CostEstimate(
            flops=4 * area, bytes_accessed=queries.size, transcendentals=0
        ),
    )(*operands)


def per_device(queries, keys, values, lengths):
    count = lax.axis_size("dp") * lax.axis_size("ctx")
    rounds = lax.axis_size("ctx")

    def from_behind(block, r):
        by = 2 * (r + 1)
        return lax.ppermute(block, AXES, [(i, i + by) for i in range(count - by)])

    own = pack(keys, values)
    fetched = [from_behind(own, 0)]
    longer, bias, needed, own_bias, queries, *kept = own_part(lengths, queries, own, rounds)
    fetched += [from_behind(longer, r) for r in range(1, rounds)]
    odd, *parts = own_rest(own, own_bias, queries, kept)
    swap = [(i, i ^ 1) for i in range(count)]
    nearer = own
    size = 2 * keys.shape[0]
    for r, further in enumerate(fetched):
        last = r == rounds - 1
        near = lax.ppermute(jnp.where(odd == 1, further[:size], nearer[:size]), AXES, swap)
        result = behind_part(2 * r, last, needed, bias, queries, near, further, parts)
        if not last:
            nearer, *parts = result
    return result


def solution(mesh):
    in_specs = (P(AXES, None), P(AXES, None), P(AXES, None), P())
    return jax.shard_map(
        per_device, mesh=mesh, in_specs=in_specs, out_specs=P(AXES, None), check_vma=False
    )
```
